32 devices in a mesh: copy: 2 (over x), ctx: 8 (over z, y), tp: 2 (over core).
Axes of the slice: x: 2, y: 2, z: 4, core: 2. Of those that a mesh axis runs over, the one named last changes fastest.
Arguments:
- clean_tokens: bfloat16 [2048, 4096], P('ctx', 'copy'), may hold values from -36 to 36
- norm_gain: bfloat16 [4096], replicated, may hold values from 0.5 to 1.5
- mask_embed: bfloat16 [4096], replicated, may hold values from -6 to 6
- time_shift: float32 [4096], replicated, may hold values from -0.5 to 0.5
- w_query: bfloat16 [4096, 2048], P(None, 'tp'), may hold values from -0.09375 to 0.09375
- w_key: bfloat16 [4096, 512], P(None, 'tp'), may hold values from -0.09375 to 0.09375
- w_value: bfloat16 [4096, 512], P(None, 'tp'), may hold values from -0.09375 to 0.09375
- w_out: bfloat16 [2048, 4096], P('tp'), may hold values from -0.125 to 0.125
- q_gain: float32 [128], replicated, may hold values from 2 to 3
- k_gain: float32 [128], replicated, may hold values from 0.5 to 1.5
- masked: int32 [2, 2048], P('copy', 'ctx'), may hold values 0 or 1
- block_live: int32 [2, 32], P('copy', 'ctx'), may hold values 0 or 1
- timesteps: int32 [2], P('copy'), may hold values from 1 to 1000
Outputs:
- clean_out: bfloat16 [2048, 4096], P('ctx', 'tp')
- noised_out: bfloat16 [2, 2048, 4096], P('copy', 'ctx', 'tp')
The draws below stay inside these ranges and needn't reach their ends.
All inputs are finite; a program needn't handle non-finite values. No bound on the sum of `masked` or of `block_live` on one device may be relied on, other than what follows from the above.
Results may differ from the reference program's by a relative error of at most 0.012.
The reference program's roundings to bfloat16 on the way count: a program that leaves them out, or rounds other values in their place, can miss the bound.
Values may be sent and summed in bfloat16 or wider, within the bound.
No kernel may reach another device: no remote copies, remote signals or barrier semaphores. Data moves between devices by JAX's collectives and lax.ppermute only.
A program may use at most 320 MiB of HBM per device.

```python
import math
import jax
import jax.numpy as jnp
from jax import lax

D = 4096
H = 16
KVH = 4
HD = 128
BLK = 64
TSTEPS = 1000
SEQ = 2048
NBLK = 32
COPIES = 2


def draw_clean_tokens(key, part):
    key_base = jax.random.fold_in(key, 101)
    key_lines = jax.random.fold_in(key, 102)
    key_features = jax.random.fold_in(key, 103)
    line_scale = jnp.exp(jax.random.uniform(key_lines, (SEQ, 1), minval=math.log(0.3), maxval=math.log(3.0)))
    feature_scale = jnp.exp(jax.random.uniform(key_features, (1, D), minval=math.log(0.3), maxval=math.log(3.0)))
    base = jnp.clip(jax.random.normal(key_base, (SEQ, D)), -4.0, 4.0)
    return (base * line_scale * feature_scale).astype(jnp.bfloat16)


def set_ends(values, rng, smallest, top_value):
    index_at = [jax.random.randint(jax.random.fold_in(rng, axis), (), 0, length) for axis, length in enumerate(values.shape)]
    longest = values.shape.index(max(values.shape))
    next_to = index_at[:longest] + [(index_at[longest] + 1) % values.shape[longest]] + index_at[longest + 1:]
    return values.at[tuple(index_at)].set(smallest).at[tuple(next_to)].set(top_value)


def steps_of(rng, dims, pieces, least, top_value):
    def one(dim, shards_of):
        steps = jax.random.uniform(jax.random.fold_in(jax.random.fold_in(rng, 6), dim), (shards_of,), jnp.float32, least / len(pieces), top_value / len(pieces))
        return jnp.repeat(jnp.exp(steps), dims[dim] // shards_of).reshape((-1,) + (1,) * (len(dims) - dim - 1))

    level = one(*pieces[0])
    for cut in pieces[1:]:
        level = level * one(*cut)
    return level


def scatter_about(own_key, shape, deviation, bound, split=(), kind=jnp.bfloat16):
    result = jax.random.normal(own_key, shape, jnp.float32) * deviation
    if len(split) > 0:
        result = steps_of(own_key, shape, split, -0.22, 0.18) * result
    return jnp.clip(result, min=-bound, max=bound).astype(kind)


def setup_inputs(seed: int = 0) -> dict:
    splits = jax.random.split(jax.random.key(seed), 14)
    clean_tokens = draw_clean_tokens(jax.random.fold_in(splits[13], 71), 0)
    norm_gain = jnp.clip(1.0 + 0.1 * jax.random.normal(splits[1], (D,), jnp.float32), 0.5, 1.5).astype(jnp.bfloat16)
    mask_embed = scatter_about(splits[2], (D,), 1.0, 6.0)
    time_shift = jnp.clip(jax.random.uniform(splits[3], (D,), jnp.float32, -0.5, 0.5), -0.5, 0.5)
    w_query = scatter_about(splits[4], (D, H * HD), D ** -0.5, 0.09375, ((1, 2),))
    w_key = scatter_about(splits[5], (D, KVH * HD), D ** -0.5, 0.09375, ((1, 2),))
    w_value = scatter_about(splits[6], (D, KVH * HD), D ** -0.5, 0.09375, ((1, 2),))
    w_out = scatter_about(splits[7], (H * HD, D), (H * HD) ** -0.5, 0.125, ((0, 2),))
    q_gain = jnp.clip(jax.random.uniform(splits[8], (HD,), jnp.float32, 2.0, 3.0), 2.0, 3.0)
    k_gain = jnp.clip(1.0 + 0.1 * jax.random.normal(splits[9], (HD,), jnp.float32), 0.5, 1.5)
    masked = set_ends((jax.random.randint(splits[10], (COPIES, SEQ), 0, 2) < 1).astype(jnp.int32), jax.random.fold_in(splits[10], 1), 0, 1)
    block_live = set_ends((jax.random.randint(splits[11], (COPIES, NBLK), 0, 4) < 3).astype(jnp.int32), jax.random.fold_in(splits[11], 1), 0, 1)
    timesteps = jax.random.randint(splits[12], (COPIES,), 1, 1001).astype(jnp.int32)
    return {"clean_tokens": clean_tokens, "norm_gain": norm_gain, "mask_embed": mask_embed, "time_shift": time_shift, "w_query": w_query, "w_key": w_key, "w_value": w_value, "w_out": w_out, "q_gain": q_gain, "k_gain": k_gain, "masked": masked, "block_live": block_live, "timesteps": timesteps}


EPS = 1e-06

def inverse_rms(values):
    return lax.rsqrt(lax.optimization_barrier(jnp.mean(values * values, axis=-1, keepdims=True)) + EPS)

def reference(clean_tokens, norm_gain, mask_embed, time_shift, w_query, w_key, w_value, w_out, q_gain, k_gain, masked, block_live, timesteps):
    streams_count = 1 + COPIES
    clean_wide = clean_tokens.astype(jnp.float32)
    gain_wide = norm_gain.astype(jnp.float32)
    normed_clean = (clean_wide * inverse_rms(clean_wide) * gain_wide).astype(jnp.bfloat16)
    noisy_tokens = jnp.where(masked[:, :, None] == 1, mask_embed[None, None, :], clean_tokens[None, :, :])
    noisy_wide = noisy_tokens.astype(jnp.float32)
    condition = 1.0 + timesteps.astype(jnp.float32)[:, None, None] / TSTEPS * time_shift[None, None, :]
    normed_noisy = (noisy_wide * inverse_rms(noisy_wide) * gain_wide * condition).astype(jnp.bfloat16)
    all_rows = jnp.concatenate([normed_clean[None], normed_noisy], axis=0).reshape(-1, D)
    query_wide = jnp.dot(all_rows, w_query, preferred_element_type=jnp.float32).reshape(streams_count, SEQ, H, HD)
    queries = (query_wide * inverse_rms(query_wide) * q_gain).astype(jnp.bfloat16)
    key_wide = jnp.dot(all_rows, w_key, preferred_element_type=jnp.float32).reshape(streams_count, SEQ, KVH, HD)
    key_heads = (key_wide * inverse_rms(key_wide) * k_gain).astype(jnp.bfloat16)
    value_heads = jnp.dot(all_rows, w_value, preferred_element_type=jnp.float32).astype(jnp.bfloat16).reshape(streams_count, SEQ, KVH, HD)
    blocks = jnp.arange(SEQ, dtype=jnp.int32) // BLK
    heads_per_kv = H // KVH
    reciprocal_root = 1.0 / math.sqrt(HD)

    def one_head(pair_index):
        stream_index = pair_index // H
        head_index = pair_index % H
        kv_head = head_index // heads_per_kv
        query_rows = queries[stream_index, :, head_index, :].astype(jnp.float32)
        clean_key = key_heads[0, :, kv_head, :].astype(jnp.float32)
        clean_value = value_heads[0, :, kv_head, :].astype(jnp.float32)
        scores = jnp.dot(query_rows, clean_key.T) * reciprocal_root
        offset = jnp.minimum(stream_index, 1)
        allowed = blocks[None, :] + offset <= blocks[:, None]
        weights = jnp.where(allowed, jnp.exp(scores), 0.0)
        numerator = jnp.dot(weights.astype(jnp.bfloat16).astype(jnp.float32), clean_value)
        denominator = lax.optimization_barrier(jnp.sum(weights, axis=1))
        self_block_key = key_heads[stream_index, :, kv_head, :].astype(jnp.float32).reshape(NBLK, BLK, HD)
        self_block_value = value_heads[stream_index, :, kv_head, :].astype(jnp.float32).reshape(NBLK, BLK, HD)
        self_block_query = query_rows.reshape(NBLK, BLK, HD)
        self_block_scores = jnp.einsum('xau,xvu->xav', self_block_query, self_block_key) * reciprocal_root
        own_flag = offset.astype(jnp.float32)
        self_block_weights = jnp.exp(self_block_scores) * own_flag
        self_numerator = jnp.einsum('osf,ofg->osg', self_block_weights.astype(jnp.bfloat16).astype(jnp.float32), self_block_value)
        numerator = numerator + self_numerator.reshape(SEQ, HD)
        denominator = denominator + lax.optimization_barrier(jnp.sum(self_block_weights, axis=2)).reshape(SEQ)
        return (numerator / denominator[:, None]).astype(jnp.bfloat16)
    attended = lax.map(one_head, jnp.arange(streams_count * H, dtype=jnp.int32))
    attended = attended.reshape(streams_count, H, SEQ, HD).transpose(0, 2, 1, 3).reshape(streams_count * SEQ, H * HD)
    mixed = jnp.dot(attended, w_out, preferred_element_type=jnp.float32)
    clean_out = mixed[:SEQ].astype(jnp.bfloat16)
    live_rows = jnp.repeat(block_live, BLK, axis=1).astype(jnp.float32)
    noised_out = (mixed[SEQ:].reshape(COPIES, SEQ, D) * live_rows[:, :, None]).astype(jnp.bfloat16)
    return (clean_out, noised_out)
```

```python
import functools
import math

import jax
import jax.numpy as jnp
from jax import lax
from jax.experimental import pallas as pl
from jax.experimental.pallas import tpu as pltpu
from jax.sharding import PartitionSpec as P

HD = 128
BLK = 64
TSTEPS = 1000
EPS = 1e-06
VMEM_LIMIT = 48 * 1024 * 1024
F32 = jnp.float32
BF16 = jnp.bfloat16
SCORE_SCALE = math.log2(math.e) / math.sqrt(HD)


def to_column(row, n):
    eye = lax.broadcasted_iota(jnp.int32, (n, n), 0) == lax.broadcasted_iota(jnp.int32, (n, n), 1)
    return jnp.sum(jnp.where(eye, jnp.broadcast_to(row, (n, n)), 0.0), axis=1, keepdims=True)


def row_scales(own_ref, other_ref, mask_ref, embed_ref, width):
    n = own_ref.shape[1]
    clean = lax.rsqrt(to_column(own_ref[...] + other_ref[...], n) * (1.0 / width) + EPS)
    embed = embed_ref[...].astype(F32)
    embed_scale = lax.rsqrt(jnp.sum(embed * embed, axis=1, keepdims=True) * (1.0 / width) + EPS)
    masked = to_column(mask_ref[...].astype(F32), n)
    return clean, embed_scale, masked


def normed_clean(x, clean_scale, gain):
    return (x * clean_scale * gain).astype(BF16)


def normed_noisy(x, clean_scale, embed_scale, masked, gain, embed, condition):
    is_masked = masked == 1.0
    noisy = jnp.where(is_masked, embed, x)
    scale = jnp.where(is_masked, embed_scale, clean_scale)
    return (noisy * scale * gain * condition).astype(BF16)


def dot(a, b):
    return jnp.dot(a, b, preferred_element_type=F32)


def head_norm(wide, gain):
    scale = lax.rsqrt(jnp.mean(wide * wide, axis=1, keepdims=True) + EPS)
    return (wide * scale * gain).astype(BF16)


def kv_out(ref, wide, gain):
    ref[:, :HD] = head_norm(wide[:, :HD], gain)
    ref[:, HD:] = wide[:, HD:].astype(BF16)


def first_half_kernel(
    info, x_ref, own_ref, other_ref, mask_ref, embed_all, gain_ref, embed_ref, shift_ref,
    wq_ref, wka_ref, wva_ref, wkb_ref, wvb_ref, q_ref, a_ref, b_ref, scales, *, width,
):
    step = pl.program_id(0)
    rows = x_ref.shape[0]

    @pl.when(step == 0)
    def _():
        clean, embed_scale, masked = row_scales(own_ref, other_ref, mask_ref, embed_all, width)
        scales[:, 0:1] = clean
        scales[:, 1:2] = jnp.broadcast_to(embed_scale, clean.shape)
        scales[:, 2:3] = masked

    x = x_ref[...].astype(F32)
    gain = gain_ref[...].astype(F32)
    condition = 1.0 + info[3].astype(F32) / TSTEPS * shift_ref[...]
    clean = normed_clean(x, scales[:, 0:1], gain)
    noisy = normed_noisy(
        x, scales[:, 0:1], scales[:, 1:2], scales[:, 2:3], gain, embed_ref[...].astype(F32), condition
    )
    both = jnp.concatenate([clean, noisy], axis=0)
    q = dot(both, wq_ref[...])
    a = dot(both, jnp.concatenate([wka_ref[...], wva_ref[...]], axis=1))
    b = dot(both, jnp.concatenate([wkb_ref[...], wvb_ref[...]], axis=1))

    @pl.when(step == 0)
    def _():
        q_ref[...] = q
        a_ref[...] = a
        b_ref[...] = b

    @pl.when(step > 0)
    def _():
        q_ref[...] += q
        a_ref[...] += a
        b_ref[...] += b


def other_rows(info, xs_ref, xt_ref):
    near, far = xs_ref[...].astype(F32), xt_ref[...].astype(F32)
    first = info[1] == 0
    return jnp.concatenate([jnp.where(first, near, far), jnp.where(first, far, near)], axis=0)


def clean_kv_kernel(
    info, xs_ref, xt_ref, own_ref, other_ref, mask_ref, embed_all, gain_ref,
    wka_ref, wva_ref, wkb_ref, wvb_ref, pa_ref, pb_ref, kgain_ref, a_ref, b_ref, scales, acc, *, width,
):
    step = pl.program_id(0)

    @pl.when(step == 0)
    def _():
        clean, _, _ = row_scales(own_ref, other_ref, mask_ref, embed_all, width)
        scales[...] = clean
        acc[:, : 2 * HD] = pa_ref[...]
        acc[:, 2 * HD :] = pb_ref[...]

    x = other_rows(info, xs_ref, xt_ref)
    clean = normed_clean(x, scales[...], gain_ref[...].astype(F32))
    weights = jnp.concatenate([wka_ref[...], wva_ref[...], wkb_ref[...], wvb_ref[...]], axis=1)
    acc[...] += dot(clean, weights)

    @pl.when(step == pl.num_programs(0) - 1)
    def _():
        kv_out(a_ref, acc[:, : 2 * HD], kgain_ref[...])
        kv_out(b_ref, acc[:, 2 * HD :], kgain_ref[...])


def second_half_kernel(
    info, xs_ref, xt_ref, own_ref, other_ref, mask_ref, embed_all, gain_ref, embed_ref, shift_ref,
    wq_ref, wka_ref, wva_ref, wkb_ref, wvb_ref, pq_ref, pa_ref, pb_ref, qgain_ref, kgain_ref,
    q_ref, a_ref, b_ref, scales, acc_q, acc_kv, *, width,
):
    step = pl.program_id(0)

    @pl.when(step == 0)
    def _():
        clean, embed_scale, masked = row_scales(own_ref, other_ref, mask_ref, embed_all, width)
        scales[:, 0:1] = clean
        scales[:, 1:2] = jnp.broadcast_to(embed_scale, clean.shape)
        scales[:, 2:3] = masked
        acc_q[...] = pq_ref[...]
        acc_kv[:, : 2 * HD] = pa_ref[...]
        acc_kv[:, 2 * HD :] = pb_ref[...]

    x = other_rows(info, xs_ref, xt_ref)
    gain = gain_ref[...].astype(F32)
    condition = 1.0 + info[3].astype(F32) / TSTEPS * shift_ref[...]
    clean = normed_clean(x, scales[:, 0:1], gain)
    noisy = normed_noisy(
        x, scales[:, 0:1], scales[:, 1:2], scales[:, 2:3], gain, embed_ref[...].astype(F32), condition
    )
    acc_q[...] += dot(jnp.concatenate([clean, noisy], axis=0), wq_ref[...])
    weights = jnp.concatenate([wka_ref[...], wva_ref[...], wkb_ref[...], wvb_ref[...]], axis=1)
    acc_kv[...] += dot(noisy, weights)

    @pl.when(step == pl.num_programs(0) - 1)
    def _():
        for head in range(q_ref.shape[1] // HD):
            cols = slice(head * HD, (head + 1) * HD)
            q_ref[:, cols] = head_norm(acc_q[:, cols], qgain_ref[...])
        kv_out(a_ref, acc_kv[:, : 2 * HD], kgain_ref[...])
        kv_out(b_ref, acc_kv[:, 2 * HD :], kgain_ref[...])


def terms(q, kv_ref, mask):
    scores = lax.dot_general(
        q, kv_ref[:, :HD], (((1,), (1,)), ((), ())), preferred_element_type=F32
    )
    e = jnp.exp2(scores * SCORE_SCALE)
    if mask is not None:
        e = jnp.where(mask, e, 0.0)
    den = e[:, :HD]
    for start in range(HD, e.shape[1], HD):
        den = den + e[:, start : start + HD]
    return dot(e.astype(BF16), kv_ref[:, HD:]), den


def attention_first_kernel(info, q_ref, kv_ref, self_ref, near_ref, num_ref, den_ref):
    rows = kv_ref.shape[0]
    row_block = lax.broadcasted_iota(jnp.int32, (rows, rows), 0) // BLK
    key_block = lax.broadcasted_iota(jnp.int32, (rows, rows), 1) // BLK
    q_clean, q_noisy = q_ref[:rows], q_ref[rows:]
    num, den = terms(q_clean, kv_ref, key_block <= row_block)
    num_ref[:rows], den_ref[:rows] = num, den
    num, den = terms(q_noisy, kv_ref, key_block < row_block)
    own_num, own_den = terms(q_noisy, self_ref, key_block == row_block)
    num_ref[rows:], den_ref[rows:] = num + own_num, den + own_den

    @pl.when(info[2] % 2 == 1)
    def _():
        for part in range(2):
            cut = slice(part * rows, (part + 1) * rows)
            num, den = terms(q_ref[cut], near_ref, None)
            num_ref[cut] += num
            den_ref[cut] += den


def attention_later_kernel(info, q_ref, *refs, offsets, last):
    kv_refs = refs[: len(offsets)]
    num_in, den_in = refs[len(offsets) : len(offsets) + 2]
    rest = refs[len(offsets) + 2 :]
    num_ref, den_ref = rest[-2:]
    rows = kv_refs[0].shape[0]
    num_ref[...] = num_in[...]
    den_ref[...] = den_in[...]
    for offset, kv_ref in zip(offsets, kv_refs):
        @pl.when(jnp.bitwise_xor(info[2], offset) < info[2])
        def _(kv_ref=kv_ref):
            for part in range(2):
                cut = slice(part * rows, (part + 1) * rows)
                num, den = terms(q_ref[cut], kv_ref, None)
                num_ref[cut] += num
                den_ref[cut] += den

    if last:
        total = jnp.sum(den_ref[...], axis=1, keepdims=True)
        rest[0][...] = (num_ref[...] / total).astype(BF16)


def out_kernel(info, live, ga, gb, ha, hb, wga, wgb, wha, whb, clean_ref, noisy_ref):
    mixed = dot(ga[...], wga[...]) + dot(gb[...], wgb[...]) + dot(ha[...], wha[...]) + dot(hb[...], whb[...])
    rows = clean_ref.shape[0]
    clean_ref[...] = mixed[:rows].astype(BF16)
    for block in range(rows // BLK):
        part = mixed[rows + block * BLK : rows + (block + 1) * BLK]
        noisy_ref[block * BLK : (block + 1) * BLK] = (part * live[block].astype(F32)).astype(BF16)


def call(kernel, grid, scalars, ins, outs, scratch, arrays, flops, num_bytes, exps=0, aliases=None):
    return pl.pallas_call(
        kernel,
        grid_spec=pltpu.PrefetchScalarGridSpec(
            num_scalar_prefetch=len(scalars),
            grid=(grid,),
            in_specs=ins,
            out_specs=[spec for spec, _ in outs],
            scratch_shapes=scratch,
        ),
        out_shape=[shape for _, shape in outs],
        compiler_params=pltpu.CompilerParams(vmem_limit_bytes=VMEM_LIMIT),
        cost_estimate=pl.CostEstimate(flops=flops, bytes_accessed=num_bytes, transcendentals=exps),
        input_output_aliases=aliases or {},
    )(*scalars, *arrays)


def on_device(
    mesh, clean_tokens, norm_gain, mask_embed, time_shift, w_query, w_key, w_value, w_out,
    q_gain, k_gain, masked, block_live, timesteps,
):
    rows, half = clean_tokens.shape
    width = norm_gain.shape[0]
    heads_width = w_query.shape[1]
    part = heads_width // 2
    group = part // HD
    ctx = mesh.shape["ctx"]
    c, p, t = lax.axis_index("copy"), lax.axis_index("ctx"), lax.axis_index("tp")
    info = jnp.stack([c, t, p, timesteps[0]]).astype(jnp.int32)
    pair = [(0, 1), (1, 0)]
    cross_x = lambda v: lax.ppermute(v, "copy", pair)
    cross_core = lambda v: lax.ppermute(v, "tp", pair)
    cross_ctx = lambda v, offset: lax.ppermute(v, "ctx", [(i, i ^ offset) for i in range(ctx)])

    cut = rows // 2
    near = cross_x(lax.dynamic_slice_in_dim(clean_tokens, t * cut, cut, 0))
    wide = clean_tokens.astype(F32)
    squares = jnp.sum(wide * wide, axis=1)
    other_squares = cross_x(squares)
    far = cross_core(near)
    out_cols = w_out.shape[1] // 2
    w_far = cross_core(lax.dynamic_slice_in_dim(w_out, (1 - t) * out_cols, out_cols, 1))

    gain2, embed2, shift2 = norm_gain[None], mask_embed[None], time_shift[None]
    squares2, other2 = squares[None], other_squares[None]
    qg, kg = q_gain[None], k_gain[None]
    depth = 512
    steps = half // depth
    full = lambda shape: pl.BlockSpec(shape, lambda k, s: (0,) * len(shape))

    def depth_specs(own):
        at = (lambda k, s: s[0] * steps + k) if own else (lambda k, s: (1 - s[0]) * steps + k)
        vec = pl.BlockSpec((1, depth), lambda k, s: (0, at(k, s)))
        wq = pl.BlockSpec((depth, heads_width), lambda k, s: (at(k, s), 0))
        wa = pl.BlockSpec((depth, HD), lambda k, s: (at(k, s), s[0]))
        wb = pl.BlockSpec((depth, HD), lambda k, s: (at(k, s), 1 - s[0]))
        return vec, wq, wa, wb

    stats = [full((1, rows)), full((1, rows)), full((1, rows)), full((1, width))]
    stat_arrays = [squares2, other2, masked, embed2]
    shape = jax.ShapeDtypeStruct
    kv_shape = shape((rows, 2 * HD), BF16)

    vec, wq, wa, wb = depth_specs(True)
    pq, pa, pb = call(
        functools.partial(first_half_kernel, width=width), steps, [info],
        [pl.BlockSpec((rows, depth), lambda k, s: (0, k))] + stats + [vec, vec, vec, wq, wa, wa, wb, wb],
        [
            (full((2 * rows, heads_width)), shape((2 * rows, heads_width), F32)),
            (full((2 * rows, 2 * HD)), shape((2 * rows, 2 * HD), F32)),
            (full((2 * rows, 2 * HD)), shape((2 * rows, 2 * HD), F32)),
        ],
        [pltpu.VMEM((rows, HD), F32)],
        [clean_tokens] + stat_arrays + [gain2, embed2, shift2, w_query, w_key, w_value, w_key, w_value],
        2 * 2 * rows * half * (heads_width + 4 * HD), half * (heads_width + 4 * HD) * 2,
    )

    vec, wq, wa, wb = depth_specs(False)
    strip = pl.BlockSpec((cut, depth), lambda k, s: (0, k))
    top = pl.BlockSpec((rows, 2 * HD), lambda k, s: (0, 0))
    bottom = pl.BlockSpec((rows, 2 * HD), lambda k, s: (1, 0))
    kva, kvb = call(
        functools.partial(clean_kv_kernel, width=width), steps, [info],
        [strip, strip] + stats + [vec, wa, wa, wb, wb, top, top, full((1, HD))],
        [(top, kv_shape), (top, kv_shape)],
        [pltpu.VMEM((rows, 1), F32), pltpu.VMEM((rows, 4 * HD), F32)],
        [near, far] + stat_arrays + [gain2, w_key, w_value, w_key, w_value, pa, pb, kg],
        2 * rows * half * 4 * HD, half * 4 * HD * 2,
    )

    a = {0: kva, 1: cross_ctx(kva, 1)}
    b = {0: kvb, 1: cross_ctx(kvb, 1)}
    for offset in range(2, ctx, 2):
        a[offset] = cross_ctx(kva, offset)
    for offset in range(2, ctx, 2):
        a[offset + 1] = cross_ctx(a[offset], 1)
        b[offset] = cross_x(a[offset])
        b[offset + 1] = cross_x(a[offset + 1])

    q, sa, sb = call(
        functools.partial(second_half_kernel, width=width), steps, [info],
        [strip, strip] + stats + [vec, vec, vec, wq, wa, wa, wb, wb]
        + [full((2 * rows, heads_width)), bottom, bottom, full((1, HD)), full((1, HD))],
        [(full((2 * rows, heads_width)), shape((2 * rows, heads_width), BF16)), (top, kv_shape), (top, kv_shape)],
        [pltpu.VMEM((rows, HD), F32), pltpu.VMEM((2 * rows, heads_width), F32), pltpu.VMEM((rows, 4 * HD), F32)],
        [near, far] + stat_arrays
        + [gain2, embed2, shift2, w_query, w_key, w_value, w_key, w_value, pq, pa, pb, qg, kg],
        2 * 2 * rows * half * heads_width + 2 * rows * half * 4 * HD, half * (heads_width + 4 * HD) * 2,
    )

    def attend(which, pieces, own):
        head = lambda h, s: (0, (s[0] if which == 0 else 1 - s[0]) * group + h)
        qspec = pl.BlockSpec((2 * rows, HD), head)
        acc = pl.BlockSpec((2 * rows, HD), lambda h, s: (0, h))
        acc_shape = shape((2 * rows, part), F32)
        kv_spec = full((rows, 2 * HD))
        unit = 2 * rows * rows * group
        num, den = call(
            attention_first_kernel, group, [info], [qspec] + [kv_spec] * 3,
            [(acc, acc_shape), (acc, acc_shape)], [], [q, pieces[0], own, pieces[1]],
            3 * unit * HD * 4, 3 * rows * HD * 4, 3 * unit,
        )
        offsets = list(range(2, ctx))
        middle, final = offsets[:-2], offsets[-2:]
        if middle:
            num, den = call(
                functools.partial(attention_later_kernel, offsets=middle, last=False), group, [info],
                [qspec] + [kv_spec] * len(middle) + [acc, acc],
                [(acc, acc_shape), (acc, acc_shape)], [], [q] + [pieces[o] for o in middle] + [num, den],
                len(middle) * unit * HD * 4, len(middle) * rows * HD * 4, len(middle) * unit,
            )
        return call(
            functools.partial(attention_later_kernel, offsets=final, last=True), group, [info],
            [qspec] + [kv_spec] * len(final) + [acc, acc],
            [(acc, shape((2 * rows, part), BF16))],
            [pltpu.VMEM((2 * rows, HD), F32), pltpu.VMEM((2 * rows, HD), F32)],
            [q] + [pieces[o] for o in final] + [num, den],
            len(final) * unit * HD * 4, len(final) * rows * HD * 4, len(final) * unit,
        )[0]

    ga = attend(0, a, sa)
    ha = cross_core(ga)
    gb = attend(1, b, sb)
    hb = cross_core(gb)

    tile = 512
    tiles = out_cols // tile
    att = pl.BlockSpec((2 * rows, part), lambda n, s, l: (0, 0))
    wide_tile = lambda which, base: pl.BlockSpec(
        (part, tile),
        lambda n, s, l: (s[0] if which == 0 else 1 - s[0], s[1] * base + n),
    )
    out = pl.BlockSpec((rows, tile), lambda n, s, l: (0, n))
    clean_out, noised_out = call(
        out_kernel, tiles, [info, block_live[0]],
        [att] * 4 + [wide_tile(0, tiles), wide_tile(1, tiles), wide_tile(0, 0), wide_tile(1, 0)],
        [(out, shape((rows, out_cols), BF16)), (out, shape((rows, out_cols), BF16))], [],
        [ga, gb, ha, hb, w_out, w_out, w_far, w_far],
        2 * 2 * rows * 2 * heads_width * out_cols, 2 * heads_width * out_cols * 2,
    )
    return (clean_out, noised_out[None])


def solution(mesh):
    in_specs = (
        P("ctx", "copy"),
        P(),
        P(),
        P(),
        P(None, "tp"),
        P(None, "tp"),
        P(None, "tp"),
        P("tp", None),
        P(),
        P(),
        P("copy", "ctx"),
        P("copy", "ctx"),
        P("copy"),
    )
    out_specs = (P("ctx", "tp"), P("copy", "ctx", "tp"))
    return jax.shard_map(
        functools.partial(on_device, mesh), mesh=mesh, in_specs=in_specs, out_specs=out_specs, check_vma=False
    )
```

```python
import functools
import math

import jax
import jax.numpy as jnp
from jax import lax
from jax.experimental import pallas as pl
from jax.experimental.pallas import tpu as pltpu
from jax.sharding import PartitionSpec as P

HD = 128
BLK = 64
TSTEPS = 1000
EPS = 1e-06
VMEM_LIMIT = 32 * 1024 * 1024
F32 = jnp.float32
BF16 = jnp.bfloat16
SCORE_SCALE = math.log2(math.e) / math.sqrt(HD)


def to_column(row, n):
    eye = lax.broadcasted_iota(jnp.int32, (n, n), 0) == lax.broadcasted_iota(jnp.int32, (n, n), 1)
    return jnp.sum(jnp.where(eye, jnp.broadcast_to(row, (n, n)), 0.0), axis=1, keepdims=True)


def row_scales(own_ref, other_ref, mask_ref, embed_ref, width):
    n = own_ref.shape[1]
    clean = lax.rsqrt(to_column(own_ref[...] + other_ref[...], n) * (1.0 / width) + EPS)
    embed = embed_ref[...].astype(F32)
    embed_scale = lax.rsqrt(jnp.sum(embed * embed, axis=1, keepdims=True) * (1.0 / width) + EPS)
    masked = to_column(mask_ref[...].astype(F32), n)
    return clean, embed_scale, masked


def normed_clean(x, clean_scale, gain):
    return (x * clean_scale * gain).astype(BF16)


def normed_noisy(x, clean_scale, embed_scale, masked, gain, embed, condition):
    is_masked = masked == 1.0
    noisy = jnp.where(is_masked, embed, x)
    scale = jnp.where(is_masked, embed_scale, clean_scale)
    return (noisy * scale * gain * condition).astype(BF16)


def dot(a, b):
    return jnp.dot(a, b, preferred_element_type=F32)


def head_norm(wide, gain):
    scale = lax.rsqrt(jnp.mean(wide * wide, axis=1, keepdims=True) + EPS)
    return (wide * scale * gain).astype(BF16)


def both_streams(x, scales, gain, embed, condition):
    clean = normed_clean(x, scales[0], gain)
    noisy = normed_noisy(x, scales[0], scales[1], scales[2], gain, embed, condition)
    return clean, noisy


def half_vectors(at, info, gain_ref, embed_ref, shift_ref):
    gain = gain_ref[:, at].astype(F32)
    embed = embed_ref[:, at].astype(F32)
    condition = 1.0 + info[3].astype(F32) / TSTEPS * shift_ref[:, at]
    return gain, embed, condition


def first_half_kernel(
    info, x_ref, own_ref, other_ref, mask_ref, gain_ref, embed_ref, shift_ref,
    wq_ref, wk_ref, wv_ref, w_out, q_ref, k_ref, v_ref, w_send, w_mine, sems,
):
    half = x_ref.shape[1]
    cols = w_send.shape[1]
    moves = []
    for number, (target, side) in enumerate(((w_send, 1 - info[1]), (w_mine, info[1]))):
        start = pl.multiple_of(side * cols, 128)
        moves.append(pltpu.make_async_copy(w_out.at[:, pl.ds(start, cols)], target, sems.at[number]))
        moves[-1].start()
    scales = row_scales(own_ref, other_ref, mask_ref, embed_ref, embed_ref.shape[1])
    at = pl.ds(pl.multiple_of(info[0] * half, 128), half)
    gain, embed, condition = half_vectors(at, info, gain_ref, embed_ref, shift_ref)
    clean, noisy = both_streams(x_ref[...].astype(F32), scales, gain, embed, condition)
    both = jnp.concatenate([clean, noisy], axis=0)
    k_ref[...] = dot(both, wk_ref[at])
    v_ref[...] = dot(both, wv_ref[at])
    q_ref[...] = dot(both, wq_ref[at])
    for move in moves:
        move.wait()


def other_rows(info, near_ref, far_ref):
    near, far = near_ref[...].astype(F32), far_ref[...].astype(F32)
    first = info[1] == 0
    return jnp.concatenate([jnp.where(first, near, far), jnp.where(first, far, near)], axis=0)


def kv_out(ref, k, v, gain):
    for head in range(k.shape[1] // HD):
        cols = slice(head * HD, (head + 1) * HD)
        ref[:, 2 * head * HD : (2 * head + 1) * HD] = head_norm(k[:, cols], gain)
        ref[:, (2 * head + 1) * HD : 2 * (head + 1) * HD] = v[:, cols].astype(BF16)


def clean_kv_kernel(
    info, near_ref, far_ref, own_ref, other_ref, mask_ref, gain_ref, embed_ref,
    wk_ref, wv_ref, pk_ref, pv_ref, kgain_ref, all_ref, one_ref,
):
    half = near_ref.shape[1]
    rows = all_ref.shape[0]
    clean_scale = row_scales(own_ref, other_ref, mask_ref, embed_ref, embed_ref.shape[1])[0]
    at = pl.ds(pl.multiple_of((1 - info[0]) * half, 128), half)
    clean = normed_clean(other_rows(info, near_ref, far_ref), clean_scale, gain_ref[:, at].astype(F32))
    k = pk_ref[:rows] + dot(clean, wk_ref[at])
    v = pv_ref[:rows] + dot(clean, wv_ref[at])
    kv_out(all_ref, k, v, kgain_ref[...])
    width = one_ref.shape[1]
    one_ref[...] = all_ref[:, pl.ds(pl.multiple_of(info[0] * width, 128), width)]


def second_half_kernel(
    info, near_ref, far_ref, own_ref, other_ref, mask_ref, gain_ref, embed_ref, shift_ref,
    wq_ref, wk_ref, wv_ref, pq_ref, pk_ref, pv_ref, qgain_ref, kgain_ref, q_ref, self_ref,
):
    half = near_ref.shape[1]
    rows = self_ref.shape[0]
    scales = row_scales(own_ref, other_ref, mask_ref, embed_ref, embed_ref.shape[1])
    at = pl.ds(pl.multiple_of((1 - info[0]) * half, 128), half)
    gain, embed, condition = half_vectors(at, info, gain_ref, embed_ref, shift_ref)
    clean, noisy = both_streams(other_rows(info, near_ref, far_ref), scales, gain, embed, condition)
    k = pk_ref[rows:] + dot(noisy, wk_ref[at])
    v = pv_ref[rows:] + dot(noisy, wv_ref[at])
    kv_out(self_ref, k, v, kgain_ref[...])
    q = pq_ref[...] + dot(jnp.concatenate([clean, noisy], axis=0), wq_ref[at])
    for head in range(q_ref.shape[1] // HD):
        cols = slice(head * HD, (head + 1) * HD)
        q_ref[:, cols] = head_norm(q[:, cols], qgain_ref[...])


def terms(q, k, v, mask):
    scores = lax.dot_general(q, k, (((1,), (1,)), ((), ())), preferred_element_type=F32)
    e = jnp.exp2(scores * SCORE_SCALE)
    if mask is not None:
        e = jnp.where(mask, e, 0.0)
    den = e[:, :HD]
    for start in range(HD, e.shape[1], HD):
        den = den + e[:, start : start + HD]
    return dot(e.astype(BF16), v), den


def add_pieces(q_ref, num_ref, den_ref, first_head, heads, pieces, rows):
    k = jnp.concatenate([piece[:, :HD] for piece in pieces], axis=0)
    v = jnp.concatenate([piece[:, HD:] for piece in pieces], axis=0)
    for head in range(first_head, first_head + heads):
        cols = slice(head * HD, (head + 1) * HD)
        for part in range(2):
            cut = slice(part * rows, (part + 1) * rows)
            num, den = terms(q_ref[cut, cols], k, v, None)
            num_ref[cut, cols] += num
            den_ref[cut, cols] += den


def attention_first_kernel(info, q_ref, kv_ref, self_ref, near_ref, num_ref, den_ref):
    rows = kv_ref.shape[0]
    kv_heads = kv_ref.shape[1] // (2 * HD)
    group = q_ref.shape[1] // HD // kv_heads
    row_block = lax.broadcasted_iota(jnp.int32, (rows, rows), 0) // BLK
    key_block = lax.broadcasted_iota(jnp.int32, (rows, rows), 1) // BLK
    both = jnp.concatenate([key_block < row_block, key_block == row_block], axis=1)
    for kv_head in range(kv_heads):
        k_cols = slice(2 * kv_head * HD, (2 * kv_head + 1) * HD)
        v_cols = slice((2 * kv_head + 1) * HD, 2 * (kv_head + 1) * HD)
        k, v = kv_ref[:, k_cols], kv_ref[:, v_cols]
        k_both = jnp.concatenate([k, self_ref[:, k_cols]], axis=0)
        v_both = jnp.concatenate([v, self_ref[:, v_cols]], axis=0)
        for head in range(kv_head * group, (kv_head + 1) * group):
            cols = slice(head * HD, (head + 1) * HD)
            num_ref[:rows, cols], den_ref[:rows, cols] = terms(q_ref[:rows, cols], k, v, key_block <= row_block)
            num_ref[rows:, cols], den_ref[rows:, cols] = terms(q_ref[rows:, cols], k_both, v_both, both)

    @pl.when(info[2] % 2 == 1)
    def _():
        for kv_head in range(kv_heads):
            piece = near_ref[:, 2 * kv_head * HD : 2 * (kv_head + 1) * HD]
            add_pieces(q_ref, num_ref, den_ref, kv_head * group, group, [piece], rows)


def attention_near_kernel(info, q_ref, num_in, den_in, left_ref, right_ref, num_ref, den_ref):
    rows = left_ref.shape[0]
    kv_heads = left_ref.shape[1] // (2 * HD)
    group = q_ref.shape[1] // HD // kv_heads
    num_ref[...] = num_in[...]
    den_ref[...] = den_in[...]

    @pl.when(jnp.bitwise_xor(info[2], 2) < info[2])
    def _():
        for kv_head in range(kv_heads):
            cols = slice(2 * kv_head * HD, 2 * (kv_head + 1) * HD)
            add_pieces(
                q_ref, num_ref, den_ref, kv_head * group, group, [left_ref[:, cols], right_ref[:, cols]], rows
            )


def attention_far_kernel(info, q_all, num_in, den_in, *refs, offsets, which):
    kv_refs = refs[: 2 * len(offsets)]
    out_ref, q_ref, num_ref, den_ref = refs[2 * len(offsets) :]
    rows = kv_refs[0].shape[0] if kv_refs else out_ref.shape[0] // 2
    width = out_ref.shape[1]
    at = pl.ds(pl.multiple_of((info[0] if which == 0 else 1 - info[0]) * width, 128), width)
    q_ref[...] = q_all[:, at]
    num_ref[...] = num_in[:, at]
    den_ref[...] = den_in[:, at]
    for number, offset in enumerate(offsets):
        @pl.when(jnp.bitwise_xor(info[2], offset) < info[2])
        def _(number=number):
            pieces = [kv_refs[2 * number][...], kv_refs[2 * number + 1][...]]
            add_pieces(q_ref, num_ref, den_ref, 0, width // HD, pieces, rows)

    for head in range(width // HD):
        cols = slice(head * HD, (head + 1) * HD)
        total = jnp.sum(den_ref[:, cols], axis=1, keepdims=True)
        out_ref[:, cols] = (num_ref[:, cols] / total).astype(BF16)


def out_kernel(info, live, ga, gb, ha, hb, w_mine, w_far, clean_ref, noisy_ref):
    rows, tile = clean_ref.shape
    part = ga.shape[1]
    cols = pl.ds(pl.multiple_of(pl.program_id(0) * tile, 128), tile)
    first = pl.ds(pl.multiple_of(info[0] * part, 128), part)
    second = pl.ds(pl.multiple_of((1 - info[0]) * part, 128), part)
    mixed = dot(ga[...], w_mine[first, cols]) + dot(gb[...], w_mine[second, cols])
    mixed = mixed + dot(ha[...], w_far[first, cols]) + dot(hb[...], w_far[second, cols])
    clean_ref[...] = mixed[:rows].astype(BF16)
    for block in range(rows // BLK):
        part_rows = mixed[rows + block * BLK : rows + (block + 1) * BLK]
        noisy_ref[block * BLK : (block + 1) * BLK] = (part_rows * live[block].astype(F32)).astype(BF16)


WHOLE = pl.BlockSpec(memory_space=pltpu.VMEM)
HBM = pl.BlockSpec(memory_space=pl.ANY)


def call(kernel, scalars, ins, outs, arrays, flops, num_bytes, scratch=(), exps=0, grid=1):
    return pl.pallas_call(
        kernel,
        grid_spec=pltpu.PrefetchScalarGridSpec(
            num_scalar_prefetch=len(scalars),
            grid=(grid,),
            in_specs=ins,
            out_specs=[spec for spec, _ in outs],
            scratch_shapes=list(scratch),
        ),
        out_shape=[shape for _, shape in outs],
        compiler_params=pltpu.CompilerParams(vmem_limit_bytes=VMEM_LIMIT),
        cost_estimate=pl.CostEstimate(flops=flops, bytes_accessed=num_bytes, transcendentals=exps),
    )(*scalars, *arrays)


def on_device(
    mesh, clean_tokens, norm_gain, mask_embed, time_shift, w_query, w_key, w_value, w_out,
    q_gain, k_gain, masked, block_live, timesteps,
):
    rows, half = clean_tokens.shape
    heads_width = w_query.shape[1]
    kv_width = w_key.shape[1]
    part = heads_width // 2
    ctx = mesh.shape["ctx"]
    c, p, t = lax.axis_index("copy"), lax.axis_index("ctx"), lax.axis_index("tp")
    info = jnp.stack([c, t, p, timesteps[0]]).astype(jnp.int32)
    pair = [(0, 1), (1, 0)]
    cross_x = lambda v: lax.ppermute(v, "copy", pair)
    cross_core = lambda v: lax.ppermute(v, "tp", pair)
    cross_ctx = lambda v, offset: lax.ppermute(v, "ctx", [(i, i ^ offset) for i in range(ctx)])
    shape = jax.ShapeDtypeStruct

    cut = rows // 2
    near = cross_x(lax.dynamic_slice_in_dim(clean_tokens, t * cut, cut, 0))
    wide = clean_tokens.astype(F32)
    squares = jnp.sum(wide * wide, axis=1)
    other_squares = cross_x(squares)
    out_cols = w_out.shape[1] // 2
    stats = [squares[None], other_squares[None], masked]
    vectors = [norm_gain[None], mask_embed[None], time_shift[None]]
    qg, kg = q_gain[None], k_gain[None]

    w_half = shape((heads_width, out_cols), BF16)
    pq, pk, pv, w_send, w_mine = call(
        first_half_kernel, [info], [WHOLE] * 10 + [HBM],
        [
            (WHOLE, shape((2 * rows, heads_width), F32)),
            (WHOLE, shape((2 * rows, kv_width), F32)),
            (WHOLE, shape((2 * rows, kv_width), F32)),
            (HBM, w_half),
            (HBM, w_half),
        ],
        [clean_tokens] + stats + vectors + [w_query, w_key, w_value, w_out],
        2 * 2 * rows * half * (heads_width + 2 * kv_width), 4 * heads_width * out_cols * 2,
        [pltpu.SemaphoreType.DMA((2,))],
    )
    near, pk = lax.optimization_barrier((near, pk))
    far = cross_core(near)

    kv, kva = call(
        clean_kv_kernel, [info], [WHOLE] * 12,
        [(WHOLE, shape((rows, 2 * kv_width), BF16)), (WHOLE, shape((rows, kv_width), BF16))],
        [near, far] + stats + vectors[:2] + [w_key, w_value, pk, pv, kg],
        2 * rows * half * 2 * kv_width, half * 2 * kv_width * 2,
    )

    far_pieces = [{}, {}]
    beside = cross_ctx(kv, 1)
    left = cross_ctx(kv, 2) if ctx > 2 else None
    offsets = list(range(4, ctx, 2))
    for offset in offsets:
        far_pieces[0][offset] = cross_ctx(kva, offset)
    right = cross_ctx(left, 1) if ctx > 2 else None
    for offset in offsets:
        far_pieces[0][offset + 1] = cross_ctx(far_pieces[0][offset], 1)
        far_pieces[1][offset] = cross_x(far_pieces[0][offset])
        far_pieces[1][offset + 1] = cross_x(far_pieces[0][offset + 1])

    q, own = call(
        second_half_kernel, [info], [WHOLE] * 16,
        [(WHOLE, shape((2 * rows, heads_width), BF16)), (WHOLE, shape((rows, 2 * kv_width), BF16))],
        [near, far] + stats + vectors + [w_query, w_key, w_value, pq, pk, pv, qg, kg],
        2 * 2 * rows * half * heads_width + 2 * rows * half * 2 * kv_width, half * (heads_width + 2 * kv_width) * 2,
    )
    w_send, q = lax.optimization_barrier((w_send, q))
    w_far = cross_core(w_send)

    acc = (WHOLE, shape((2 * rows, heads_width), F32))
    unit = 2 * rows * rows * (heads_width // HD)
    num, den = call(
        attention_first_kernel, [info], [WHOLE] * 4, [acc, acc], [q, kv, own, beside],
        5 * unit * HD * 2, unit * 8, exps=2 * unit,
    )
    if ctx > 2:
        num, den = call(
            attention_near_kernel, [info], [WHOLE] * 5, [acc, acc], [q, num, den, left, right],
            2 * unit * HD * 4, unit * 8, exps=2 * unit,
        )

    def far_part(which):
        pieces = [far_pieces[which][o + side] for o in offsets for side in (0, 1)]
        return call(
            functools.partial(attention_far_kernel, offsets=offsets, which=which), [info],
            [WHOLE] * (3 + len(pieces)), [(WHOLE, shape((2 * rows, part), BF16))], [q, num, den] + pieces,
            len(pieces) * unit * HD * 2, unit * 8,
            [pltpu.VMEM((2 * rows, part), BF16)] + [pltpu.VMEM((2 * rows, part), F32)] * 2,
            exps=len(pieces) * unit // 2,
        )[0]

    ga = far_part(0)
    ha = cross_core(ga)
    gb = far_part(1)
    hb = cross_core(gb)

    tile = 512
    out = pl.BlockSpec((rows, tile), lambda n, s, l: (0, n))
    out_shape = shape((rows, out_cols), BF16)
    clean_out, noised_out = call(
        out_kernel, [info, block_live[0]], [WHOLE] * 6, [(out, out_shape), (out, out_shape)],
        [ga, gb, ha, hb, w_mine, w_far],
        2 * 2 * rows * 2 * heads_width * out_cols, 2 * heads_width * out_cols * 2, grid=out_cols // tile,
    )
    return (clean_out, noised_out[None])


def solution(mesh):
    in_specs = (
        P("ctx", "copy"),
        P(),
        P(),
        P(),
        P(None, "tp"),
        P(None, "tp"),
        P(None, "tp"),
        P("tp", None),
        P(),
        P(),
        P("copy", "ctx"),
        P("copy", "ctx"),
        P("copy"),
    )
    out_specs = (P("ctx", "tp"), P("copy", "ctx", "tp"))
    return jax.shard_map(
        functools.partial(on_device, mesh), mesh=mesh, in_specs=in_specs, out_specs=out_specs, check_vma=False
    )
```

```python
import functools
import math

import jax
import jax.numpy as jnp
from jax import lax
from jax.experimental import pallas as pl
from jax.experimental.pallas import tpu as pltpu
from jax.sharding import PartitionSpec as P

HD = 128
BLK = 64
TSTEPS = 1000
EPS = 1e-06
F32 = jnp.float32
BF16 = jnp.bfloat16
SCORE_SCALE = math.log2(math.e) / math.sqrt(HD)


def to_column(row, n):
    eye = lax.broadcasted_iota(jnp.int32, (n, n), 0) == lax.broadcasted_iota(jnp.int32, (n, n), 1)
    return jnp.sum(jnp.where(eye, jnp.broadcast_to(row, (n, n)), 0.0), axis=1, keepdims=True)


def row_scales(own_ref, other_ref, mask_ref, embed_ref, width):
    n = own_ref.shape[1]
    clean = lax.rsqrt(to_column(own_ref[...] + other_ref[...], n) * (1.0 / width) + EPS)
    embed = embed_ref[...].astype(F32)
    embed_scale = lax.rsqrt(jnp.sum(embed * embed, axis=1, keepdims=True) * (1.0 / width) + EPS)
    masked = to_column(mask_ref[...].astype(F32), n)
    return clean, embed_scale, masked


def normed_clean(x, clean_scale, gain):
    return (x * clean_scale * gain).astype(BF16)


def normed_noisy(x, clean_scale, embed_scale, masked, gain, embed, condition):
    is_masked = masked == 1.0
    noisy = jnp.where(is_masked, embed, x)
    scale = jnp.where(is_masked, embed_scale, clean_scale)
    return (noisy * scale * gain * condition).astype(BF16)


def dot(a, b):
    return jnp.dot(a, b, preferred_element_type=F32)


def head_norm(wide, gain):
    scale = lax.rsqrt(jnp.mean(wide * wide, axis=1, keepdims=True) + EPS)
    return (wide * scale * gain).astype(BF16)


def both_streams(x, scales, gain, embed, condition):
    clean = normed_clean(x, scales[0], gain)
    noisy = normed_noisy(x, scales[0], scales[1], scales[2], gain, embed, condition)
    return clean, noisy


def half_vectors(at, info, gain_ref, embed_ref, shift_ref):
    gain = gain_ref[:, at].astype(F32)
    embed = embed_ref[:, at].astype(F32)
    condition = 1.0 + info[3].astype(F32) / TSTEPS * shift_ref[:, at]
    return gain, embed, condition


def both_streams(x, scales, gain, embed, condition):
    clean = normed_clean(x, scales[0], gain)
    noisy = normed_noisy(x, scales[0], scales[1], scales[2], gain, embed, condition)
    return clean, noisy


def vectors_at(at, info, gain_ref, embed_ref, shift_ref):
    gain = gain_ref[:, at].astype(F32)
    embed = embed_ref[:, at].astype(F32)
    condition = 1.0 + info[3].astype(F32) / TSTEPS * shift_ref[:, at]
    return gain, embed, condition


def own_half_kernel(
    info, x_ref, own_ref, other_ref, mask_ref, gain_ref, embed_ref, shift_ref, wq, wk, wv, w_out,
    q_ref, k_ref, v_ref, rest_q, rest_k, rest_v, w_send, own_q, own_k, own_v, sems,
):
    half = x_ref.shape[1]
    depth = half // 2
    cols = w_send.shape[1]
    first = info[0] * half
    moves = []

    def move(source, target):
        moves.append(pltpu.make_async_copy(source, target, sems.at[len(moves)]))
        moves[-1].start()

    for chunk in range(2):
        there = pl.ds(pl.multiple_of(first + chunk * depth, 128), depth)
        here = pl.ds(chunk * depth, depth)
        for source, target in ((wk, own_k), (wv, own_v), (wq, own_q)):
            move(source.at[there], target.at[here])
    rest = pl.ds(pl.multiple_of(half - first, 128), half)
    for source, target in ((wk, rest_k), (wv, rest_v), (wq, rest_q)):
        move(source.at[rest], target)
    side = pl.ds(pl.multiple_of((1 - info[1]) * cols, 128), cols)
    move(w_out.at[:, side], w_send)

    scales = row_scales(own_ref, other_ref, mask_ref, embed_ref, embed_ref.shape[1])
    at = pl.ds(pl.multiple_of(first, 128), half)
    gain, embed, condition = vectors_at(at, info, gain_ref, embed_ref, shift_ref)
    clean, noisy = both_streams(x_ref[...].astype(F32), scales, gain, embed, condition)
    both = jnp.concatenate([clean, noisy], axis=0)
    for chunk in range(2):
        here = slice(chunk * depth, (chunk + 1) * depth)
        for number, (target, weight) in enumerate(((k_ref, own_k), (v_ref, own_v), (q_ref, own_q))):
            moves[3 * chunk + number].wait()
            product = dot(both[:, here], weight[here])
            target[...] = product if chunk == 0 else target[...] + product
    for copy in moves[6:]:
        copy.wait()


def other_rows(info, near_ref, far_ref):
    near, far = near_ref[...].astype(F32), far_ref[...].astype(F32)
    first = info[1] == 0
    return jnp.concatenate([jnp.where(first, near, far), jnp.where(first, far, near)], axis=0)


def chunk_at(info, chunk, depth, width):
    return pl.ds(pl.multiple_of((1 - info[0]) * (width // 2) + chunk * depth, 128), depth)


def chunk_kernel(
    info, near_ref, far_ref, own_ref, other_ref, mask_ref, gain_ref, embed_ref, shift_ref,
    wq_ref, wk_ref, wv_ref, pq_ref, pk_ref, pv_ref, q_ref, k_ref, v_ref,
):
    width = embed_ref.shape[1]
    scales = row_scales(own_ref, other_ref, mask_ref, embed_ref, width)
    at = chunk_at(info, 0, near_ref.shape[1], width)
    gain, embed, condition = vectors_at(at, info, gain_ref, embed_ref, shift_ref)
    clean, noisy = both_streams(other_rows(info, near_ref, far_ref), scales, gain, embed, condition)
    both = jnp.concatenate([clean, noisy], axis=0)
    here = slice(0, near_ref.shape[1])
    k_ref[...] = pk_ref[...] + dot(both, wk_ref[here])
    v_ref[...] = pv_ref[...] + dot(both, wv_ref[here])
    q_ref[...] = pq_ref[...] + dot(both, wq_ref[here])


def kv_out(ref, k, v, gain):
    for head in range(k.shape[1] // HD):
        cols = slice(head * HD, (head + 1) * HD)
        ref[:, 2 * head * HD : (2 * head + 1) * HD] = head_norm(k[:, cols], gain)
        ref[:, (2 * head + 1) * HD : 2 * (head + 1) * HD] = v[:, cols].astype(BF16)


def clean_kv_kernel(
    info, near_ref, far_ref, own_ref, other_ref, mask_ref, gain_ref, embed_ref,
    wk_ref, wv_ref, pk_ref, pv_ref, kgain_ref, all_ref, one_ref,
):
    rows = all_ref.shape[0]
    width = embed_ref.shape[1]
    clean_scale = row_scales(own_ref, other_ref, mask_ref, embed_ref, width)[0]
    at = chunk_at(info, 1, near_ref.shape[1], width)
    clean = normed_clean(other_rows(info, near_ref, far_ref), clean_scale, gain_ref[:, at].astype(F32))
    here = slice(near_ref.shape[1], 2 * near_ref.shape[1])
    k = pk_ref[:rows] + dot(clean, wk_ref[here])
    v = pv_ref[:rows] + dot(clean, wv_ref[here])
    kv_out(all_ref, k, v, kgain_ref[...])
    cols = one_ref.shape[1]
    one_ref[...] = all_ref[:, pl.ds(pl.multiple_of(info[0] * cols, 128), cols)]


def last_chunk_kernel(
    info, near_ref, far_ref, own_ref, other_ref, mask_ref, gain_ref, embed_ref, shift_ref,
    wq_ref, wk_ref, wv_ref, pq_ref, pk_ref, pv_ref, qgain_ref, kgain_ref, q_ref, self_ref,
):
    rows = self_ref.shape[0]
    width = embed_ref.shape[1]
    scales = row_scales(own_ref, other_ref, mask_ref, embed_ref, width)
    at = chunk_at(info, 1, near_ref.shape[1], width)
    gain, embed, condition = vectors_at(at, info, gain_ref, embed_ref, shift_ref)
    clean, noisy = both_streams(other_rows(info, near_ref, far_ref), scales, gain, embed, condition)
    here = slice(near_ref.shape[1], 2 * near_ref.shape[1])
    k = pk_ref[rows:] + dot(noisy, wk_ref[here])
    v = pv_ref[rows:] + dot(noisy, wv_ref[here])
    kv_out(self_ref, k, v, kgain_ref[...])
    q = pq_ref[...] + dot(jnp.concatenate([clean, noisy], axis=0), wq_ref[here])
    for head in range(q_ref.shape[1] // HD):
        cols = slice(head * HD, (head + 1) * HD)
        q_ref[:, cols] = head_norm(q[:, cols], qgain_ref[...])


def terms(q, k, v, mask):
    scores = lax.dot_general(q, k, (((1,), (1,)), ((), ())), preferred_element_type=F32)
    e = jnp.exp2(scores * SCORE_SCALE)
    if mask is not None:
        e = jnp.where(mask, e, 0.0)
    den = e[:, :HD]
    for start in range(HD, e.shape[1], HD):
        den = den + e[:, start : start + HD]
    return dot(e.astype(BF16), v), den


def add_pieces(q_ref, num_ref, den_ref, base, heads, pieces, rows):
    k = jnp.concatenate([piece[:, :HD] for piece in pieces], axis=0)
    v = jnp.concatenate([piece[:, HD:] for piece in pieces], axis=0)
    for head in range(heads):
        cols = pl.ds(base + head * HD, HD)
        for part in range(2):
            cut = slice(part * rows, (part + 1) * rows)
            num, den = terms(q_ref[cut, cols], k, v, None)
            num_ref[cut, cols] += num
            den_ref[cut, cols] += den


def add_all_heads(q_ref, num_ref, den_ref, piece_refs, rows):
    kv_heads = piece_refs[0].shape[1] // (2 * HD)
    group_cols = q_ref.shape[1] // kv_heads
    for kv_head in range(kv_heads):
        cols = slice(2 * kv_head * HD, 2 * (kv_head + 1) * HD)
        pieces = [ref[:, cols] for ref in piece_refs]
        add_pieces(q_ref, num_ref, den_ref, kv_head * group_cols, group_cols // HD, pieces, rows)


def add_far(info, q_ref, num_ref, den_ref, which, offsets, refs, rows):
    cols = q_ref.shape[1] // 2
    base = pl.multiple_of((info[0] if which == 0 else 1 - info[0]) * cols, 128)
    for bit in sorted({offset.bit_length() for offset in offsets}):
        group = [ref for offset, ref in zip(offsets, refs) if offset.bit_length() == bit]

        @pl.when(jnp.bitwise_and(info[2], 1 << (bit - 1)) != 0)
        def _(group=group):
            add_pieces(q_ref, num_ref, den_ref, base, cols // HD, [ref[...] for ref in group], rows)


def finish(info, num_ref, den_ref, which, out_ref):
    width = out_ref.shape[1]
    base = pl.multiple_of((info[0] if which == 0 else 1 - info[0]) * width, 128)
    for head in range(width // HD):
        cols = pl.ds(base + head * HD, HD)
        total = jnp.sum(den_ref[:, cols], axis=1, keepdims=True)
        out_ref[:, head * HD : (head + 1) * HD] = (num_ref[:, cols] / total).astype(BF16)


def attention_own_kernel(info, q_ref, kv_ref, self_ref, near_ref, num_ref, den_ref):
    rows = kv_ref.shape[0]
    kv_heads = kv_ref.shape[1] // (2 * HD)
    group = q_ref.shape[1] // HD // kv_heads
    row_block = lax.broadcasted_iota(jnp.int32, (rows, rows), 0) // BLK
    key_block = lax.broadcasted_iota(jnp.int32, (rows, rows), 1) // BLK
    both = jnp.concatenate([key_block < row_block, key_block == row_block], axis=1)
    for kv_head in range(kv_heads):
        k_cols = slice(2 * kv_head * HD, (2 * kv_head + 1) * HD)
        v_cols = slice((2 * kv_head + 1) * HD, 2 * (kv_head + 1) * HD)
        k, v = kv_ref[:, k_cols], kv_ref[:, v_cols]
        k_both = jnp.concatenate([k, self_ref[:, k_cols]], axis=0)
        v_both = jnp.concatenate([v, self_ref[:, v_cols]], axis=0)
        for head in range(kv_head * group, (kv_head + 1) * group):
            cols = slice(head * HD, (head + 1) * HD)
            num_ref[:rows, cols], den_ref[:rows, cols] = terms(q_ref[:rows, cols], k, v, key_block <= row_block)
            num_ref[rows:, cols], den_ref[rows:, cols] = terms(q_ref[rows:, cols], k_both, v_both, both)

    @pl.when(jnp.bitwise_and(info[2], 1) != 0)
    def _():
        add_all_heads(q_ref, num_ref, den_ref, [near_ref], rows)


def attention_column_kernel(info, q_ref, num_in, den_in, left_ref, *refs, offsets):
    num_ref, den_ref = refs[-2:]
    rows = left_ref.shape[0]

    @pl.when(jnp.bitwise_and(info[2], 2) != 0)
    def _():
        add_all_heads(q_ref, num_ref, den_ref, [left_ref], rows)

    add_far(info, q_ref, num_ref, den_ref, 0, offsets, refs[: len(offsets)], rows)


def attention_first_head_kernel(info, q_ref, num_in, den_in, right_ref, *refs, offsets):
    num_ref, den_ref, out_ref = refs[-3:]
    rows = right_ref.shape[0]
    count = len(offsets)

    @pl.when(jnp.bitwise_and(info[2], 2) != 0)
    def _():
        add_all_heads(q_ref, num_ref, den_ref, [right_ref], rows)

    add_far(info, q_ref, num_ref, den_ref, 0, offsets, refs[:count], rows)
    finish(info, num_ref, den_ref, 0, out_ref)
    add_far(info, q_ref, num_ref, den_ref, 1, offsets, refs[count : 2 * count], rows)


def attention_second_head_kernel(info, q_ref, num_in, den_in, *refs, offsets):
    num_ref, den_ref, out_ref = refs[-3:]
    rows = out_ref.shape[0] // 2
    add_far(info, q_ref, num_ref, den_ref, 1, offsets, refs[: len(offsets)], rows)
    finish(info, num_ref, den_ref, 1, out_ref)


def out_kernel(info, live, ga, gb, ha, hb, w_mine, w_far, clean_ref, noisy_ref):
    rows, tile = clean_ref.shape
    part = ga.shape[1]
    cols = pl.ds(pl.multiple_of(pl.program_id(0) * tile, 128), tile)
    first = pl.ds(pl.multiple_of(info[0] * part, 128), part)
    second = pl.ds(pl.multiple_of((1 - info[0]) * part, 128), part)
    mixed = dot(ga[...], w_mine[first]) + dot(gb[...], w_mine[second])
    mixed = mixed + dot(ha[...], w_far[first, cols]) + dot(hb[...], w_far[second, cols])
    clean_ref[...] = mixed[:rows].astype(BF16)
    for block in range(rows // BLK):
        part_rows = mixed[rows + block * BLK : rows + (block + 1) * BLK]
        noisy_ref[block * BLK : (block + 1) * BLK] = (part_rows * live[block].astype(F32)).astype(BF16)


WHOLE = pl.BlockSpec(memory_space=pltpu.VMEM)
HBM = pl.BlockSpec(memory_space=pltpu.HBM)
HINT = 1


def call(kernel, scalars, ins, outs, arrays, flops, num_bytes, scratch=(), exps=0, grid=1, aliases=None, limit=20):
    return pl.pallas_call(
        kernel,
        grid_spec=pltpu.PrefetchScalarGridSpec(
            num_scalar_prefetch=len(scalars),
            grid=(grid,),
            in_specs=ins,
            out_specs=[spec for spec, _ in outs],
            scratch_shapes=list(scratch),
        ),
        out_shape=[shape for _, shape in outs],
        compiler_params=pltpu.CompilerParams(vmem_limit_bytes=limit << 20),
        cost_estimate=pl.CostEstimate(
            flops=flops // HINT, bytes_accessed=num_bytes // HINT, transcendentals=exps // HINT
        ),
        input_output_aliases=aliases or {},
    )(*scalars, *arrays)


def after(value, *others):
    return lax.optimization_barrier((value, *others))[0]


def on_device(
    mesh, clean_tokens, norm_gain, mask_embed, time_shift, w_query, w_key, w_value, w_out,
    q_gain, k_gain, masked, block_live, timesteps,
):
    rows, half = clean_tokens.shape
    heads_width = w_query.shape[1]
    kv_width = w_key.shape[1]
    part = heads_width // 2
    ctx = mesh.shape["ctx"]
    c, p, t = lax.axis_index("copy"), lax.axis_index("ctx"), lax.axis_index("tp")
    info = jnp.stack([c, t, p, timesteps[0]]).astype(jnp.int32)
    pair = [(0, 1), (1, 0)]
    cross_x = lambda v: lax.ppermute(v, "copy", pair)
    cross_core = lambda v: lax.ppermute(v, "tp", pair)
    cross_ctx = lambda v, offset: lax.ppermute(v, "ctx", [(i, i ^ offset) for i in range(ctx)])
    shape = jax.ShapeDtypeStruct

    cut, depth = rows // 2, half // 2
    strip = lambda v, chunk: lax.dynamic_slice(v, (t * cut, chunk * depth), (cut, depth))
    near_first = cross_x(strip(clean_tokens, 0))
    wide = clean_tokens.astype(F32)
    squares = jnp.sum(wide * wide, axis=1)
    other_squares = cross_x(squares)
    near_last = cross_x(strip(after(clean_tokens, squares), 1))
    out_cols = w_out.shape[1] // 2
    stats = [squares[None], other_squares[None], masked]
    vectors = [norm_gain[None], mask_embed[None], time_shift[None]]
    qg, kg = q_gain[None], k_gain[None]
    partial = [
        (WHOLE, shape((2 * rows, heads_width), F32)),
        (WHOLE, shape((2 * rows, kv_width), F32)),
        (WHOLE, shape((2 * rows, kv_width), F32)),
    ]
    per_row = heads_width + 2 * kv_width

    bf = lambda *dims: (WHOLE, shape(dims, BF16))
    buffers = [(half, heads_width), (half, kv_width), (half, kv_width)]
    pq, pk, pv, *weights, w_send = call(
        own_half_kernel, [info], [WHOLE] * 7 + [HBM] * 4,
        partial + [bf(*dims) for dims in buffers] + [bf(heads_width, out_cols)],
        [clean_tokens] + stats + vectors + [w_query, w_key, w_value, w_out],
        4 * rows * half * per_row, heads_width * out_cols * 2,
        [pltpu.VMEM(dims, BF16) for dims in buffers] + [pltpu.SemaphoreType.DMA((10,))],
        limit=40,
    )
    far_first = cross_core(near_first)
    pq, pk, pv = call(
        chunk_kernel, [info], [WHOLE] * 14, partial,
        [near_first, far_first] + stats + vectors + weights + [pq, pk, pv],
        4 * rows * depth * per_row, depth * per_row * 2, aliases={12: 0, 13: 1, 14: 2},
    )
    near_last = after(near_last, pk)
    far_last = cross_core(near_last)

    kv, kva = call(
        clean_kv_kernel, [info], [WHOLE] * 12,
        [(WHOLE, shape((rows, 2 * kv_width), BF16)), (WHOLE, shape((rows, kv_width), BF16))],
        [near_last, far_last] + stats + vectors[:2] + weights[1:] + [pk, pv, kg],
        4 * rows * depth * kv_width, depth * 2 * kv_width * 2,
    )

    offsets = list(range(4, ctx, 2))
    beside = cross_ctx(kv, 1)
    left = cross_ctx(kv, 2)
    column = [cross_ctx(kva, offset) for offset in offsets]

    near_last = after(near_last, kv)
    q, own = call(
        last_chunk_kernel, [info], [WHOLE] * 16,
        [(WHOLE, shape((2 * rows, heads_width), BF16)), (WHOLE, shape((rows, 2 * kv_width), BF16))],
        [near_last, far_last] + stats + vectors + weights + [pq, pk, pv, qg, kg],
        4 * rows * depth * per_row, depth * per_row * 2,
    )
    w_far = cross_core(after(w_send, kv))

    acc_shape = shape((2 * rows, heads_width), F32)
    acc = [(WHOLE, acc_shape), (WHOLE, acc_shape)]
    attended = (WHOLE, shape((2 * rows, part), BF16))
    unit = rows * rows * heads_width // HD
    cost = lambda units: (4 * HD * unit * units, 8 * unit, (), unit * units)
    in_place = {2: 0, 3: 1}
    num, den = call(attention_own_kernel, [info], [WHOLE] * 4, acc, [q, kv, own, beside], *cost(5))
    column = [after(piece, num) for piece in column]
    left = after(left, num)
    column_right = [cross_ctx(piece, 1) for piece in column]
    other = [cross_x(piece) for piece in column]
    right = cross_ctx(left, 1)
    num, den = call(
        functools.partial(attention_column_kernel, offsets=offsets), [info], [WHOLE] * (4 + len(column)), acc,
        [q, num, den, left] + column, *cost(4), aliases=in_place,
    )
    column_right = [after(piece, num) for piece in column_right]
    other_right = [cross_x(piece) for piece in column_right]
    num, den, ga = call(
        functools.partial(attention_first_head_kernel, offsets=offsets), [info],
        [WHOLE] * (4 + 2 * len(column)), acc + [attended],
        [q, num, den, right] + column_right + other, *cost(6), aliases=in_place,
    )
    ha = cross_core(ga)
    num, den, gb = call(
        functools.partial(attention_second_head_kernel, offsets=offsets), [info],
        [WHOLE] * (3 + len(column)), acc + [attended], [q, num, den] + other_right, *cost(2), aliases=in_place,
    )
    hb = cross_core(gb)

    tile = 512
    tiles = out_cols // tile
    mine = pl.BlockSpec((heads_width, tile), lambda n, s, l: (0, s[1] * tiles + n))
    out = pl.BlockSpec((rows, tile), lambda n, s, l: (0, n))
    out_shape = shape((rows, out_cols), BF16)
    clean_out, noised_out = call(
        out_kernel, [info, block_live[0]], [WHOLE] * 4 + [mine, WHOLE], [(out, out_shape), (out, out_shape)],
        [ga, gb, ha, hb, w_out, w_far],
        8 * rows * heads_width * out_cols, 2 * heads_width * out_cols * 2, grid=tiles,
    )
    return (clean_out, noised_out[None])


def solution(mesh):
    in_specs = (
        P("ctx", "copy"),
        P(),
        P(),
        P(),
        P(None, "tp"),
        P(None, "tp"),
        P(None, "tp"),
        P("tp", None),
        P(),
        P(),
        P("copy", "ctx"),
        P("copy", "ctx"),
        P("copy"),
    )
    out_specs = (P("ctx", "tp"), P("copy", "ctx", "tp"))
    return jax.shard_map(
        functools.partial(on_device, mesh), mesh=mesh, in_specs=in_specs, out_specs=out_specs, check_vma=False
    )
```

```python
import functools
import math

import jax
import jax.numpy as jnp
from jax import lax
from jax.experimental import pallas as pl
from jax.experimental.pallas import tpu as pltpu
from jax.sharding import PartitionSpec as P

HD = 128
BLK = 64
TSTEPS = 1000
EPS = 1e-06
F32 = jnp.float32
BF16 = jnp.bfloat16
SCORE_SCALE = math.log2(math.e) / math.sqrt(HD)


def to_column(row, n):
    eye = lax.broadcasted_iota(jnp.int32, (n, n), 0) == lax.broadcasted_iota(jnp.int32, (n, n), 1)
    return jnp.sum(jnp.where(eye, jnp.broadcast_to(row, (n, n)), 0.0), axis=1, keepdims=True)


def row_scales(own_ref, other_ref, mask_ref, embed_ref, width):
    n = own_ref.shape[1]
    clean = lax.rsqrt(to_column(own_ref[...] + other_ref[...], n) * (1.0 / width) + EPS)
    embed = embed_ref[...].astype(F32)
    embed_scale = lax.rsqrt(jnp.sum(embed * embed, axis=1, keepdims=True) * (1.0 / width) + EPS)
    masked = to_column(mask_ref[...].astype(F32), n)
    return clean, embed_scale, masked


def normed_clean(x, clean_scale, gain):
    return (x * clean_scale * gain).astype(BF16)


def normed_noisy(x, clean_scale, embed_scale, masked, gain, embed, condition):
    is_masked = masked == 1.0
    noisy = jnp.where(is_masked, embed, x)
    scale = jnp.where(is_masked, embed_scale, clean_scale)
    return (noisy * scale * gain * condition).astype(BF16)


def dot(a, b):
    return jnp.dot(a, b, preferred_element_type=F32)


def head_norm(wide, gain):
    scale = lax.rsqrt(jnp.mean(wide * wide, axis=1, keepdims=True) + EPS)
    return (wide * scale * gain).astype(BF16)


def both_streams(x, scales, gain, embed, condition):
    clean = normed_clean(x, scales[0], gain)
    noisy = normed_noisy(x, scales[0], scales[1], scales[2], gain, embed, condition)
    return clean, noisy


def half_vectors(at, info, gain_ref, embed_ref, shift_ref):
    gain = gain_ref[:, at].astype(F32)
    embed = embed_ref[:, at].astype(F32)
    condition = 1.0 + info[3].astype(F32) / TSTEPS * shift_ref[:, at]
    return gain, embed, condition


def both_streams(x, scales, gain, embed, condition):
    clean = normed_clean(x, scales[0], gain)
    noisy = normed_noisy(x, scales[0], scales[1], scales[2], gain, embed, condition)
    return clean, noisy


def vectors_at(at, info, gain_ref, embed_ref, shift_ref):
    gain = gain_ref[:, at].astype(F32)
    embed = embed_ref[:, at].astype(F32)
    condition = 1.0 + info[3].astype(F32) / TSTEPS * shift_ref[:, at]
    return gain, embed, condition


def squares_kernel(info, x_ref, squares_ref, first_ref, last_ref):
    rows = x_ref.shape[0]
    cut, depth = first_ref.shape
    x = x_ref[...].astype(F32)
    sums = jnp.sum(x * x, axis=1, keepdims=True)
    eye = lax.broadcasted_iota(jnp.int32, (rows, rows), 0) == lax.broadcasted_iota(jnp.int32, (rows, rows), 1)
    squares_ref[...] = jnp.sum(jnp.where(eye, jnp.broadcast_to(sums, (rows, rows)), 0.0), axis=0, keepdims=True)
    strip = pl.ds(pl.multiple_of(info[1] * cut, 128), cut)
    first_ref[...] = x_ref[strip, :depth]
    last_ref[...] = x_ref[strip, depth:]


def own_half_kernel(
    info, x_ref, own_ref, other_ref, mask_ref, gain_ref, embed_ref, shift_ref, wq, wk, wv,
    q_ref, k_ref, v_ref, rest_q, rest_k, rest_v, own_q, own_k, own_v, sems,
):
    half = x_ref.shape[1]
    depth = half // 2
    first = info[0] * half
    moves = []

    def move(source, target):
        moves.append(pltpu.make_async_copy(source, target, sems.at[len(moves)]))
        moves[-1].start()

    for chunk in range(2):
        there = pl.ds(pl.multiple_of(first + chunk * depth, 128), depth)
        here = pl.ds(chunk * depth, depth)
        for source, target in ((wk, own_k), (wv, own_v), (wq, own_q)):
            move(source.at[there], target.at[here])
    rest = pl.ds(pl.multiple_of(half - first, 128), half)
    for source, target in ((wk, rest_k), (wv, rest_v), (wq, rest_q)):
        move(source.at[rest], target)

    scales = row_scales(own_ref, other_ref, mask_ref, embed_ref, embed_ref.shape[1])
    at = pl.ds(pl.multiple_of(first, 128), half)
    gain, embed, condition = vectors_at(at, info, gain_ref, embed_ref, shift_ref)
    clean, noisy = both_streams(x_ref[...].astype(F32), scales, gain, embed, condition)
    both = jnp.concatenate([clean, noisy], axis=0)
    for chunk in range(2):
        here = slice(chunk * depth, (chunk + 1) * depth)
        for number, (target, weight) in enumerate(((k_ref, own_k), (v_ref, own_v), (q_ref, own_q))):
            moves[3 * chunk + number].wait()
            product = dot(both[:, here], weight[here])
            target[...] = product if chunk == 0 else target[...] + product
    for copy in moves[6:]:
        copy.wait()


def other_rows(info, near_ref, far_ref):
    near, far = near_ref[...].astype(F32), far_ref[...].astype(F32)
    first = info[1] == 0
    return jnp.concatenate([jnp.where(first, near, far), jnp.where(first, far, near)], axis=0)


def chunk_at(info, chunk, depth, width):
    return pl.ds(pl.multiple_of((1 - info[0]) * (width // 2) + chunk * depth, 128), depth)


def chunk_kernel(
    info, near_ref, far_ref, own_ref, other_ref, mask_ref, gain_ref, embed_ref, shift_ref,
    wq_ref, wk_ref, wv_ref, pq_ref, pk_ref, pv_ref, w_out, q_ref, k_ref, v_ref, w_send, sem,
):
    width = embed_ref.shape[1]
    cols = w_send.shape[1]
    side = pl.ds(pl.multiple_of((1 - info[1]) * cols, 128), cols)
    move = pltpu.make_async_copy(w_out.at[:, side], w_send, sem)
    move.start()
    scales = row_scales(own_ref, other_ref, mask_ref, embed_ref, width)
    at = chunk_at(info, 0, near_ref.shape[1], width)
    gain, embed, condition = vectors_at(at, info, gain_ref, embed_ref, shift_ref)
    clean, noisy = both_streams(other_rows(info, near_ref, far_ref), scales, gain, embed, condition)
    both = jnp.concatenate([clean, noisy], axis=0)
    here = slice(0, near_ref.shape[1])
    k_ref[...] = pk_ref[...] + dot(both, wk_ref[here])
    v_ref[...] = pv_ref[...] + dot(both, wv_ref[here])
    q_ref[...] = pq_ref[...] + dot(both, wq_ref[here])
    move.wait()


def kv_out(ref, k, v, gain):
    for head in range(k.shape[1] // HD):
        cols = slice(head * HD, (head + 1) * HD)
        ref[:, 2 * head * HD : (2 * head + 1) * HD] = head_norm(k[:, cols], gain)
        ref[:, (2 * head + 1) * HD : 2 * (head + 1) * HD] = v[:, cols].astype(BF16)


def clean_kv_kernel(
    info, near_ref, far_ref, own_ref, other_ref, mask_ref, gain_ref, embed_ref,
    wk_ref, wv_ref, pk_ref, pv_ref, kgain_ref, all_ref,
):
    rows = all_ref.shape[0]
    width = embed_ref.shape[1]
    clean_scale = row_scales(own_ref, other_ref, mask_ref, embed_ref, width)[0]
    at = chunk_at(info, 1, near_ref.shape[1], width)
    clean = normed_clean(other_rows(info, near_ref, far_ref), clean_scale, gain_ref[:, at].astype(F32))
    here = slice(near_ref.shape[1], 2 * near_ref.shape[1])
    k = pk_ref[:rows] + dot(clean, wk_ref[here])
    v = pv_ref[:rows] + dot(clean, wv_ref[here])
    kv_out(all_ref, k, v, kgain_ref[...])


def last_chunk_kernel(
    info, near_ref, far_ref, own_ref, other_ref, mask_ref, gain_ref, embed_ref, shift_ref,
    wq_ref, wk_ref, wv_ref, pq_ref, pk_ref, pv_ref, qgain_ref, kgain_ref, q_ref, self_ref,
):
    rows = self_ref.shape[0]
    width = embed_ref.shape[1]
    scales = row_scales(own_ref, other_ref, mask_ref, embed_ref, width)
    at = chunk_at(info, 1, near_ref.shape[1], width)
    gain, embed, condition = vectors_at(at, info, gain_ref, embed_ref, shift_ref)
    clean, noisy = both_streams(other_rows(info, near_ref, far_ref), scales, gain, embed, condition)
    here = slice(near_ref.shape[1], 2 * near_ref.shape[1])
    k = pk_ref[rows:] + dot(noisy, wk_ref[here])
    v = pv_ref[rows:] + dot(noisy, wv_ref[here])
    kv_out(self_ref, k, v, kgain_ref[...])
    q = pq_ref[...] + dot(jnp.concatenate([clean, noisy], axis=0), wq_ref[here])
    for head in range(q_ref.shape[1] // HD):
        cols = slice(head * HD, (head + 1) * HD)
        q_ref[:, cols] = head_norm(q[:, cols], qgain_ref[...])


def terms(q, k, v, mask):
    scores = lax.dot_general(q, k, (((1,), (1,)), ((), ())), preferred_element_type=F32)
    e = jnp.exp2(scores * SCORE_SCALE)
    if mask is not None:
        e = jnp.where(mask, e, 0.0)
    den = e[:, :HD]
    for start in range(HD, e.shape[1], HD):
        den = den + e[:, start : start + HD]
    return dot(e.astype(BF16), v), den


def add_pieces(q_ref, num_ref, den_ref, kv_head, piece_refs):
    rows, width = piece_refs[0].shape
    group = q_ref.shape[1] // HD // (width // (2 * HD))
    base = 2 * kv_head * HD
    k = jnp.concatenate([ref[:, base : base + HD] for ref in piece_refs], axis=0)
    v = jnp.concatenate([ref[:, base + HD : base + 2 * HD] for ref in piece_refs], axis=0)
    for head in range(kv_head * group, (kv_head + 1) * group):
        cols = slice(head * HD, (head + 1) * HD)
        for part in range(2):
            cut = slice(part * rows, (part + 1) * rows)
            num, den = terms(q_ref[cut, cols], k, v, None)
            num_ref[cut, cols] += num
            den_ref[cut, cols] += den


def attention_own_kernel(info, q_ref, kv_ref, self_ref, num_ref, den_ref):
    rows = kv_ref.shape[0]
    kv_heads = kv_ref.shape[1] // (2 * HD)
    group = q_ref.shape[1] // HD // kv_heads
    row_block = lax.broadcasted_iota(jnp.int32, (rows, rows), 0) // BLK
    key_block = lax.broadcasted_iota(jnp.int32, (rows, rows), 1) // BLK
    both = jnp.concatenate([key_block < row_block, key_block == row_block], axis=1)
    for kv_head in range(kv_heads):
        k_cols = slice(2 * kv_head * HD, (2 * kv_head + 1) * HD)
        v_cols = slice((2 * kv_head + 1) * HD, 2 * (kv_head + 1) * HD)
        k, v = kv_ref[:, k_cols], kv_ref[:, v_cols]
        k_both = jnp.concatenate([k, self_ref[:, k_cols]], axis=0)
        v_both = jnp.concatenate([v, self_ref[:, v_cols]], axis=0)
        for head in range(kv_head * group, (kv_head + 1) * group):
            cols = slice(head * HD, (head + 1) * HD)
            num_ref[:rows, cols], den_ref[:rows, cols] = terms(q_ref[:rows, cols], k, v, key_block <= row_block)
            num_ref[rows:, cols], den_ref[rows:, cols] = terms(q_ref[rows:, cols], k_both, v_both, both)


def attention_pair_kernel(info, q_ref, num_in, den_in, first_ref, second_ref, num_ref, den_ref, *, step):
    first_valid = jnp.bitwise_and(info[2], 1) == 1 if step == 1 else info[2] >= 2 * (step - 1)
    second_valid = info[2] >= 2 * step
    cases = (
        (jnp.logical_and(first_valid, second_valid), [first_ref, second_ref]),
        (jnp.logical_and(first_valid, jnp.logical_not(second_valid)), [first_ref]),
        (jnp.logical_and(jnp.logical_not(first_valid), second_valid), [second_ref]),
    )
    for valid, refs in cases:
        @pl.when(valid)
        def _(refs=refs):
            for kv_head in range(refs[0].shape[1] // (2 * HD)):
                add_pieces(q_ref, num_ref, den_ref, kv_head, refs)


def attention_last_kernel(info, q_ref, num_in, den_in, piece_ref, num_ref, den_ref, out_ref, *, step, kv_head):
    valid = jnp.bitwise_and(info[2], 1) == 1 if step == 0 else info[2] >= 2 * step

    @pl.when(valid)
    def _():
        add_pieces(q_ref, num_ref, den_ref, kv_head, [piece_ref])

    width = out_ref.shape[1]
    for head in range(width // HD):
        cols = slice(kv_head * width + head * HD, kv_head * width + (head + 1) * HD)
        total = jnp.sum(den_ref[:, cols], axis=1, keepdims=True)
        out_ref[:, head * HD : (head + 1) * HD] = (num_ref[:, cols] / total).astype(BF16)


def out_first_kernel(info, ga, gb, ha, w_out, w_far, mixed_ref, *, tile):
    part = ga.shape[1]
    total = mixed_ref.shape[1]
    for start in range(0, total, tile):
        mine = pl.ds(pl.multiple_of(info[1] * total + start, 128), tile)
        cols = slice(start, start + tile)
        mixed = dot(ga[...], w_out[:part, mine]) + dot(gb[...], w_out[part:, mine])
        mixed_ref[:, cols] = mixed + dot(ha[...], w_far[:part, cols])


def out_last_kernel(info, live, hb, mixed_ref, w_far, clean_ref, noisy_ref):
    rows, tile = clean_ref.shape
    part = hb.shape[1]
    cols = pl.ds(pl.multiple_of(pl.program_id(0) * tile, 128), tile)
    mixed = mixed_ref[:, cols] + dot(hb[...], w_far[part:, cols])
    clean_ref[...] = mixed[:rows].astype(BF16)
    for block in range(rows // BLK):
        part_rows = mixed[rows + block * BLK : rows + (block + 1) * BLK]
        noisy_ref[block * BLK : (block + 1) * BLK] = (part_rows * live[block].astype(F32)).astype(BF16)


WHOLE = pl.BlockSpec(memory_space=pltpu.VMEM)
HBM = pl.BlockSpec(memory_space=pltpu.HBM)
HINT = 1


def call(kernel, scalars, ins, outs, arrays, flops, num_bytes, scratch=(), exps=0, grid=1, aliases=None, limit=20):
    return pl.pallas_call(
        kernel,
        grid_spec=pltpu.PrefetchScalarGridSpec(
            num_scalar_prefetch=len(scalars),
            grid=(grid,),
            in_specs=ins,
            out_specs=[spec for spec, _ in outs],
            scratch_shapes=list(scratch),
        ),
        out_shape=[shape for _, shape in outs],
        compiler_params=pltpu.CompilerParams(vmem_limit_bytes=limit << 20),
        cost_estimate=pl.CostEstimate(
            flops=flops // HINT, bytes_accessed=num_bytes // HINT, transcendentals=exps // HINT
        ),
        input_output_aliases=aliases or {},
    )(*scalars, *arrays)


def after(value, *others):
    return lax.optimization_barrier((value, *others))[0]


def on_device(
    mesh, clean_tokens, norm_gain, mask_embed, time_shift, w_query, w_key, w_value, w_out,
    q_gain, k_gain, masked, block_live, timesteps,
):
    rows, half = clean_tokens.shape
    heads_width = w_query.shape[1]
    kv_width = w_key.shape[1]
    part = heads_width // 2
    ctx = mesh.shape["ctx"]
    c, p, t = lax.axis_index("copy"), lax.axis_index("ctx"), lax.axis_index("tp")
    info = jnp.stack([c, t, p, timesteps[0]]).astype(jnp.int32)
    pair = [(0, 1), (1, 0)]
    cross_x = lambda v: lax.ppermute(v, "copy", pair)
    cross_core = lambda v: lax.ppermute(v, "tp", pair)
    shape = jax.ShapeDtypeStruct

    cut, depth = rows // 2, half // 2
    out_cols = w_out.shape[1] // 2
    qg, kg = q_gain[None], k_gain[None]
    vmem = lambda dims, kind: (WHOLE, pltpu.VMEM(dims, kind))
    in_hbm = lambda v: pltpu.with_memory_space_constraint(v, pltpu.HBM)

    squares, strip_first, strip_last = call(
        squares_kernel, [info], [WHOLE], [vmem((1, rows), F32)] + [vmem((cut, depth), BF16)] * 2, [clean_tokens],
        2 * rows * half, rows * half * 2,
    )
    other_squares = cross_x(squares)
    near_first = cross_x(strip_first)
    near_last = cross_x(strip_last)
    stats = [squares, other_squares, masked]
    vectors = [norm_gain[None], mask_embed[None], time_shift[None]]
    partial = [vmem((2 * rows, width), F32) for width in (heads_width, kv_width, kv_width)]
    buffers = [(half, heads_width), (half, kv_width), (half, kv_width)]
    per_row = heads_width + 2 * kv_width

    pq, pk, pv, *weights = call(
        own_half_kernel, [info], [WHOLE] * 7 + [HBM] * 3, partial + [vmem(dims, BF16) for dims in buffers],
        [clean_tokens] + stats + vectors + [in_hbm(w_query), in_hbm(w_key), in_hbm(w_value)],
        4 * rows * half * per_row, 2 * half * per_row * 2,
        [pltpu.VMEM(dims, BF16) for dims in buffers] + [pltpu.SemaphoreType.DMA((9,))], limit=32,
    )
    far_first = cross_core(near_first)
    pq, pk, pv, w_send = call(
        chunk_kernel, [info], [WHOLE] * 14 + [HBM], partial + [vmem((heads_width, out_cols), BF16)],
        [near_first, far_first] + stats + vectors + weights + [pq, pk, pv, in_hbm(w_out)],
        4 * rows * depth * per_row, depth * per_row * 2, [pltpu.SemaphoreType.DMA(())],
        aliases={12: 0, 13: 1, 14: 2},
    )
    near_last = after(near_last, pk)
    far_last = cross_core(near_last)

    kv, = call(
        clean_kv_kernel, [info], [WHOLE] * 12, [vmem((rows, 2 * kv_width), BF16)],
        [near_last, far_last] + stats + vectors[:2] + weights[1:] + [pk, pv, kg],
        4 * rows * depth * kv_width, depth * 2 * kv_width * 2,
    )

    steps = ctx // 2
    along = lambda v: lax.ppermute(v, "ctx", [(i, (i + 2) % ctx) for i in range(ctx)])
    across = lambda v: lax.ppermute(v, "ctx", [(i, i ^ 1) for i in range(ctx)])
    crossed = across(kv)
    column = along(kv)
    w_far = cross_core(after(w_send, kv))
    near_last = after(near_last, kv)
    q, own = call(
        last_chunk_kernel, [info], [WHOLE] * 16,
        [vmem((2 * rows, heads_width), BF16), vmem((rows, 2 * kv_width), BF16)],
        [near_last, far_last] + stats + vectors + weights + [pq, pk, pv, qg, kg],
        4 * rows * depth * per_row, depth * per_row * 2,
    )

    acc = [vmem((2 * rows, heads_width), F32)] * 2
    unit = rows * rows * heads_width // HD
    cost = lambda units: (4 * HD * unit * units, 8 * unit, (), unit * units)
    in_place = {2: 0, 3: 1}
    num, den = call(attention_own_kernel, [info], [WHOLE] * 3, acc, [q, kv, own], *cost(3))
    w_far = after(w_far, num)
    for step in range(1, steps):
        column = after(column, num)
        before, crossed = crossed, across(column)
        here, column = column, along(column) if step < steps - 1 else None
        num, den = call(
            functools.partial(attention_pair_kernel, step=step), [info], [WHOLE] * 5, acc,
            [q, num, den, before, here], *cost(4), aliases=in_place,
        )
    attended = []
    for kv_head in range(2):
        num, den, result = call(
            functools.partial(attention_last_kernel, step=steps - 1, kv_head=kv_head), [info], [WHOLE] * 4,
            acc + [vmem((2 * rows, part), BF16)], [q, num, den, crossed], *cost(1), aliases=in_place,
        )
        attended.append((result, cross_core(result)))

    (ga, ha), (gb, hb) = attended
    tile = 512
    mixed, = call(
        functools.partial(out_first_kernel, tile=tile), [info], [WHOLE] * 5, [vmem((2 * rows, out_cols), F32)],
        [ga, gb, ha, w_out, w_far], 6 * rows * heads_width * out_cols, 2 * heads_width * out_cols * 2,
    )
    out = pl.BlockSpec((rows, tile), lambda n, s, l: (0, n))
    out_shape = shape((rows, out_cols), BF16)
    clean_out, noised_out = call(
        out_last_kernel, [info, block_live[0]], [WHOLE] * 3, [(out, out_shape), (out, out_shape)],
        [hb, mixed, w_far], 2 * rows * heads_width * out_cols, heads_width * out_cols * 2, grid=out_cols // tile,
    )
    return (clean_out, noised_out[None])


def solution(mesh):
    in_specs = (
        P("ctx", "copy"),
        P(),
        P(),
        P(),
        P(None, "tp"),
        P(None, "tp"),
        P(None, "tp"),
        P("tp", None),
        P(),
        P(),
        P("copy", "ctx"),
        P("copy", "ctx"),
        P("copy"),
    )
    out_specs = (P("ctx", "tp"), P("copy", "ctx", "tp"))
    return jax.shard_map(
        functools.partial(on_device, mesh), mesh=mesh, in_specs=in_specs, out_specs=out_specs, check_vma=False
    )
```

```python
import functools
import math

import jax
import jax.numpy as jnp
from jax import lax
from jax.experimental import pallas as pl
from jax.experimental.pallas import tpu as pltpu
from jax.sharding import PartitionSpec as P

HD = 128
BLK = 64
TSTEPS = 1000
EPS = 1e-06
F32 = jnp.float32
BF16 = jnp.bfloat16
SCORE_SCALE = math.log2(math.e) / math.sqrt(HD)


def to_column(row, n):
    eye = lax.broadcasted_iota(jnp.int32, (n, n), 0) == lax.broadcasted_iota(jnp.int32, (n, n), 1)
    return jnp.sum(jnp.where(eye, jnp.broadcast_to(row, (n, n)), 0.0), axis=1, keepdims=True)


def row_scales(own_ref, other_ref, mask_ref, embed_ref, width):
    n = own_ref.shape[1]
    clean = lax.rsqrt(to_column(own_ref[...] + other_ref[...], n) * (1.0 / width) + EPS)
    embed = embed_ref[...].astype(F32)
    embed_scale = lax.rsqrt(jnp.sum(embed * embed, axis=1, keepdims=True) * (1.0 / width) + EPS)
    masked = to_column(mask_ref[...].astype(F32), n)
    return clean, embed_scale, masked


def normed_clean(x, clean_scale, gain):
    return (x * clean_scale * gain).astype(BF16)


def normed_noisy(x, clean_scale, embed_scale, masked, gain, embed, condition):
    is_masked = masked == 1.0
    noisy = jnp.where(is_masked, embed, x)
    scale = jnp.where(is_masked, embed_scale, clean_scale)
    return (noisy * scale * gain * condition).astype(BF16)


def dot(a, b):
    return jnp.dot(a, b, preferred_element_type=F32)


def head_norm(wide, gain):
    scale = lax.rsqrt(jnp.mean(wide * wide, axis=1, keepdims=True) + EPS)
    return (wide * scale * gain).astype(BF16)


def both_streams(x, scales, gain, embed, condition):
    clean = normed_clean(x, scales[0], gain)
    noisy = normed_noisy(x, scales[0], scales[1], scales[2], gain, embed, condition)
    return clean, noisy


def half_vectors(at, info, gain_ref, embed_ref, shift_ref):
    gain = gain_ref[:, at].astype(F32)
    embed = embed_ref[:, at].astype(F32)
    condition = 1.0 + info[3].astype(F32) / TSTEPS * shift_ref[:, at]
    return gain, embed, condition


def both_streams(x, scales, gain, embed, condition):
    clean = normed_clean(x, scales[0], gain)
    noisy = normed_noisy(x, scales[0], scales[1], scales[2], gain, embed, condition)
    return clean, noisy


def vectors_at(at, info, gain_ref, embed_ref, shift_ref):
    gain = gain_ref[:, at].astype(F32)
    embed = embed_ref[:, at].astype(F32)
    condition = 1.0 + info[3].astype(F32) / TSTEPS * shift_ref[:, at]
    return gain, embed, condition


def squares_kernel(x_hbm, mask_hbm, shift_hbm, x_ref, mask_ref, shift_ref, squares_ref, sems):
    moves = [
        pltpu.make_async_copy(source, target, sems.at[number])
        for number, (source, target) in enumerate(((x_hbm, x_ref), (mask_hbm, mask_ref), (shift_hbm, shift_ref)))
    ]
    for move in moves:
        move.start()
    for move in moves:
        move.wait()
    rows = x_ref.shape[0]
    x = x_ref[...].astype(F32)
    sums = jnp.sum(x * x, axis=1, keepdims=True)
    eye = lax.broadcasted_iota(jnp.int32, (rows, rows), 0) == lax.broadcasted_iota(jnp.int32, (rows, rows), 1)
    squares_ref[...] = jnp.sum(jnp.where(eye, jnp.broadcast_to(sums, (rows, rows)), 0.0), axis=0, keepdims=True)


def strip_kernel(info, x_ref, strip_ref):
    rows = strip_ref.shape[0]
    strip_ref[...] = x_ref[pl.ds(pl.multiple_of(info[1] * rows, 128), rows)]


def own_half_kernel(
    info, x_ref, own_ref, other_ref, mask_ref, gain_ref, embed_ref, shift_ref, wq, wk, wv, w_out,
    q_ref, k_ref, v_ref, rest_q, rest_k, rest_v, w_send, own_q, own_k, own_v, sems,
):
    half = x_ref.shape[1]
    depth = half // 2
    first = info[0] * half
    moves = []

    def move(source, target):
        moves.append(pltpu.make_async_copy(source, target, sems.at[len(moves)]))
        moves[-1].start()

    for chunk in range(2):
        there = pl.ds(pl.multiple_of(first + chunk * depth, 128), depth)
        here = pl.ds(chunk * depth, depth)
        for source, target in ((wk, own_k), (wv, own_v), (wq, own_q)):
            move(source.at[there], target.at[here])
    rest = pl.ds(pl.multiple_of(half - first, 128), half)
    for source, target in ((wk, rest_k), (wv, rest_v), (wq, rest_q)):
        move(source.at[rest], target)
    cols = w_send.shape[1]
    move(w_out.at[:, pl.ds(pl.multiple_of((1 - info[1]) * cols, 128), cols)], w_send)

    scales = row_scales(own_ref, other_ref, mask_ref, embed_ref, embed_ref.shape[1])
    at = pl.ds(pl.multiple_of(first, 128), half)
    gain, embed, condition = vectors_at(at, info, gain_ref, embed_ref, shift_ref)
    clean, noisy = both_streams(x_ref[...].astype(F32), scales, gain, embed, condition)
    both = jnp.concatenate([clean, noisy], axis=0)
    for chunk in range(2):
        here = slice(chunk * depth, (chunk + 1) * depth)
        for number, (target, weight) in enumerate(((k_ref, own_k), (v_ref, own_v), (q_ref, own_q))):
            moves[3 * chunk + number].wait()
            product = dot(both[:, here], weight[here])
            target[...] = product if chunk == 0 else target[...] + product
    for copy in moves[6:]:
        copy.wait()


def other_rows(info, near_ref, far_ref):
    near, far = near_ref[...].astype(F32), far_ref[...].astype(F32)
    first = info[1] == 0
    return jnp.concatenate([jnp.where(first, near, far), jnp.where(first, far, near)], axis=0)


def other_half(info, half):
    return pl.ds(pl.multiple_of((1 - info[0]) * half, 128), half)


def kv_out(ref, k, v, gain):
    for head in range(k.shape[1] // HD):
        cols = slice(head * HD, (head + 1) * HD)
        ref[:, 2 * head * HD : (2 * head + 1) * HD] = head_norm(k[:, cols], gain)
        ref[:, (2 * head + 1) * HD : 2 * (head + 1) * HD] = v[:, cols].astype(BF16)


def clean_kv_kernel(
    info, near_ref, far_ref, own_ref, other_ref, mask_ref, gain_ref, embed_ref,
    wk_ref, wv_ref, pk_ref, pv_ref, kgain_ref, all_ref,
):
    rows = all_ref.shape[0]
    width = embed_ref.shape[1]
    clean_scale = row_scales(own_ref, other_ref, mask_ref, embed_ref, width)[0]
    at = other_half(info, near_ref.shape[1])
    clean = normed_clean(other_rows(info, near_ref, far_ref), clean_scale, gain_ref[:, at].astype(F32))
    k = pk_ref[:rows] + dot(clean, wk_ref[...])
    v = pv_ref[:rows] + dot(clean, wv_ref[...])
    kv_out(all_ref, k, v, kgain_ref[...])


def other_half_kernel(
    info, near_ref, far_ref, own_ref, other_ref, mask_ref, gain_ref, embed_ref, shift_ref,
    wq_ref, wk_ref, wv_ref, pq_ref, pk_ref, pv_ref, qgain_ref, kgain_ref, q_ref, self_ref,
):
    rows = self_ref.shape[0]
    width = embed_ref.shape[1]
    scales = row_scales(own_ref, other_ref, mask_ref, embed_ref, width)
    at = other_half(info, near_ref.shape[1])
    gain, embed, condition = vectors_at(at, info, gain_ref, embed_ref, shift_ref)
    clean, noisy = both_streams(other_rows(info, near_ref, far_ref), scales, gain, embed, condition)
    k = pk_ref[rows:] + dot(noisy, wk_ref[...])
    v = pv_ref[rows:] + dot(noisy, wv_ref[...])
    kv_out(self_ref, k, v, kgain_ref[...])
    q = pq_ref[...] + dot(jnp.concatenate([clean, noisy], axis=0), wq_ref[...])
    for head in range(q_ref.shape[1] // HD):
        cols = slice(head * HD, (head + 1) * HD)
        q_ref[:, cols] = head_norm(q[:, cols], qgain_ref[...])


def terms(q, k, v, mask):
    scores = lax.dot_general(q, k, (((1,), (1,)), ((), ())), preferred_element_type=F32)
    e = jnp.exp2(scores * SCORE_SCALE)
    if mask is not None:
        e = jnp.where(mask, e, 0.0)
    den = e[:, :HD]
    for start in range(HD, e.shape[1], HD):
        den = den + e[:, start : start + HD]
    return dot(e.astype(BF16), v), den


def add_pieces(q_ref, num_ref, den_ref, kv_head, piece_refs):
    rows, width = piece_refs[0].shape
    group = q_ref.shape[1] // HD // (width // (2 * HD))
    base = 2 * kv_head * HD
    k = jnp.concatenate([ref[:, base : base + HD] for ref in piece_refs], axis=0)
    v = jnp.concatenate([ref[:, base + HD : base + 2 * HD] for ref in piece_refs], axis=0)
    for head in range(kv_head * group, (kv_head + 1) * group):
        cols = slice(head * HD, (head + 1) * HD)
        for part in range(2):
            cut = slice(part * rows, (part + 1) * rows)
            num, den = terms(q_ref[cut, cols], k, v, None)
            num_ref[cut, cols] += num
            den_ref[cut, cols] += den


def attention_own_kernel(info, q_ref, kv_ref, self_ref, num_ref, den_ref):
    rows = kv_ref.shape[0]
    kv_heads = kv_ref.shape[1] // (2 * HD)
    group = q_ref.shape[1] // HD // kv_heads
    row_block = lax.broadcasted_iota(jnp.int32, (rows, rows), 0) // BLK
    key_block = lax.broadcasted_iota(jnp.int32, (rows, rows), 1) // BLK
    both = jnp.concatenate([key_block < row_block, key_block == row_block], axis=1)
    for kv_head in range(kv_heads):
        k_cols = slice(2 * kv_head * HD, (2 * kv_head + 1) * HD)
        v_cols = slice((2 * kv_head + 1) * HD, 2 * (kv_head + 1) * HD)
        k, v = kv_ref[:, k_cols], kv_ref[:, v_cols]
        k_both = jnp.concatenate([k, self_ref[:, k_cols]], axis=0)
        v_both = jnp.concatenate([v, self_ref[:, v_cols]], axis=0)
        for head in range(kv_head * group, (kv_head + 1) * group):
            cols = slice(head * HD, (head + 1) * HD)
            num_ref[:rows, cols], den_ref[:rows, cols] = terms(q_ref[:rows, cols], k, v, key_block <= row_block)
            num_ref[rows:, cols], den_ref[rows:, cols] = terms(q_ref[rows:, cols], k_both, v_both, both)


def attention_pair_kernel(info, q_ref, num_in, den_in, first_ref, second_ref, num_ref, den_ref, *, step):
    first_valid = jnp.bitwise_and(info[2], 1) == 1 if step == 1 else info[2] >= 2 * (step - 1)
    second_valid = info[2] >= 2 * step
    cases = (
        (jnp.logical_and(first_valid, second_valid), [first_ref, second_ref]),
        (jnp.logical_and(first_valid, jnp.logical_not(second_valid)), [first_ref]),
        (jnp.logical_and(jnp.logical_not(first_valid), second_valid), [second_ref]),
    )
    for valid, refs in cases:
        @pl.when(valid)
        def _(refs=refs):
            for kv_head in range(refs[0].shape[1] // (2 * HD)):
                add_pieces(q_ref, num_ref, den_ref, kv_head, refs)


def attention_last_kernel(info, q_ref, num_in, den_in, piece_ref, num_ref, den_ref, out_ref, *, step, kv_head):
    valid = jnp.bitwise_and(info[2], 1) == 1 if step == 0 else info[2] >= 2 * step

    @pl.when(valid)
    def _():
        add_pieces(q_ref, num_ref, den_ref, kv_head, [piece_ref])

    width = out_ref.shape[1]
    for head in range(width // HD):
        cols = slice(kv_head * width + head * HD, kv_head * width + (head + 1) * HD)
        total = jnp.sum(den_ref[:, cols], axis=1, keepdims=True)
        out_ref[:, head * HD : (head + 1) * HD] = (num_ref[:, cols] / total).astype(BF16)


def out_first_kernel(info, ga, gb, ha, w_out, w_far, mixed_ref, *, tile):
    part = ga.shape[1]
    total = mixed_ref.shape[1]
    for start in range(0, total, tile):
        mine = pl.ds(pl.multiple_of(info[1] * total + start, 128), tile)
        cols = slice(start, start + tile)
        mixed = dot(ga[...], w_out[:part, mine]) + dot(gb[...], w_out[part:, mine])
        mixed_ref[:, cols] = mixed + dot(ha[...], w_far[:part, cols])


def out_last_kernel(info, live, hb, mixed_ref, w_far, clean_out, noisy_out, clean_ref, noisy_ref, sems, *, tile):
    rows, total = clean_ref.shape
    part = hb.shape[1]
    moves = []
    for start in range(0, total, tile):
        cols = slice(start, start + tile)
        mixed = mixed_ref[:, cols] + dot(hb[...], w_far[part:, cols])
        clean_ref[:, cols] = mixed[:rows].astype(BF16)
        for block in range(rows // BLK):
            part_rows = mixed[rows + block * BLK : rows + (block + 1) * BLK]
            noisy_ref[block * BLK : (block + 1) * BLK, cols] = (part_rows * live[block].astype(F32)).astype(BF16)
        for source, target in ((clean_ref, clean_out), (noisy_ref, noisy_out)):
            moves.append(pltpu.make_async_copy(source.at[:, cols], target.at[:, cols], sems.at[len(moves)]))
            moves[-1].start()
    for move in moves:
        move.wait()


WHOLE = pl.BlockSpec(memory_space=pltpu.VMEM)
HBM = pl.BlockSpec(memory_space=pltpu.HBM)
HINT = 1


def call(kernel, scalars, ins, outs, arrays, flops, num_bytes, scratch=(), exps=0, grid=1, aliases=None, limit=20):
    return pl.pallas_call(
        kernel,
        grid_spec=pltpu.PrefetchScalarGridSpec(
            num_scalar_prefetch=len(scalars),
            grid=(grid,),
            in_specs=ins,
            out_specs=[spec for spec, _ in outs],
            scratch_shapes=list(scratch),
        ),
        out_shape=[shape for _, shape in outs],
        compiler_params=pltpu.CompilerParams(vmem_limit_bytes=limit << 20),
        cost_estimate=pl.CostEstimate(
            flops=flops // HINT, bytes_accessed=num_bytes // HINT, transcendentals=exps // HINT
        ),
        input_output_aliases=aliases or {},
    )(*scalars, *arrays)


def after(value, *others):
    return lax.optimization_barrier((value, *others))[0]


def on_device(
    mesh, clean_tokens, norm_gain, mask_embed, time_shift, w_query, w_key, w_value, w_out,
    q_gain, k_gain, masked, block_live, timesteps,
):
    rows, half = clean_tokens.shape
    heads_width = w_query.shape[1]
    kv_width = w_key.shape[1]
    part = heads_width // 2
    ctx = mesh.shape["ctx"]
    c, p, t = lax.axis_index("copy"), lax.axis_index("ctx"), lax.axis_index("tp")
    info = jnp.stack([c, t, p, timesteps[0]]).astype(jnp.int32)
    pair = [(0, 1), (1, 0)]
    cross_x = lambda v: lax.ppermute(v, "copy", pair)
    cross_core = lambda v: lax.ppermute(v, "tp", pair)
    shape = jax.ShapeDtypeStruct

    cut = rows // 2
    out_cols = w_out.shape[1] // 2
    qg, kg = q_gain[None], k_gain[None]
    vmem = lambda dims, kind: (WHOLE, pltpu.VMEM(dims, kind))
    in_hbm = lambda v: pltpu.with_memory_space_constraint(v, pltpu.HBM)

    x, mask, shift, squares = call(
        squares_kernel, [], [HBM] * 3,
        [vmem((rows, half), BF16), vmem((1, rows), jnp.int32), vmem((1, 2 * half), F32), vmem((1, rows), F32)],
        [in_hbm(clean_tokens), in_hbm(masked), in_hbm(time_shift[None])], 2 * rows * half, rows * half * 2,
        [pltpu.SemaphoreType.DMA((3,))],
    )
    other_squares = cross_x(squares)
    strip, = call(strip_kernel, [info], [WHOLE], [vmem((cut, half), BF16)], [x], 0, rows * half)
    near = cross_x(strip)
    stats = [squares, other_squares, mask]
    vectors = [norm_gain[None], mask_embed[None], shift]
    buffers = [(half, heads_width), (half, kv_width), (half, kv_width)]
    per_row = heads_width + 2 * kv_width

    pq, pk, pv, *weights, w_send = call(
        own_half_kernel, [info], [WHOLE] * 7 + [HBM] * 4,
        [vmem((2 * rows, width), F32) for width in (heads_width, kv_width, kv_width)]
        + [vmem(dims, BF16) for dims in buffers] + [vmem((heads_width, out_cols), BF16)],
        [x] + stats + vectors + [in_hbm(w) for w in (w_query, w_key, w_value, w_out)],
        32 * rows * half * per_row, 2 * half * per_row * 2,
        [pltpu.VMEM(dims, BF16) for dims in buffers] + [pltpu.SemaphoreType.DMA((10,))], limit=32,
    )
    near = after(near, pk)
    far = cross_core(near)

    kv, = call(
        clean_kv_kernel, [info], [WHOLE] * 12, [vmem((rows, 2 * kv_width), BF16)],
        [near, far] + stats + vectors[:2] + weights[1:] + [pk, pv, kg],
        4 * rows * half * kv_width, half * 2 * kv_width * 2,
    )

    steps = ctx // 2
    along = lambda v: lax.ppermute(v, "ctx", [(i, i + 2) for i in range(ctx - 2)])
    across = lambda v: lax.ppermute(v, "ctx", [(i, i ^ 1) for i in range(ctx)])
    crossed = across(kv)
    column = along(kv)
    w_far = cross_core(after(w_send, kv))
    near = after(near, kv)
    q, own = call(
        other_half_kernel, [info], [WHOLE] * 16,
        [vmem((2 * rows, heads_width), BF16), vmem((rows, 2 * kv_width), BF16)],
        [near, far] + stats + vectors + weights + [pq, pk, pv, qg, kg],
        4 * rows * half * per_row, half * per_row * 2,
    )

    acc = [vmem((2 * rows, heads_width), F32)] * 2
    unit = rows * rows * heads_width // HD
    cost = lambda units: (4 * HD * unit * units, 8 * unit, (), unit * units)
    in_place = {2: 0, 3: 1}
    num, den = call(attention_own_kernel, [info], [WHOLE] * 3, acc, [q, kv, own], *cost(3))
    w_far = after(w_far, num)
    for step in range(1, steps):
        column = after(column, num)
        before, crossed = crossed, across(column)
        here, column = column, along(column) if step < steps - 1 else None
        num, den = call(
            functools.partial(attention_pair_kernel, step=step), [info], [WHOLE] * 5, acc,
            [q, num, den, before, here], *cost(4), aliases=in_place,
        )
    attended = []
    for kv_head in range(2):
        num, den, result = call(
            functools.partial(attention_last_kernel, step=steps - 1, kv_head=kv_head), [info], [WHOLE] * 4,
            acc + [vmem((2 * rows, part), BF16)], [q, num, den, crossed], *cost(1), aliases=in_place,
        )
        attended.append((result, cross_core(result)))

    (ga, ha), (gb, hb) = attended
    tile = 512
    mixed, = call(
        functools.partial(out_first_kernel, tile=tile), [info], [WHOLE] * 5, [vmem((2 * rows, out_cols), F32)],
        [ga, gb, ha, w_out, w_far], 6 * rows * heads_width * out_cols, 2 * heads_width * out_cols * 2,
    )
    out = shape((rows, out_cols), BF16)
    clean_out, noised_out = call(
        functools.partial(out_last_kernel, tile=tile), [info, block_live[0]], [WHOLE] * 3, [(HBM, out), (HBM, out)],
        [hb, mixed, w_far], 2 * rows * heads_width * out_cols, heads_width * out_cols * 2,
        [pltpu.VMEM((rows, out_cols), BF16)] * 2 + [pltpu.SemaphoreType.DMA((2 * (out_cols // tile),))],
    )
    return (clean_out, noised_out[None])


def solution(mesh):
    in_specs = (
        P("ctx", "copy"),
        P(),
        P(),
        P(),
        P(None, "tp"),
        P(None, "tp"),
        P(None, "tp"),
        P("tp", None),
        P(),
        P(),
        P("copy", "ctx"),
        P("copy", "ctx"),
        P("copy"),
    )
    out_specs = (P("ctx", "tp"), P("copy", "ctx", "tp"))
    return jax.shard_map(
        functools.partial(on_device, mesh), mesh=mesh, in_specs=in_specs, out_specs=out_specs, check_vma=False
    )
```

```python
import functools
import math

import jax
import jax.numpy as jnp
from jax import lax
from jax.experimental import pallas as pl
from jax.experimental.pallas import tpu as pltpu
from jax.sharding import PartitionSpec as P

HD = 128
BLK = 64
TSTEPS = 1000
EPS = 1e-06
F32 = jnp.float32
BF16 = jnp.bfloat16
SCORE_SCALE = math.log2(math.e) / math.sqrt(HD)


def to_column(row, n):
    eye = lax.broadcasted_iota(jnp.int32, (n, n), 0) == lax.broadcasted_iota(jnp.int32, (n, n), 1)
    return jnp.sum(jnp.where(eye, jnp.broadcast_to(row, (n, n)), 0.0), axis=1, keepdims=True)


def row_scales(own_ref, other_ref, mask_ref, embed_ref, width):
    n = own_ref.shape[1]
    clean = lax.rsqrt(to_column(own_ref[...] + other_ref[...], n) * (1.0 / width) + EPS)
    embed = embed_ref[...].astype(F32)
    embed_scale = lax.rsqrt(jnp.sum(embed * embed, axis=1, keepdims=True) * (1.0 / width) + EPS)
    masked = to_column(mask_ref[...].astype(F32), n)
    return clean, embed_scale, masked


def normed_clean(x, clean_scale, gain):
    return (x * clean_scale * gain).astype(BF16)


def normed_noisy(x, clean_scale, embed_scale, masked, gain, embed, condition):
    is_masked = masked == 1.0
    noisy = jnp.where(is_masked, embed, x)
    scale = jnp.where(is_masked, embed_scale, clean_scale)
    return (noisy * scale * gain * condition).astype(BF16)


def dot(a, b):
    return jnp.dot(a, b, preferred_element_type=F32)


def head_norm(wide, gain):
    scale = lax.rsqrt(jnp.mean(wide * wide, axis=1, keepdims=True) + EPS)
    return (wide * scale * gain).astype(BF16)


def both_streams(x, scales, gain, embed, condition):
    clean = normed_clean(x, scales[0], gain)
    noisy = normed_noisy(x, scales[0], scales[1], scales[2], gain, embed, condition)
    return clean, noisy


def half_vectors(at, info, gain_ref, embed_ref, shift_ref):
    gain = gain_ref[:, at].astype(F32)
    embed = embed_ref[:, at].astype(F32)
    condition = 1.0 + info[3].astype(F32) / TSTEPS * shift_ref[:, at]
    return gain, embed, condition


def both_streams(x, scales, gain, embed, condition):
    clean = normed_clean(x, scales[0], gain)
    noisy = normed_noisy(x, scales[0], scales[1], scales[2], gain, embed, condition)
    return clean, noisy


def vectors_at(at, info, gain_ref, embed_ref, shift_ref):
    gain = gain_ref[:, at].astype(F32)
    embed = embed_ref[:, at].astype(F32)
    condition = 1.0 + info[3].astype(F32) / TSTEPS * shift_ref[:, at]
    return gain, embed, condition


def squares_kernel(x_hbm, mask_hbm, shift_hbm, x_ref, mask_ref, shift_ref, squares_ref, strip_ref, sems):
    moves = [
        pltpu.make_async_copy(source, target, sems.at[number])
        for number, (source, target) in enumerate(((x_hbm, x_ref), (mask_hbm, mask_ref), (shift_hbm, shift_ref)))
    ]
    for move in moves:
        move.start()
    for move in moves:
        move.wait()
    rows = x_ref.shape[0]
    x = x_ref[...].astype(F32)
    sums = jnp.sum(x * x, axis=1, keepdims=True)
    eye = lax.broadcasted_iota(jnp.int32, (rows, rows), 0) == lax.broadcasted_iota(jnp.int32, (rows, rows), 1)
    squares_ref[...] = jnp.sum(jnp.where(eye, jnp.broadcast_to(sums, (rows, rows)), 0.0), axis=0, keepdims=True)
    cut = strip_ref.shape[0]
    strip = pl.ds(pl.multiple_of(lax.axis_index("tp") * cut, 128), cut)
    strip_ref[...] = x_ref[strip]


def own_half_kernel(
    info, x_ref, own_ref, other_ref, mask_ref, gain_ref, embed_ref, shift_ref, wq, wk, wv, w_out,
    q_ref, k_ref, v_ref, rest_q, rest_k, rest_v, w_send, own_q, own_k, own_v, sems,
):
    half = x_ref.shape[1]
    depth = half // 2
    first = info[0] * half
    moves = []

    def move(source, target):
        moves.append(pltpu.make_async_copy(source, target, sems.at[len(moves)]))
        moves[-1].start()

    for chunk in range(2):
        there = pl.ds(pl.multiple_of(first + chunk * depth, 128), depth)
        here = pl.ds(chunk * depth, depth)
        for source, target in ((wk, own_k), (wv, own_v), (wq, own_q)):
            move(source.at[there], target.at[here])
    rest = pl.ds(pl.multiple_of(half - first, 128), half)
    for source, target in ((wk, rest_k), (wv, rest_v), (wq, rest_q)):
        move(source.at[rest], target)
    cols = w_send.shape[1]
    move(w_out.at[:, pl.ds(pl.multiple_of((1 - info[1]) * cols, 128), cols)], w_send)

    scales = row_scales(own_ref, other_ref, mask_ref, embed_ref, embed_ref.shape[1])
    at = pl.ds(pl.multiple_of(first, 128), half)
    gain, embed, condition = vectors_at(at, info, gain_ref, embed_ref, shift_ref)
    clean, noisy = both_streams(x_ref[...].astype(F32), scales, gain, embed, condition)
    both = jnp.concatenate([clean, noisy], axis=0)
    for chunk in range(2):
        here = slice(chunk * depth, (chunk + 1) * depth)
        for number, (target, weight) in enumerate(((k_ref, own_k), (v_ref, own_v), (q_ref, own_q))):
            moves[3 * chunk + number].wait()
            product = dot(both[:, here], weight[here])
            target[...] = product if chunk == 0 else target[...] + product
    for copy in moves[6:]:
        copy.wait()


def other_rows(info, near_ref, far_ref):
    near, far = near_ref[...].astype(F32), far_ref[...].astype(F32)
    first = info[1] == 0
    return jnp.concatenate([jnp.where(first, near, far), jnp.where(first, far, near)], axis=0)


def other_half(info, half):
    return pl.ds(pl.multiple_of((1 - info[0]) * half, 128), half)


def kv_out(ref, k, v, gain):
    for head in range(k.shape[1] // HD):
        cols = slice(head * HD, (head + 1) * HD)
        ref[:, 2 * head * HD : (2 * head + 1) * HD] = head_norm(k[:, cols], gain)
        ref[:, (2 * head + 1) * HD : 2 * (head + 1) * HD] = v[:, cols].astype(BF16)


def clean_kv_kernel(
    info, near_ref, far_ref, own_ref, other_ref, mask_ref, gain_ref, embed_ref,
    wk_ref, wv_ref, pk_ref, pv_ref, kgain_ref, all_ref,
):
    rows = all_ref.shape[0]
    width = embed_ref.shape[1]
    clean_scale = row_scales(own_ref, other_ref, mask_ref, embed_ref, width)[0]
    at = other_half(info, near_ref.shape[1])
    clean = normed_clean(other_rows(info, near_ref, far_ref), clean_scale, gain_ref[:, at].astype(F32))
    k = pk_ref[:rows] + dot(clean, wk_ref[...])
    v = pv_ref[:rows] + dot(clean, wv_ref[...])
    kv_out(all_ref, k, v, kgain_ref[...])


def other_half_kernel(
    info, near_ref, far_ref, own_ref, other_ref, mask_ref, gain_ref, embed_ref, shift_ref,
    wq_ref, wk_ref, wv_ref, pq_ref, pk_ref, pv_ref, qgain_ref, kgain_ref, q_ref, self_ref,
):
    rows = self_ref.shape[0]
    width = embed_ref.shape[1]
    scales = row_scales(own_ref, other_ref, mask_ref, embed_ref, width)
    at = other_half(info, near_ref.shape[1])
    gain, embed, condition = vectors_at(at, info, gain_ref, embed_ref, shift_ref)
    clean, noisy = both_streams(other_rows(info, near_ref, far_ref), scales, gain, embed, condition)
    k = pk_ref[rows:] + dot(noisy, wk_ref[...])
    v = pv_ref[rows:] + dot(noisy, wv_ref[...])
    kv_out(self_ref, k, v, kgain_ref[...])
    q = pq_ref[...] + dot(jnp.concatenate([clean, noisy], axis=0), wq_ref[...])
    for head in range(q_ref.shape[1] // HD):
        cols = slice(head * HD, (head + 1) * HD)
        q_ref[:, cols] = head_norm(q[:, cols], qgain_ref[...])


def terms(q, k, v, mask):
    scores = lax.dot_general(q, k, (((1,), (1,)), ((), ())), preferred_element_type=F32)
    e = jnp.exp2(scores * SCORE_SCALE)
    if mask is not None:
        e = jnp.where(mask, e, 0.0)
    den = e[:, :HD]
    for start in range(HD, e.shape[1], HD):
        den = den + e[:, start : start + HD]
    return dot(e.astype(BF16), v), den


def add_pieces(q_ref, num_ref, den_ref, kv_head, piece_refs):
    rows, width = piece_refs[0].shape
    group = q_ref.shape[1] // HD // (width // (2 * HD))
    base = 2 * kv_head * HD
    k = jnp.concatenate([ref[:, base : base + HD] for ref in piece_refs], axis=0)
    v = jnp.concatenate([ref[:, base + HD : base + 2 * HD] for ref in piece_refs], axis=0)
    for head in range(kv_head * group, (kv_head + 1) * group):
        cols = slice(head * HD, (head + 1) * HD)
        num, den = terms(q_ref[:, cols], k, v, None)
        num_ref[:, cols] += num
        den_ref[:, cols] += den


def attention_own_kernel(info, q_ref, kv_ref, self_ref, num_ref, den_ref):
    rows = kv_ref.shape[0]
    kv_heads = kv_ref.shape[1] // (2 * HD)
    group = q_ref.shape[1] // HD // kv_heads
    row = lax.broadcasted_iota(jnp.int32, (2 * rows, rows), 0)
    key_block = lax.broadcasted_iota(jnp.int32, (2 * rows, rows), 1) // BLK
    noisy = row >= rows
    row_block = jnp.where(noisy, row - rows, row) // BLK
    same = key_block == row_block
    allowed = jnp.logical_or(key_block < row_block, jnp.logical_and(same, jnp.logical_not(noisy)))
    for kv_head in range(kv_heads):
        k_cols = slice(2 * kv_head * HD, (2 * kv_head + 1) * HD)
        v_cols = slice((2 * kv_head + 1) * HD, 2 * (kv_head + 1) * HD)
        for head in range(kv_head * group, (kv_head + 1) * group, 2):
            pair = [slice(one * HD, (one + 1) * HD) for one in (head, head + 1)]
            for cols in pair:
                num_ref[:, cols], den_ref[:, cols] = terms(q_ref[:, cols], kv_ref[:, k_cols], kv_ref[:, v_cols], allowed)
            q_noisy = jnp.concatenate([q_ref[rows:, cols] for cols in pair], axis=0)
            num, den = terms(q_noisy, self_ref[:, k_cols], self_ref[:, v_cols], same)
            for number, cols in enumerate(pair):
                num_ref[rows:, cols] += num[number * rows : (number + 1) * rows]
                den_ref[rows:, cols] += den[number * rows : (number + 1) * rows]


def attention_pair_kernel(info, q_ref, num_in, den_in, first_ref, second_ref, num_ref, den_ref, *, step):
    first_valid = jnp.bitwise_and(info[2], 1) == 1 if step == 1 else info[2] >= 2 * (step - 1)
    second_valid = info[2] >= 2 * step
    cases = (
        (jnp.logical_and(first_valid, second_valid), [first_ref, second_ref]),
        (jnp.logical_and(first_valid, jnp.logical_not(second_valid)), [first_ref]),
        (jnp.logical_and(jnp.logical_not(first_valid), second_valid), [second_ref]),
    )
    for valid, refs in cases:
        @pl.when(valid)
        def _(refs=refs):
            for kv_head in range(refs[0].shape[1] // (2 * HD)):
                add_pieces(q_ref, num_ref, den_ref, kv_head, refs)


def attention_last_kernel(info, q_ref, num_in, den_in, piece_ref, num_ref, den_ref, out_ref, *, step, kv_head):
    valid = jnp.bitwise_and(info[2], 1) == 1 if step == 0 else info[2] >= 2 * step

    @pl.when(valid)
    def _():
        add_pieces(q_ref, num_ref, den_ref, kv_head, [piece_ref])

    width = out_ref.shape[1]
    for head in range(width // HD):
        cols = slice(kv_head * width + head * HD, kv_head * width + (head + 1) * HD)
        total = jnp.sum(den_ref[:, cols], axis=1, keepdims=True)
        out_ref[:, head * HD : (head + 1) * HD] = (num_ref[:, cols] / total).astype(BF16)


def out_first_kernel(info, ga, gb, ha, w_out, w_far, mixed_ref, *, tile):
    part = ga.shape[1]
    total = mixed_ref.shape[1]
    for start in range(0, total, tile):
        mine = pl.ds(pl.multiple_of(info[1] * total + start, 128), tile)
        cols = slice(start, start + tile)
        mixed = dot(ga[...], w_out[:part, mine]) + dot(gb[...], w_out[part:, mine])
        mixed_ref[:, cols] = mixed + dot(ha[...], w_far[:part, cols])


def out_last_kernel(info, live, hb, mixed_ref, w_far, clean_out, noisy_out, clean_ref, noisy_ref, sems, *, tile):
    rows, total = clean_ref.shape
    part = hb.shape[1]
    moves = []
    for start in range(0, total, tile):
        cols = slice(start, start + tile)
        mixed = mixed_ref[:, cols] + dot(hb[...], w_far[part:, cols])
        clean_ref[:, cols] = mixed[:rows].astype(BF16)
        for block in range(rows // BLK):
            part_rows = mixed[rows + block * BLK : rows + (block + 1) * BLK]
            noisy_ref[block * BLK : (block + 1) * BLK, cols] = (part_rows * live[block].astype(F32)).astype(BF16)
        for source, target in ((clean_ref, clean_out), (noisy_ref, noisy_out)):
            moves.append(pltpu.make_async_copy(source.at[:, cols], target.at[:, cols], sems.at[len(moves)]))
            moves[-1].start()
    for move in moves:
        move.wait()


WHOLE = pl.BlockSpec(memory_space=pltpu.VMEM)
HBM = pl.BlockSpec(memory_space=pltpu.HBM)
HINT = 1


def call(kernel, scalars, ins, outs, arrays, flops, num_bytes, scratch=(), exps=0, grid=1, aliases=None, limit=20):
    return pl.pallas_call(
        kernel,
        grid_spec=pltpu.PrefetchScalarGridSpec(
            num_scalar_prefetch=len(scalars),
            grid=(grid,),
            in_specs=ins,
            out_specs=[spec for spec, _ in outs],
            scratch_shapes=list(scratch),
        ),
        out_shape=[shape for _, shape in outs],
        compiler_params=pltpu.CompilerParams(vmem_limit_bytes=limit << 20),
        cost_estimate=pl.CostEstimate(
            flops=flops // HINT, bytes_accessed=num_bytes // HINT, transcendentals=exps // HINT
        ),
        input_output_aliases=aliases or {},
    )(*scalars, *arrays)


def after(value, *others):
    return lax.optimization_barrier((value, *others))[0]


def on_device(
    mesh, clean_tokens, norm_gain, mask_embed, time_shift, w_query, w_key, w_value, w_out,
    q_gain, k_gain, masked, block_live, timesteps,
):
    rows, half = clean_tokens.shape
    heads_width = w_query.shape[1]
    kv_width = w_key.shape[1]
    part = heads_width // 2
    ctx = mesh.shape["ctx"]
    c, p, t = lax.axis_index("copy"), lax.axis_index("ctx"), lax.axis_index("tp")
    info = jnp.stack([c, t, p, timesteps[0]]).astype(jnp.int32)
    pair = [(0, 1), (1, 0)]
    cross_x = lambda v: lax.ppermute(v, "copy", pair)
    cross_core = lambda v: lax.ppermute(v, "tp", pair)
    shape = jax.ShapeDtypeStruct

    cut = rows // 2
    out_cols = w_out.shape[1] // 2
    qg, kg = q_gain[None], k_gain[None]
    vmem = lambda dims, kind: (WHOLE, pltpu.VMEM(dims, kind))
    in_hbm = lambda v: pltpu.with_memory_space_constraint(v, pltpu.HBM)

    x, mask, shift, squares, strip = call(
        squares_kernel, [], [HBM] * 3,
        [vmem((rows, half), BF16), vmem((1, rows), jnp.int32), vmem((1, 2 * half), F32), vmem((1, rows), F32),
         vmem((cut, half), BF16)],
        [in_hbm(clean_tokens), in_hbm(masked), in_hbm(time_shift[None])], 2 * rows * half, rows * half * 2,
        [pltpu.SemaphoreType.DMA((3,))],
    )
    other_squares = cross_x(squares)
    near = cross_x(strip)
    stats = [squares, other_squares, mask]
    vectors = [norm_gain[None], mask_embed[None], shift]
    buffers = [(half, heads_width), (half, kv_width), (half, kv_width)]
    per_row = heads_width + 2 * kv_width

    pq, pk, pv, *weights, w_send = call(
        own_half_kernel, [info], [WHOLE] * 7 + [HBM] * 4,
        [vmem((2 * rows, width), F32) for width in (heads_width, kv_width, kv_width)]
        + [vmem(dims, BF16) for dims in buffers] + [vmem((heads_width, out_cols), BF16)],
        [x] + stats + vectors + [in_hbm(w) for w in (w_query, w_key, w_value, w_out)],
        32 * rows * half * per_row, 2 * half * per_row * 2,
        [pltpu.VMEM(dims, BF16) for dims in buffers] + [pltpu.SemaphoreType.DMA((10,))], limit=32,
    )
    near = after(near, pk)
    far = cross_core(near)

    kv, = call(
        clean_kv_kernel, [info], [WHOLE] * 12, [vmem((rows, 2 * kv_width), BF16)],
        [near, far] + stats + vectors[:2] + weights[1:] + [pk, pv, kg],
        4 * rows * half * kv_width, half * 2 * kv_width * 2,
    )

    steps = ctx // 2
    along = lambda v: lax.ppermute(v, "ctx", [(i, i + 2) for i in range(ctx - 2)])
    across = lambda v: lax.ppermute(v, "ctx", [(i, i ^ 1) for i in range(ctx)])
    crossed = across(kv)
    column = along(kv)
    w_far = cross_core(after(w_send, kv))
    near = after(near, kv)
    q, own = call(
        other_half_kernel, [info], [WHOLE] * 16,
        [vmem((2 * rows, heads_width), BF16), vmem((rows, 2 * kv_width), BF16)],
        [near, far] + stats + vectors + weights + [pq, pk, pv, qg, kg],
        4 * rows * half * per_row, half * per_row * 2,
    )

    acc = [vmem((2 * rows, heads_width), F32)] * 2
    unit = rows * rows * heads_width // HD
    cost = lambda units: (4 * HD * unit * units, 8 * unit, (), unit * units)
    in_place = {2: 0, 3: 1}
    num, den = call(attention_own_kernel, [info], [WHOLE] * 3, acc, [q, kv, own], *cost(3))
    w_far = after(w_far, num)
    for step in range(1, steps):
        column = after(column, num)
        before, crossed = crossed, across(column)
        here, column = column, along(column) if step < steps - 1 else None
        num, den = call(
            functools.partial(attention_pair_kernel, step=step), [info], [WHOLE] * 5, acc,
            [q, num, den, before, here], *cost(4), aliases=in_place,
        )
    attended = []
    for kv_head in range(2):
        num, den, result = call(
            functools.partial(attention_last_kernel, step=steps - 1, kv_head=kv_head), [info], [WHOLE] * 4,
            acc + [vmem((2 * rows, part), BF16)], [q, num, den, crossed], *cost(1), aliases=in_place,
        )
        attended.append((result, cross_core(result)))

    (ga, ha), (gb, hb) = attended
    tile = 512
    mixed, = call(
        functools.partial(out_first_kernel, tile=tile), [info], [WHOLE] * 5, [vmem((2 * rows, out_cols), F32)],
        [ga, gb, ha, w_out, w_far], 6 * rows * heads_width * out_cols, 2 * heads_width * out_cols * 2,
    )
    out = shape((rows, out_cols), BF16)
    clean_out, noised_out = call(
        functools.partial(out_last_kernel, tile=tile), [info, block_live[0]], [WHOLE] * 3, [(HBM, out), (HBM, out)],
        [hb, mixed, w_far], 2 * rows * heads_width * out_cols, heads_width * out_cols * 2,
        [pltpu.VMEM((rows, out_cols), BF16)] * 2 + [pltpu.SemaphoreType.DMA((2 * (out_cols // tile),))],
    )
    return (clean_out, noised_out[None])


def solution(mesh):
    in_specs = (
        P("ctx", "copy"),
        P(),
        P(),
        P(),
        P(None, "tp"),
        P(None, "tp"),
        P(None, "tp"),
        P("tp", None),
        P(),
        P(),
        P("copy", "ctx"),
        P("copy", "ctx"),
        P("copy"),
    )
    out_specs = (P("ctx", "tp"), P("copy", "ctx", "tp"))
    return jax.shard_map(
        functools.partial(on_device, mesh), mesh=mesh, in_specs=in_specs, out_specs=out_specs, check_vma=False
    )
```

```python
import functools
import math

import jax
import jax.numpy as jnp
from jax import lax
from jax.experimental import pallas as pl
from jax.experimental.pallas import tpu as pltpu
from jax.sharding import PartitionSpec as P

HD = 128
BLK = 64
TSTEPS = 1000
EPS = 1e-06
F32 = jnp.float32
BF16 = jnp.bfloat16
SCORE_SCALE = math.log2(math.e) / math.sqrt(HD)


def to_column(row, n):
    eye = lax.broadcasted_iota(jnp.int32, (n, n), 0) == lax.broadcasted_iota(jnp.int32, (n, n), 1)
    return jnp.sum(jnp.where(eye, jnp.broadcast_to(row, (n, n)), 0.0), axis=1, keepdims=True)


def row_scales(own_ref, other_ref, mask_ref, embed_ref, width):
    n = own_ref.shape[1]
    clean = lax.rsqrt(to_column(own_ref[...] + other_ref[...], n) * (1.0 / width) + EPS)
    embed = embed_ref[...].astype(F32)
    embed_scale = lax.rsqrt(jnp.sum(embed * embed, axis=1, keepdims=True) * (1.0 / width) + EPS)
    masked = to_column(mask_ref[...].astype(F32), n)
    return clean, embed_scale, masked


def normed_clean(x, clean_scale, gain):
    return (x * clean_scale * gain).astype(BF16)


def normed_noisy(x, clean_scale, embed_scale, masked, gain, embed, condition):
    is_masked = masked == 1.0
    noisy = jnp.where(is_masked, embed, x)
    scale = jnp.where(is_masked, embed_scale, clean_scale)
    return (noisy * scale * gain * condition).astype(BF16)


def dot(a, b):
    return jnp.dot(a, b, preferred_element_type=F32)


def head_norm(wide, gain):
    scale = lax.rsqrt(jnp.mean(wide * wide, axis=1, keepdims=True) + EPS)
    return (wide * scale * gain).astype(BF16)


def both_streams(x, scales, gain, embed, condition):
    clean = normed_clean(x, scales[0], gain)
    noisy = normed_noisy(x, scales[0], scales[1], scales[2], gain, embed, condition)
    return clean, noisy


def half_vectors(at, info, gain_ref, embed_ref, shift_ref):
    gain = gain_ref[:, at].astype(F32)
    embed = embed_ref[:, at].astype(F32)
    condition = 1.0 + info[3].astype(F32) / TSTEPS * shift_ref[:, at]
    return gain, embed, condition


def both_streams(x, scales, gain, embed, condition):
    clean = normed_clean(x, scales[0], gain)
    noisy = normed_noisy(x, scales[0], scales[1], scales[2], gain, embed, condition)
    return clean, noisy


def vectors_at(at, info, gain_ref, embed_ref, shift_ref):
    gain = gain_ref[:, at].astype(F32)
    embed = embed_ref[:, at].astype(F32)
    condition = 1.0 + info[3].astype(F32) / TSTEPS * shift_ref[:, at]
    return gain, embed, condition


def squares_kernel(x_hbm, mask_hbm, shift_hbm, x_ref, mask_ref, shift_ref, squares_ref, strip_ref, sems):
    moves = [
        pltpu.make_async_copy(source, target, sems.at[number])
        for number, (source, target) in enumerate(((x_hbm, x_ref), (mask_hbm, mask_ref), (shift_hbm, shift_ref)))
    ]
    for move in moves:
        move.start()
    for move in moves:
        move.wait()
    rows = x_ref.shape[0]
    x = x_ref[...].astype(F32)
    sums = jnp.sum(x * x, axis=1, keepdims=True)
    eye = lax.broadcasted_iota(jnp.int32, (rows, rows), 0) == lax.broadcasted_iota(jnp.int32, (rows, rows), 1)
    squares_ref[...] = jnp.sum(jnp.where(eye, jnp.broadcast_to(sums, (rows, rows)), 0.0), axis=0, keepdims=True)
    cut = strip_ref.shape[0]
    strip = pl.ds(pl.multiple_of(lax.axis_index("tp") * cut, 128), cut)
    strip_ref[...] = x_ref[strip]


def own_half_kernel(
    info, x_ref, own_ref, other_ref, mask_ref, gain_ref, embed_ref, shift_ref, wq, wk, wv, w_out,
    q_ref, k_ref, v_ref, rest_q, rest_k, rest_v, w_send, own_q, own_k, own_v, sems,
):
    half = x_ref.shape[1]
    depth = half // 2
    first = info[0] * half
    moves = []

    def move(source, target):
        moves.append(pltpu.make_async_copy(source, target, sems.at[len(moves)]))
        moves[-1].start()

    for chunk in range(2):
        there = pl.ds(pl.multiple_of(first + chunk * depth, 128), depth)
        here = pl.ds(chunk * depth, depth)
        for source, target in ((wk, own_k), (wv, own_v), (wq, own_q)):
            move(source.at[there], target.at[here])
    rest = pl.ds(pl.multiple_of(half - first, 128), half)
    for source, target in ((wk, rest_k), (wv, rest_v), (wq, rest_q)):
        move(source.at[rest], target)
    cols = w_send.shape[1]
    move(w_out.at[:, pl.ds(pl.multiple_of((1 - info[1]) * cols, 128), cols)], w_send)

    scales = row_scales(own_ref, other_ref, mask_ref, embed_ref, embed_ref.shape[1])
    at = pl.ds(pl.multiple_of(first, 128), half)
    gain, embed, condition = vectors_at(at, info, gain_ref, embed_ref, shift_ref)
    clean, noisy = both_streams(x_ref[...].astype(F32), scales, gain, embed, condition)
    both = jnp.concatenate([clean, noisy], axis=0)
    for chunk in range(2):
        here = slice(chunk * depth, (chunk + 1) * depth)
        for number, (target, weight) in enumerate(((k_ref, own_k), (v_ref, own_v), (q_ref, own_q))):
            moves[3 * chunk + number].wait()
            product = dot(both[:, here], weight[here])
            target[...] = product if chunk == 0 else target[...] + product
    for copy in moves[6:]:
        copy.wait()


def other_rows(info, near_ref, far_ref):
    near, far = near_ref[...].astype(F32), far_ref[...].astype(F32)
    first = info[1] == 0
    return jnp.concatenate([jnp.where(first, near, far), jnp.where(first, far, near)], axis=0)


def other_half(info, half):
    return pl.ds(pl.multiple_of((1 - info[0]) * half, 128), half)


def kv_out(ref, k, v, gain):
    for head in range(k.shape[1] // HD):
        cols = slice(head * HD, (head + 1) * HD)
        ref[:, 2 * head * HD : (2 * head + 1) * HD] = head_norm(k[:, cols], gain)
        ref[:, (2 * head + 1) * HD : 2 * (head + 1) * HD] = v[:, cols].astype(BF16)


def clean_kv_kernel(
    info, near_ref, far_ref, own_ref, other_ref, mask_ref, gain_ref, embed_ref,
    wk_ref, wv_ref, pk_ref, pv_ref, kgain_ref, all_ref, one_ref,
):
    rows = all_ref.shape[0]
    width = embed_ref.shape[1]
    clean_scale = row_scales(own_ref, other_ref, mask_ref, embed_ref, width)[0]
    at = other_half(info, near_ref.shape[1])
    clean = normed_clean(other_rows(info, near_ref, far_ref), clean_scale, gain_ref[:, at].astype(F32))
    k = pk_ref[:rows] + dot(clean, wk_ref[...])
    v = pv_ref[:rows] + dot(clean, wv_ref[...])
    kv_out(all_ref, k, v, kgain_ref[...])
    cols = one_ref.shape[1]
    one_ref[...] = all_ref[:, pl.ds(pl.multiple_of(info[0] * cols, 128), cols)]


def other_half_kernel(
    info, near_ref, far_ref, own_ref, other_ref, mask_ref, gain_ref, embed_ref, shift_ref,
    wq_ref, wk_ref, wv_ref, pq_ref, pk_ref, pv_ref, qgain_ref, kgain_ref, q_ref, self_ref,
):
    rows = self_ref.shape[0]
    width = embed_ref.shape[1]
    scales = row_scales(own_ref, other_ref, mask_ref, embed_ref, width)
    at = other_half(info, near_ref.shape[1])
    gain, embed, condition = vectors_at(at, info, gain_ref, embed_ref, shift_ref)
    clean, noisy = both_streams(other_rows(info, near_ref, far_ref), scales, gain, embed, condition)
    k = pk_ref[rows:] + dot(noisy, wk_ref[...])
    v = pv_ref[rows:] + dot(noisy, wv_ref[...])
    kv_out(self_ref, k, v, kgain_ref[...])
    q = pq_ref[...] + dot(jnp.concatenate([clean, noisy], axis=0), wq_ref[...])
    for head in range(q_ref.shape[1] // HD):
        cols = slice(head * HD, (head + 1) * HD)
        q_ref[:, cols] = head_norm(q[:, cols], qgain_ref[...])


def terms(q, k, v, mask):
    scores = lax.dot_general(q, k, (((1,), (1,)), ((), ())), preferred_element_type=F32)
    e = jnp.exp2(scores * SCORE_SCALE)
    if mask is not None:
        e = jnp.where(mask, e, 0.0)
    den = e[:, :HD]
    for start in range(HD, e.shape[1], HD):
        den = den + e[:, start : start + HD]
    return dot(e.astype(BF16), v), den


def add_pieces(q_ref, num_ref, den_ref, base, heads, pieces):
    k = jnp.concatenate([piece[:, :HD] for piece in pieces], axis=0)
    v = jnp.concatenate([piece[:, HD:] for piece in pieces], axis=0)
    for head in range(heads):
        cols = pl.ds(base + head * HD, HD)
        num, den = terms(q_ref[:, cols], k, v, None)
        num_ref[:, cols] += num
        den_ref[:, cols] += den


def head_base(info, which, width):
    return pl.multiple_of((info[0] if which == 0 else 1 - info[0]) * width, 128)


def attention_own_kernel(info, q_ref, kv_ref, self_ref, num_ref, den_ref):
    rows = kv_ref.shape[0]
    kv_heads = kv_ref.shape[1] // (2 * HD)
    group = q_ref.shape[1] // HD // kv_heads
    row = lax.broadcasted_iota(jnp.int32, (2 * rows, rows), 0)
    key_block = lax.broadcasted_iota(jnp.int32, (2 * rows, rows), 1) // BLK
    noisy = row >= rows
    row_block = jnp.where(noisy, row - rows, row) // BLK
    same = key_block == row_block
    allowed = jnp.logical_or(key_block < row_block, jnp.logical_and(same, jnp.logical_not(noisy)))
    for kv_head in range(kv_heads):
        k_cols = slice(2 * kv_head * HD, (2 * kv_head + 1) * HD)
        v_cols = slice((2 * kv_head + 1) * HD, 2 * (kv_head + 1) * HD)
        for head in range(kv_head * group, (kv_head + 1) * group, 2):
            pair = [slice(one * HD, (one + 1) * HD) for one in (head, head + 1)]
            for cols in pair:
                num_ref[:, cols], den_ref[:, cols] = terms(q_ref[:, cols], kv_ref[:, k_cols], kv_ref[:, v_cols], allowed)
            q_noisy = jnp.concatenate([q_ref[rows:, cols] for cols in pair], axis=0)
            num, den = terms(q_noisy, self_ref[:, k_cols], self_ref[:, v_cols], same)
            for number, cols in enumerate(pair):
                num_ref[rows:, cols] += num[number * rows : (number + 1) * rows]
                den_ref[rows:, cols] += den[number * rows : (number + 1) * rows]


def attention_kernel(info, q_ref, num_in, den_in, *refs, pieces, ends):
    count = len(pieces)
    num_ref, den_ref = refs[count : count + 2]
    width = q_ref.shape[1] // 2
    heads = width // HD
    for bit in sorted({offset.bit_length() for offset, _ in pieces}):
        group = [(which, ref) for (offset, which), ref in zip(pieces, refs) if offset.bit_length() == bit]

        @pl.when(jnp.bitwise_and(info[2], 1 << (bit - 1)) != 0)
        def _(group=group):
            for which in range(2):
                found = [ref[...] for one, ref in group if one == which]
                if found:
                    add_pieces(q_ref, num_ref, den_ref, head_base(info, which, width), heads, found)
            found = [ref for one, ref in group if one == 2]
            for kv_head in range(2 if found else 0):
                cols = slice(2 * kv_head * HD, 2 * (kv_head + 1) * HD)
                add_pieces(q_ref, num_ref, den_ref, kv_head * width, heads, [ref[:, cols] for ref in found])

    for which, out_ref in zip(ends, refs[count + 2 :]):
        base = head_base(info, which, width)
        for head in range(heads):
            cols = pl.ds(base + head * HD, HD)
            total = jnp.sum(den_ref[:, cols], axis=1, keepdims=True)
            out_ref[:, head * HD : (head + 1) * HD] = (num_ref[:, cols] / total).astype(BF16)


def out_first_kernel(info, ga, gb, ha, w_out, w_far, mixed_ref, *, tile):
    part = ga.shape[1]
    total = mixed_ref.shape[1]
    first = pl.ds(pl.multiple_of(info[0] * part, 128), part)
    second = pl.ds(pl.multiple_of((1 - info[0]) * part, 128), part)
    for start in range(0, total, tile):
        mine = pl.ds(pl.multiple_of(info[1] * total + start, 128), tile)
        cols = slice(start, start + tile)
        mixed = dot(ga[...], w_out[first, mine]) + dot(gb[...], w_out[second, mine])
        mixed_ref[:, cols] = mixed + dot(ha[...], w_far[first, cols])


def out_last_kernel(info, live, hb, mixed_ref, w_far, clean_out, noisy_out, clean_ref, noisy_ref, sems, *, tile):
    rows, total = clean_ref.shape
    part = hb.shape[1]
    second = pl.ds(pl.multiple_of((1 - info[0]) * part, 128), part)
    moves = []
    for start in range(0, total, tile):
        cols = slice(start, start + tile)
        mixed = mixed_ref[:, cols] + dot(hb[...], w_far[second, cols])
        clean_ref[:, cols] = mixed[:rows].astype(BF16)
        for block in range(rows // BLK):
            part_rows = mixed[rows + block * BLK : rows + (block + 1) * BLK]
            noisy_ref[block * BLK : (block + 1) * BLK, cols] = (part_rows * live[block].astype(F32)).astype(BF16)
        for source, target in ((clean_ref, clean_out), (noisy_ref, noisy_out)):
            moves.append(pltpu.make_async_copy(source.at[:, cols], target.at[:, cols], sems.at[len(moves)]))
            moves[-1].start()
    for move in moves:
        move.wait()


WHOLE = pl.BlockSpec(memory_space=pltpu.VMEM)
HBM = pl.BlockSpec(memory_space=pltpu.HBM)
HINT = 1


def call(kernel, scalars, ins, outs, arrays, flops, num_bytes, scratch=(), exps=0, grid=1, aliases=None, limit=20):
    return pl.pallas_call(
        kernel,
        grid_spec=pltpu.PrefetchScalarGridSpec(
            num_scalar_prefetch=len(scalars),
            grid=(grid,),
            in_specs=ins,
            out_specs=[spec for spec, _ in outs],
            scratch_shapes=list(scratch),
        ),
        out_shape=[shape for _, shape in outs],
        compiler_params=pltpu.CompilerParams(vmem_limit_bytes=limit << 20),
        cost_estimate=pl.CostEstimate(
            flops=flops // HINT, bytes_accessed=num_bytes // HINT, transcendentals=exps // HINT
        ),
        input_output_aliases=aliases or {},
    )(*scalars, *arrays)


def after(value, *others):
    return lax.optimization_barrier((value, *others))[0]


def on_device(
    mesh, clean_tokens, norm_gain, mask_embed, time_shift, w_query, w_key, w_value, w_out,
    q_gain, k_gain, masked, block_live, timesteps,
):
    rows, half = clean_tokens.shape
    heads_width = w_query.shape[1]
    kv_width = w_key.shape[1]
    part = heads_width // 2
    ctx = mesh.shape["ctx"]
    c, p, t = lax.axis_index("copy"), lax.axis_index("ctx"), lax.axis_index("tp")
    info = jnp.stack([c, t, p, timesteps[0]]).astype(jnp.int32)
    pair = [(0, 1), (1, 0)]
    cross_x = lambda v: lax.ppermute(v, "copy", pair)
    cross_core = lambda v: lax.ppermute(v, "tp", pair)
    shape = jax.ShapeDtypeStruct

    cut = rows // 2
    out_cols = w_out.shape[1] // 2
    qg, kg = q_gain[None], k_gain[None]
    vmem = lambda dims, kind: (WHOLE, pltpu.VMEM(dims, kind))
    in_hbm = lambda v: pltpu.with_memory_space_constraint(v, pltpu.HBM)

    x, mask, shift, squares, strip = call(
        squares_kernel, [], [HBM] * 3,
        [vmem((rows, half), BF16), vmem((1, rows), jnp.int32), vmem((1, 2 * half), F32), vmem((1, rows), F32),
         vmem((cut, half), BF16)],
        [in_hbm(clean_tokens), in_hbm(masked), in_hbm(time_shift[None])], 2 * rows * half, rows * half * 2,
        [pltpu.SemaphoreType.DMA((3,))],
    )
    other_squares = cross_x(squares)
    near = cross_x(strip)
    stats = [squares, other_squares, mask]
    vectors = [norm_gain[None], mask_embed[None], shift]
    buffers = [(half, heads_width), (half, kv_width), (half, kv_width)]
    per_row = heads_width + 2 * kv_width

    pq, pk, pv, *weights, w_send = call(
        own_half_kernel, [info], [WHOLE] * 7 + [HBM] * 4,
        [vmem((2 * rows, width), F32) for width in (heads_width, kv_width, kv_width)]
        + [vmem(dims, BF16) for dims in buffers] + [vmem((heads_width, out_cols), BF16)],
        [x] + stats + vectors + [in_hbm(w) for w in (w_query, w_key, w_value, w_out)],
        32 * rows * half * per_row, 2 * half * per_row * 2,
        [pltpu.VMEM(dims, BF16) for dims in buffers] + [pltpu.SemaphoreType.DMA((10,))], limit=32,
    )
    near = after(near, pk)
    far = cross_core(near)

    kv, kva = call(
        clean_kv_kernel, [info], [WHOLE] * 12,
        [vmem((rows, 2 * kv_width), BF16), vmem((rows, kv_width), BF16)],
        [near, far] + stats + vectors[:2] + weights[1:] + [pk, pv, kg],
        4 * rows * half * kv_width, half * 2 * kv_width * 2,
    )

    trade = lambda v, offset: lax.ppermute(v, "ctx", [(i, i ^ offset) for i in range(ctx)])
    offsets = list(range(2, ctx, 2))
    beside = trade(kv, 1)
    column = {offset: trade(kva, offset) for offset in offsets}
    w_far = cross_core(after(w_send, kv))
    near = after(near, kv)
    q, own = call(
        other_half_kernel, [info], [WHOLE] * 16,
        [vmem((2 * rows, heads_width), BF16), vmem((rows, 2 * kv_width), BF16)],
        [near, far] + stats + vectors + weights + [pq, pk, pv, qg, kg],
        4 * rows * half * per_row, half * per_row * 2,
    )

    acc = [vmem((2 * rows, heads_width), F32)] * 2
    unit = rows * rows * heads_width // HD
    cost = lambda units: (16 * HD * unit * units, 8 * unit, (), unit * units)
    in_place = {2: 0, 3: 1}
    num, den = call(attention_own_kernel, [info], [WHOLE] * 3, acc, [q, kv, own], *cost(3))
    first, later = offsets[0], offsets[1:]

    def attend(num, den, pieces, ends=()):
        return call(
            functools.partial(attention_kernel, pieces=tuple(key for key, _ in pieces), ends=ends), [info],
            [WHOLE] * (3 + len(pieces)), acc + [vmem((2 * rows, part), BF16)] * len(ends),
            [q, num, den] + [piece for _, piece in pieces], *cost(len(pieces)), aliases=in_place,
        )

    column[first] = after(column[first], num, w_far)
    over_x, over_y, corner = {}, {}, {}
    over_x[first], over_y[first] = cross_x(column[first]), trade(column[first], 1)
    num, den = attend(num, den, [((1, 2), beside), ((first, 0), column[first])])
    corner[first] = cross_x(over_y[first])
    for offset in later:
        column[offset] = after(column[offset], num)
        over_x[offset], over_y[offset] = cross_x(column[offset]), trade(column[offset], 1)
    num, den = attend(
        num, den,
        [((first, 1), over_x[first]), ((first, 0), over_y[first])] + [((o, 0), column[o]) for o in later],
    )
    for number, offset in enumerate(later):
        corner[offset] = trade(over_x[offset], 1) if number % 2 else cross_x(over_y[offset])
    num, den, ga = attend(
        num, den,
        [((first, 1), corner[first])]
        + [((o, 0), over_y[o]) for o in later] + [((o, 1), over_x[o]) for o in later], (0,),
    )
    ha = cross_core(ga)
    num, den, gb = attend(num, den, [((o, 1), corner[o]) for o in later], (1,))
    hb = cross_core(gb)

    tile = 512
    mixed, = call(
        functools.partial(out_first_kernel, tile=tile), [info], [WHOLE] * 5, [vmem((2 * rows, out_cols), F32)],
        [ga, gb, ha, w_out, w_far], 6 * rows * heads_width * out_cols, 2 * heads_width * out_cols * 2,
    )
    out = shape((rows, out_cols), BF16)
    clean_out, noised_out = call(
        functools.partial(out_last_kernel, tile=tile), [info, block_live[0]], [WHOLE] * 3, [(HBM, out), (HBM, out)],
        [hb, mixed, w_far], 2 * rows * heads_width * out_cols, heads_width * out_cols * 2,
        [pltpu.VMEM((rows, out_cols), BF16)] * 2 + [pltpu.SemaphoreType.DMA((2 * (out_cols // tile),))],
    )
    return (clean_out, noised_out[None])


def solution(mesh):
    in_specs = (
        P("ctx", "copy"),
        P(),
        P(),
        P(),
        P(None, "tp"),
        P(None, "tp"),
        P(None, "tp"),
        P("tp", None),
        P(),
        P(),
        P("copy", "ctx"),
        P("copy", "ctx"),
        P("copy"),
    )
    out_specs = (P("ctx", "tp"), P("copy", "ctx", "tp"))
    return jax.shard_map(
        functools.partial(on_device, mesh), mesh=mesh, in_specs=in_specs, out_specs=out_specs, check_vma=False
    )
```

```python
import functools
import math

import jax
import jax.numpy as jnp
from jax import lax
from jax.experimental import pallas as pl
from jax.experimental.pallas import tpu as pltpu
from jax.sharding import PartitionSpec as P

HD = 128
BLK = 64
TSTEPS = 1000
EPS = 1e-06
F32 = jnp.float32
BF16 = jnp.bfloat16
SCORE_SCALE = math.log2(math.e) / math.sqrt(HD)


def to_column(row, n):
    eye = lax.broadcasted_iota(jnp.int32, (n, n), 0) == lax.broadcasted_iota(jnp.int32, (n, n), 1)
    return jnp.sum(jnp.where(eye, jnp.broadcast_to(row, (n, n)), 0.0), axis=1, keepdims=True)


def row_scales(own_ref, other_ref, mask_ref, embed_ref, width):
    n = own_ref.shape[1]
    clean = lax.rsqrt(to_column(own_ref[...] + other_ref[...], n) * (1.0 / width) + EPS)
    embed = embed_ref[...].astype(F32)
    embed_scale = lax.rsqrt(jnp.sum(embed * embed, axis=1, keepdims=True) * (1.0 / width) + EPS)
    masked = to_column(mask_ref[...].astype(F32), n)
    return clean, embed_scale, masked


def normed_clean(x, clean_scale, gain):
    return (x * clean_scale * gain).astype(BF16)


def normed_noisy(x, clean_scale, embed_scale, masked, gain, embed, condition):
    is_masked = masked == 1.0
    noisy = jnp.where(is_masked, embed, x)
    scale = jnp.where(is_masked, embed_scale, clean_scale)
    return (noisy * scale * gain * condition).astype(BF16)


def dot(a, b):
    return jnp.dot(a, b, preferred_element_type=F32)


def head_norm(wide, gain):
    scale = lax.rsqrt(jnp.mean(wide * wide, axis=1, keepdims=True) + EPS)
    return (wide * scale * gain).astype(BF16)


def both_streams(x, scales, gain, embed, condition):
    clean = normed_clean(x, scales[0], gain)
    noisy = normed_noisy(x, scales[0], scales[1], scales[2], gain, embed, condition)
    return clean, noisy


def half_vectors(at, info, gain_ref, embed_ref, shift_ref):
    gain = gain_ref[:, at].astype(F32)
    embed = embed_ref[:, at].astype(F32)
    condition = 1.0 + info[3].astype(F32) / TSTEPS * shift_ref[:, at]
    return gain, embed, condition


def both_streams(x, scales, gain, embed, condition):
    clean = normed_clean(x, scales[0], gain)
    noisy = normed_noisy(x, scales[0], scales[1], scales[2], gain, embed, condition)
    return clean, noisy


def vectors_at(at, info, gain_ref, embed_ref, shift_ref):
    gain = gain_ref[:, at].astype(F32)
    embed = embed_ref[:, at].astype(F32)
    condition = 1.0 + info[3].astype(F32) / TSTEPS * shift_ref[:, at]
    return gain, embed, condition


def squares_kernel(x_hbm, mask_hbm, shift_hbm, x_ref, mask_ref, shift_ref, squares_ref, strip_ref, sems):
    moves = [
        pltpu.make_async_copy(source, target, sems.at[number])
        for number, (source, target) in enumerate(((x_hbm, x_ref), (mask_hbm, mask_ref), (shift_hbm, shift_ref)))
    ]
    for move in moves:
        move.start()
    for move in moves:
        move.wait()
    rows = x_ref.shape[0]
    x = x_ref[...].astype(F32)
    sums = jnp.sum(x * x, axis=1, keepdims=True)
    eye = lax.broadcasted_iota(jnp.int32, (rows, rows), 0) == lax.broadcasted_iota(jnp.int32, (rows, rows), 1)
    squares_ref[...] = jnp.sum(jnp.where(eye, jnp.broadcast_to(sums, (rows, rows)), 0.0), axis=0, keepdims=True)
    cut = strip_ref.shape[0]
    strip = pl.ds(pl.multiple_of(lax.axis_index("tp") * cut, 128), cut)
    strip_ref[...] = x_ref[strip]


def own_half_kernel(
    info, x_ref, own_ref, other_ref, mask_ref, gain_ref, embed_ref, shift_ref, wq, wk, wv, w_out,
    q_ref, k_ref, v_ref, rest_q, rest_k, rest_v, w_send, own_q, own_k, own_v, sems,
):
    half = x_ref.shape[1]
    depth = half // 2
    first = info[0] * half
    moves = []

    def move(source, target):
        moves.append(pltpu.make_async_copy(source, target, sems.at[len(moves)]))
        moves[-1].start()

    for chunk in range(2):
        there = pl.ds(pl.multiple_of(first + chunk * depth, 128), depth)
        here = pl.ds(chunk * depth, depth)
        for source, target in ((wk, own_k), (wv, own_v), (wq, own_q)):
            move(source.at[there], target.at[here])
    rest = pl.ds(pl.multiple_of(half - first, 128), half)
    for source, target in ((wk, rest_k), (wv, rest_v), (wq, rest_q)):
        move(source.at[rest], target)
    cols = w_send.shape[1]
    move(w_out.at[:, pl.ds(pl.multiple_of((1 - info[1]) * cols, 128), cols)], w_send)

    scales = row_scales(own_ref, other_ref, mask_ref, embed_ref, embed_ref.shape[1])
    at = pl.ds(pl.multiple_of(first, 128), half)
    gain, embed, condition = vectors_at(at, info, gain_ref, embed_ref, shift_ref)
    clean, noisy = both_streams(x_ref[...].astype(F32), scales, gain, embed, condition)
    both = jnp.concatenate([clean, noisy], axis=0)
    for chunk in range(2):
        here = slice(chunk * depth, (chunk + 1) * depth)
        for number, (target, weight) in enumerate(((k_ref, own_k), (v_ref, own_v), (q_ref, own_q))):
            moves[3 * chunk + number].wait()
            product = dot(both[:, here], weight[here])
            target[...] = product if chunk == 0 else target[...] + product
    for copy in moves[6:]:
        copy.wait()


def other_rows(info, near_ref, far_ref):
    near, far = near_ref[...].astype(F32), far_ref[...].astype(F32)
    first = info[1] == 0
    return jnp.concatenate([jnp.where(first, near, far), jnp.where(first, far, near)], axis=0)


def other_half(info, half):
    return pl.ds(pl.multiple_of((1 - info[0]) * half, 128), half)


def kv_out(ref, k, v, gain):
    for head in range(k.shape[1] // HD):
        cols = slice(head * HD, (head + 1) * HD)
        ref[:, 2 * head * HD : (2 * head + 1) * HD] = head_norm(k[:, cols], gain)
        ref[:, (2 * head + 1) * HD : 2 * (head + 1) * HD] = v[:, cols].astype(BF16)


def clean_kv_kernel(
    info, near_ref, far_ref, own_ref, other_ref, mask_ref, gain_ref, embed_ref,
    wk_ref, wv_ref, pk_ref, pv_ref, kgain_ref, all_ref, one_ref,
):
    rows = all_ref.shape[0]
    width = embed_ref.shape[1]
    clean_scale = row_scales(own_ref, other_ref, mask_ref, embed_ref, width)[0]
    at = other_half(info, near_ref.shape[1])
    clean = normed_clean(other_rows(info, near_ref, far_ref), clean_scale, gain_ref[:, at].astype(F32))
    k = pk_ref[:rows] + dot(clean, wk_ref[...])
    v = pv_ref[:rows] + dot(clean, wv_ref[...])
    kv_out(all_ref, k, v, kgain_ref[...])
    cols = one_ref.shape[1]
    one_ref[...] = all_ref[:, pl.ds(pl.multiple_of(info[0] * cols, 128), cols)]


def other_half_kernel(
    info, near_ref, far_ref, own_ref, other_ref, mask_ref, gain_ref, embed_ref, shift_ref,
    wq_ref, wk_ref, wv_ref, pq_ref, pk_ref, pv_ref, qgain_ref, kgain_ref, q_ref, self_ref,
):
    rows = self_ref.shape[0]
    width = embed_ref.shape[1]
    scales = row_scales(own_ref, other_ref, mask_ref, embed_ref, width)
    at = other_half(info, near_ref.shape[1])
    gain, embed, condition = vectors_at(at, info, gain_ref, embed_ref, shift_ref)
    clean, noisy = both_streams(other_rows(info, near_ref, far_ref), scales, gain, embed, condition)
    k = pk_ref[rows:] + dot(noisy, wk_ref[...])
    v = pv_ref[rows:] + dot(noisy, wv_ref[...])
    kv_out(self_ref, k, v, kgain_ref[...])
    q = pq_ref[...] + dot(jnp.concatenate([clean, noisy], axis=0), wq_ref[...])
    for head in range(q_ref.shape[1] // HD):
        cols = slice(head * HD, (head + 1) * HD)
        q_ref[:, cols] = head_norm(q[:, cols], qgain_ref[...])


def terms(q, k, v, mask):
    scores = lax.dot_general(q, k, (((1,), (1,)), ((), ())), preferred_element_type=F32)
    e = jnp.exp2(scores * SCORE_SCALE)
    if mask is not None:
        e = jnp.where(mask, e, 0.0)
    den = e[:, :HD]
    for start in range(HD, e.shape[1], HD):
        den = den + e[:, start : start + HD]
    return dot(e.astype(BF16), v), den


def add_pieces(q_ref, num_ref, den_ref, base, heads, pieces):
    k = jnp.concatenate([piece[:, :HD] for piece in pieces], axis=0)
    v = jnp.concatenate([piece[:, HD:] for piece in pieces], axis=0)
    for head in range(heads):
        cols = pl.ds(base + head * HD, HD)
        num, den = terms(q_ref[:, cols], k, v, None)
        num_ref[:, cols] += num
        den_ref[:, cols] += den


def head_base(info, which, width):
    return pl.multiple_of((info[0] if which == 0 else 1 - info[0]) * width, 128)


def attention_own_kernel(info, q_ref, kv_ref, self_ref, num_ref, den_ref):
    rows = kv_ref.shape[0]
    kv_heads = kv_ref.shape[1] // (2 * HD)
    group = q_ref.shape[1] // HD // kv_heads
    row = lax.broadcasted_iota(jnp.int32, (2 * rows, rows), 0)
    key_block = lax.broadcasted_iota(jnp.int32, (2 * rows, rows), 1) // BLK
    noisy = row >= rows
    row_block = jnp.where(noisy, row - rows, row) // BLK
    same = key_block == row_block
    allowed = jnp.logical_or(key_block < row_block, jnp.logical_and(same, jnp.logical_not(noisy)))
    for kv_head in range(kv_heads):
        k_cols = slice(2 * kv_head * HD, (2 * kv_head + 1) * HD)
        v_cols = slice((2 * kv_head + 1) * HD, 2 * (kv_head + 1) * HD)
        for head in range(kv_head * group, (kv_head + 1) * group, 2):
            pair = [slice(one * HD, (one + 1) * HD) for one in (head, head + 1)]
            for cols in pair:
                num_ref[:, cols], den_ref[:, cols] = terms(q_ref[:, cols], kv_ref[:, k_cols], kv_ref[:, v_cols], allowed)
            q_noisy = jnp.concatenate([q_ref[rows:, cols] for cols in pair], axis=0)
            num, den = terms(q_noisy, self_ref[:, k_cols], self_ref[:, v_cols], same)
            for number, cols in enumerate(pair):
                num_ref[rows:, cols] += num[number * rows : (number + 1) * rows]
                den_ref[rows:, cols] += den[number * rows : (number + 1) * rows]


def attention_kernel(info, q_ref, num_in, den_in, *refs, pieces):
    count = len(pieces)
    num_ref, den_ref = refs[count : count + 2]
    width = q_ref.shape[1] // 2
    heads = width // HD
    for bit in sorted({offset.bit_length() for offset, _ in pieces}):
        group = [(which, ref) for (offset, which), ref in zip(pieces, refs) if offset.bit_length() == bit]

        @pl.when(jnp.bitwise_and(info[2], 1 << (bit - 1)) != 0)
        def _(group=group):
            for which in range(2):
                found = [ref[...] for one, ref in group if one == which]
                if found:
                    add_pieces(q_ref, num_ref, den_ref, head_base(info, which, width), heads, found)
            found = [ref for one, ref in group if one == 2]
            for kv_head in range(2 if found else 0):
                cols = slice(2 * kv_head * HD, 2 * (kv_head + 1) * HD)
                add_pieces(q_ref, num_ref, den_ref, kv_head * width, heads, [ref[:, cols] for ref in found])

    for out_ref in refs[count + 2 :]:
        for start in range(0, q_ref.shape[1], HD):
            cols = slice(start, start + HD)
            total = jnp.sum(den_ref[:, cols], axis=1, keepdims=True)
            out_ref[:, cols] = (num_ref[:, cols] / total).astype(BF16)


def out_first_kernel(info, heads, w_out, mixed_ref, *, tile):
    total = mixed_ref.shape[1]
    for start in range(0, total, tile):
        mine = pl.ds(pl.multiple_of(info[1] * total + start, 128), tile)
        mixed_ref[:, start : start + tile] = dot(heads[...], w_out[:, mine])


def out_last_kernel(info, live, heads, mixed_ref, w_far, clean_out, noisy_out, clean_ref, noisy_ref, sems, *, tile):
    rows, total = clean_ref.shape
    moves = []
    for start in range(0, total, tile):
        cols = slice(start, start + tile)
        mixed = mixed_ref[:, cols] + dot(heads[...], w_far[:, cols])
        clean_ref[:, cols] = mixed[:rows].astype(BF16)
        for block in range(rows // BLK):
            part_rows = mixed[rows + block * BLK : rows + (block + 1) * BLK]
            noisy_ref[block * BLK : (block + 1) * BLK, cols] = (part_rows * live[block].astype(F32)).astype(BF16)
        for source, target in ((clean_ref, clean_out), (noisy_ref, noisy_out)):
            moves.append(pltpu.make_async_copy(source.at[:, cols], target.at[:, cols], sems.at[len(moves)]))
            moves[-1].start()
    for move in moves:
        move.wait()


WHOLE = pl.BlockSpec(memory_space=pltpu.VMEM)
HBM = pl.BlockSpec(memory_space=pltpu.HBM)
HINT = 1


def call(kernel, scalars, ins, outs, arrays, flops, num_bytes, scratch=(), exps=0, grid=1, aliases=None, limit=20):
    return pl.pallas_call(
        kernel,
        grid_spec=pltpu.PrefetchScalarGridSpec(
            num_scalar_prefetch=len(scalars),
            grid=(grid,),
            in_specs=ins,
            out_specs=[spec for spec, _ in outs],
            scratch_shapes=list(scratch),
        ),
        out_shape=[shape for _, shape in outs],
        compiler_params=pltpu.CompilerParams(vmem_limit_bytes=limit << 20),
        cost_estimate=pl.CostEstimate(
            flops=flops // HINT, bytes_accessed=num_bytes // HINT, transcendentals=exps // HINT
        ),
        input_output_aliases=aliases or {},
    )(*scalars, *arrays)


def after(value, *others):
    return lax.optimization_barrier((value, *others))[0]


def on_device(
    mesh, clean_tokens, norm_gain, mask_embed, time_shift, w_query, w_key, w_value, w_out,
    q_gain, k_gain, masked, block_live, timesteps,
):
    rows, half = clean_tokens.shape
    heads_width = w_query.shape[1]
    kv_width = w_key.shape[1]
    ctx = mesh.shape["ctx"]
    c, p, t = lax.axis_index("copy"), lax.axis_index("ctx"), lax.axis_index("tp")
    info = jnp.stack([c, t, p, timesteps[0]]).astype(jnp.int32)
    pair = [(0, 1), (1, 0)]
    cross_x = lambda v: lax.ppermute(v, "copy", pair)
    cross_core = lambda v: lax.ppermute(v, "tp", pair)
    shape = jax.ShapeDtypeStruct

    cut = rows // 2
    out_cols = w_out.shape[1] // 2
    qg, kg = q_gain[None], k_gain[None]
    vmem = lambda dims, kind: (WHOLE, pltpu.VMEM(dims, kind))
    in_hbm = lambda v: pltpu.with_memory_space_constraint(v, pltpu.HBM)

    x, mask, shift, squares, strip = call(
        squares_kernel, [], [HBM] * 3,
        [vmem((rows, half), BF16), vmem((1, rows), jnp.int32), vmem((1, 2 * half), F32), vmem((1, rows), F32),
         vmem((cut, half), BF16)],
        [in_hbm(clean_tokens), in_hbm(masked), in_hbm(time_shift[None])], 2 * rows * half, rows * half * 2,
        [pltpu.SemaphoreType.DMA((3,))],
    )
    other_squares = cross_x(squares)
    near = cross_x(strip)
    stats = [squares, other_squares, mask]
    vectors = [norm_gain[None], mask_embed[None], shift]
    buffers = [(half, heads_width), (half, kv_width), (half, kv_width)]
    per_row = heads_width + 2 * kv_width

    pq, pk, pv, *weights, w_send = call(
        own_half_kernel, [info], [WHOLE] * 7 + [HBM] * 4,
        [vmem((2 * rows, width), F32) for width in (heads_width, kv_width, kv_width)]
        + [vmem(dims, BF16) for dims in buffers] + [vmem((heads_width, out_cols), BF16)],
        [x] + stats + vectors + [in_hbm(w) for w in (w_query, w_key, w_value, w_out)],
        32 * rows * half * per_row, 2 * half * per_row * 2,
        [pltpu.VMEM(dims, BF16) for dims in buffers] + [pltpu.SemaphoreType.DMA((10,))], limit=32,
    )
    near = after(near, pk)
    far = cross_core(near)

    kv, kva = call(
        clean_kv_kernel, [info], [WHOLE] * 12,
        [vmem((rows, 2 * kv_width), BF16), vmem((rows, kv_width), BF16)],
        [near, far] + stats + vectors[:2] + weights[1:] + [pk, pv, kg],
        4 * rows * half * kv_width, half * 2 * kv_width * 2,
    )

    trade = lambda v, offset: lax.ppermute(v, "ctx", [(i, i ^ offset) for i in range(ctx)])
    later = list(range(4, ctx, 2))
    column = {offset: trade(kva, offset) for offset in later}
    left = trade(kv, 2)
    beside = trade(kv, 1)
    w_far = cross_core(after(w_send, kv))
    near = after(near, kv)
    q, own = call(
        other_half_kernel, [info], [WHOLE] * 16,
        [vmem((2 * rows, heads_width), BF16), vmem((rows, 2 * kv_width), BF16)],
        [near, far] + stats + vectors + weights + [pq, pk, pv, qg, kg],
        4 * rows * half * per_row, half * per_row * 2,
    )

    acc = [vmem((2 * rows, heads_width), F32)] * 2
    unit = rows * rows * heads_width // HD
    cost = lambda units: (16 * HD * unit * units, 8 * unit, (), unit * units)
    in_place = {2: 0, 3: 1}
    num, den = call(attention_own_kernel, [info], [WHOLE] * 3, acc, [q, kv, own], *cost(3))
    def attend(num, den, pieces, outs=()):
        return call(
            functools.partial(attention_kernel, pieces=tuple(key for key, _ in pieces)), [info],
            [WHOLE] * (3 + len(pieces)), acc + list(outs),
            [q, num, den] + [piece for _, piece in pieces], *cost(len(pieces)), aliases=in_place,
        )

    num, den = attend(num, den, [((1, 2), beside)])
    over_x, over_y = {}, {}
    left = after(left, num, w_far)
    for offset in later:
        column[offset] = after(column[offset], num)
        over_y[offset], over_x[offset] = trade(column[offset], 1), cross_x(column[offset])
    num, den = attend(num, den, [((2, 2), left)] + [((o, 0), column[o]) for o in later])
    right = trade(after(left, num), 1)
    over_y = {offset: after(piece, num) for offset, piece in over_y.items()}
    corner = {offset: cross_x(piece) for offset, piece in over_y.items()}
    pieces = [((o, 0), over_y[o]) for o in later] + [((o, 1), over_x[o]) for o in later]
    num, den = attend(num, den, pieces)
    num, den = attend(num, den, [((o, 1), corner[o]) for o in later])
    num, den, near_heads = attend(num, den, [((3, 2), right)], [vmem((2 * rows, heads_width), BF16)])
    far_heads = cross_core(near_heads)

    tile = 512
    half_cost = 4 * rows * heads_width * out_cols, heads_width * out_cols * 2
    mixed, = call(
        functools.partial(out_first_kernel, tile=tile), [info], [WHOLE] * 2, [vmem((2 * rows, out_cols), F32)],
        [near_heads, w_out], *half_cost,
    )
    out = shape((rows, out_cols), BF16)
    clean_out, noised_out = call(
        functools.partial(out_last_kernel, tile=tile), [info, block_live[0]], [WHOLE] * 3, [(HBM, out), (HBM, out)],
        [far_heads, mixed, w_far], *half_cost,
        [pltpu.VMEM((rows, out_cols), BF16)] * 2 + [pltpu.SemaphoreType.DMA((2 * (out_cols // tile),))],
    )
    return (clean_out, noised_out[None])


def solution(mesh):
    in_specs = (
        P("ctx", "copy"),
        P(),
        P(),
        P(),
        P(None, "tp"),
        P(None, "tp"),
        P(None, "tp"),
        P("tp", None),
        P(),
        P(),
        P("copy", "ctx"),
        P("copy", "ctx"),
        P("copy"),
    )
    out_specs = (P("ctx", "tp"), P("copy", "ctx", "tp"))
    return jax.shard_map(
        functools.partial(on_device, mesh), mesh=mesh, in_specs=in_specs, out_specs=out_specs, check_vma=False
    )
```

```python
import functools
import math

import jax
import jax.numpy as jnp
from jax import lax
from jax.experimental import pallas as pl
from jax.experimental.pallas import tpu as pltpu
from jax.sharding import PartitionSpec as P

HD = 128
BLK = 64
TSTEPS = 1000
EPS = 1e-06
F32 = jnp.float32
BF16 = jnp.bfloat16
SCORE_SCALE = math.log2(math.e) / math.sqrt(HD)


def to_column(row, n):
    eye = lax.broadcasted_iota(jnp.int32, (n, n), 0) == lax.broadcasted_iota(jnp.int32, (n, n), 1)
    return jnp.sum(jnp.where(eye, jnp.broadcast_to(row, (n, n)), 0.0), axis=1, keepdims=True)


def row_scales(own_ref, other_ref, mask_ref, embed_ref, width):
    n = own_ref.shape[1]
    clean = lax.rsqrt(to_column(own_ref[...] + other_ref[...], n) * (1.0 / width) + EPS)
    embed = embed_ref[...].astype(F32)
    embed_scale = lax.rsqrt(jnp.sum(embed * embed, axis=1, keepdims=True) * (1.0 / width) + EPS)
    masked = to_column(mask_ref[...].astype(F32), n)
    return clean, embed_scale, masked


def normed_clean(x, clean_scale, gain):
    return (x * clean_scale * gain).astype(BF16)


def normed_noisy(x, clean_scale, embed_scale, masked, gain, embed, condition):
    is_masked = masked == 1.0
    noisy = jnp.where(is_masked, embed, x)
    scale = jnp.where(is_masked, embed_scale, clean_scale)
    return (noisy * scale * gain * condition).astype(BF16)


def dot(a, b):
    return jnp.dot(a, b, preferred_element_type=F32)


def head_norm(wide, gain):
    scale = lax.rsqrt(jnp.mean(wide * wide, axis=1, keepdims=True) + EPS)
    return (wide * scale * gain).astype(BF16)


def both_streams(x, scales, gain, embed, condition):
    clean = normed_clean(x, scales[0], gain)
    noisy = normed_noisy(x, scales[0], scales[1], scales[2], gain, embed, condition)
    return clean, noisy


def half_vectors(at, info, gain_ref, embed_ref, shift_ref):
    gain = gain_ref[:, at].astype(F32)
    embed = embed_ref[:, at].astype(F32)
    condition = 1.0 + info[3].astype(F32) / TSTEPS * shift_ref[:, at]
    return gain, embed, condition


def both_streams(x, scales, gain, embed, condition):
    clean = normed_clean(x, scales[0], gain)
    noisy = normed_noisy(x, scales[0], scales[1], scales[2], gain, embed, condition)
    return clean, noisy


def vectors_at(at, info, gain_ref, embed_ref, shift_ref):
    gain = gain_ref[:, at].astype(F32)
    embed = embed_ref[:, at].astype(F32)
    condition = 1.0 + info[3].astype(F32) / TSTEPS * shift_ref[:, at]
    return gain, embed, condition


def squares_kernel(x_hbm, mask_hbm, shift_hbm, x_ref, mask_ref, shift_ref, squares_ref, strip_ref, sems):
    moves = [
        pltpu.make_async_copy(source, target, sems.at[number])
        for number, (source, target) in enumerate(((x_hbm, x_ref), (mask_hbm, mask_ref), (shift_hbm, shift_ref)))
    ]
    for move in moves:
        move.start()
    for move in moves:
        move.wait()
    rows = x_ref.shape[0]
    x = x_ref[...].astype(F32)
    sums = jnp.sum(x * x, axis=1, keepdims=True)
    eye = lax.broadcasted_iota(jnp.int32, (rows, rows), 0) == lax.broadcasted_iota(jnp.int32, (rows, rows), 1)
    squares_ref[...] = jnp.sum(jnp.where(eye, jnp.broadcast_to(sums, (rows, rows)), 0.0), axis=0, keepdims=True)
    cut = strip_ref.shape[0]
    strip = pl.ds(pl.multiple_of(lax.axis_index("tp") * cut, 128), cut)
    strip_ref[...] = x_ref[strip]


def own_half_kernel(
    info, x_ref, own_ref, other_ref, mask_ref, gain_ref, embed_ref, shift_ref, wq, wk, wv, w_out,
    q_ref, k_ref, v_ref, rest_q, rest_k, rest_v, w_send, own_q, own_k, own_v, sems,
):
    half = x_ref.shape[1]
    depth = half // 2
    first = info[0] * half
    moves = []

    def move(source, target):
        moves.append(pltpu.make_async_copy(source, target, sems.at[len(moves)]))
        moves[-1].start()

    for chunk in range(2):
        there = pl.ds(pl.multiple_of(first + chunk * depth, 128), depth)
        here = pl.ds(chunk * depth, depth)
        for source, target in ((wk, own_k), (wv, own_v), (wq, own_q)):
            move(source.at[there], target.at[here])
    rest = pl.ds(pl.multiple_of(half - first, 128), half)
    for source, target in ((wk, rest_k), (wv, rest_v), (wq, rest_q)):
        move(source.at[rest], target)
    cols = w_send.shape[1]
    move(w_out.at[:, pl.ds(pl.multiple_of((1 - info[1]) * cols, 128), cols)], w_send)

    scales = row_scales(own_ref, other_ref, mask_ref, embed_ref, embed_ref.shape[1])
    at = pl.ds(pl.multiple_of(first, 128), half)
    gain, embed, condition = vectors_at(at, info, gain_ref, embed_ref, shift_ref)
    clean, noisy = both_streams(x_ref[...].astype(F32), scales, gain, embed, condition)
    both = jnp.concatenate([clean, noisy], axis=0)
    for chunk in range(2):
        here = slice(chunk * depth, (chunk + 1) * depth)
        for number, (target, weight) in enumerate(((k_ref, own_k), (v_ref, own_v), (q_ref, own_q))):
            moves[3 * chunk + number].wait()
            product = dot(both[:, here], weight[here])
            target[...] = product if chunk == 0 else target[...] + product
    for copy in moves[6:]:
        copy.wait()


def other_rows(info, near_ref, far_ref):
    near, far = near_ref[...].astype(F32), far_ref[...].astype(F32)
    first = info[1] == 0
    return jnp.concatenate([jnp.where(first, near, far), jnp.where(first, far, near)], axis=0)


def other_half(info, half):
    return pl.ds(pl.multiple_of((1 - info[0]) * half, 128), half)


def kv_out(ref, k, v, gain):
    for head in range(k.shape[1] // HD):
        cols = slice(head * HD, (head + 1) * HD)
        ref[:, 2 * head * HD : (2 * head + 1) * HD] = head_norm(k[:, cols], gain)
        ref[:, (2 * head + 1) * HD : 2 * (head + 1) * HD] = v[:, cols].astype(BF16)


def clean_kv_kernel(
    info, near_ref, far_ref, own_ref, other_ref, mask_ref, gain_ref, embed_ref,
    wk_ref, wv_ref, pk_ref, pv_ref, kgain_ref, all_ref, one_ref,
):
    rows = all_ref.shape[0]
    width = embed_ref.shape[1]
    clean_scale = row_scales(own_ref, other_ref, mask_ref, embed_ref, width)[0]
    at = other_half(info, near_ref.shape[1])
    clean = normed_clean(other_rows(info, near_ref, far_ref), clean_scale, gain_ref[:, at].astype(F32))
    k = pk_ref[:rows] + dot(clean, wk_ref[...])
    v = pv_ref[:rows] + dot(clean, wv_ref[...])
    kv_out(all_ref, k, v, kgain_ref[...])
    cols = one_ref.shape[1]
    one_ref[...] = all_ref[:, pl.ds(pl.multiple_of(info[0] * cols, 128), cols)]


def other_half_kernel(
    info, near_ref, far_ref, own_ref, other_ref, mask_ref, gain_ref, embed_ref, shift_ref,
    wq_ref, wk_ref, wv_ref, pq_ref, pk_ref, pv_ref, qgain_ref, kgain_ref, q_ref, self_ref,
):
    rows = self_ref.shape[0]
    width = embed_ref.shape[1]
    scales = row_scales(own_ref, other_ref, mask_ref, embed_ref, width)
    at = other_half(info, near_ref.shape[1])
    gain, embed, condition = vectors_at(at, info, gain_ref, embed_ref, shift_ref)
    clean, noisy = both_streams(other_rows(info, near_ref, far_ref), scales, gain, embed, condition)
    k = pk_ref[rows:] + dot(noisy, wk_ref[...])
    v = pv_ref[rows:] + dot(noisy, wv_ref[...])
    kv_out(self_ref, k, v, kgain_ref[...])
    q = pq_ref[...] + dot(jnp.concatenate([clean, noisy], axis=0), wq_ref[...])
    for head in range(q_ref.shape[1] // HD):
        cols = slice(head * HD, (head + 1) * HD)
        q_ref[:, cols] = head_norm(q[:, cols], qgain_ref[...])


def terms(q, k, v, mask):
    scores = lax.dot_general(q, k, (((1,), (1,)), ((), ())), preferred_element_type=F32)
    e = jnp.exp2(scores * SCORE_SCALE)
    if mask is not None:
        e = jnp.where(mask, e, 0.0)
    den = e[:, :HD]
    for start in range(HD, e.shape[1], HD):
        den = den + e[:, start : start + HD]
    return dot(e.astype(BF16), v), den


def add_pieces(q_ref, num_ref, den_ref, base, heads, pieces):
    k = jnp.concatenate([piece[:, :HD] for piece in pieces], axis=0)
    v = jnp.concatenate([piece[:, HD:] for piece in pieces], axis=0)
    for head in range(heads):
        cols = pl.ds(base + head * HD, HD)
        num, den = terms(q_ref[:, cols], k, v, None)
        num_ref[:, cols] += num
        den_ref[:, cols] += den


def head_base(info, which, width):
    return pl.multiple_of((info[0] if which == 0 else 1 - info[0]) * width, 128)


def attention_own_kernel(info, q_ref, kv_ref, self_ref, num_ref, den_ref):
    rows = kv_ref.shape[0]
    kv_heads = kv_ref.shape[1] // (2 * HD)
    group = q_ref.shape[1] // HD // kv_heads
    row = lax.broadcasted_iota(jnp.int32, (2 * rows, rows), 0)
    key_block = lax.broadcasted_iota(jnp.int32, (2 * rows, rows), 1) // BLK
    noisy = row >= rows
    row_block = jnp.where(noisy, row - rows, row) // BLK
    same = key_block == row_block
    allowed = jnp.logical_or(key_block < row_block, jnp.logical_and(same, jnp.logical_not(noisy)))
    for kv_head in range(kv_heads):
        k_cols = slice(2 * kv_head * HD, (2 * kv_head + 1) * HD)
        v_cols = slice((2 * kv_head + 1) * HD, 2 * (kv_head + 1) * HD)
        for head in range(kv_head * group, (kv_head + 1) * group, 2):
            pair = [slice(one * HD, (one + 1) * HD) for one in (head, head + 1)]
            for cols in pair:
                num_ref[:, cols], den_ref[:, cols] = terms(q_ref[:, cols], kv_ref[:, k_cols], kv_ref[:, v_cols], allowed)
            q_noisy = jnp.concatenate([q_ref[rows:, cols] for cols in pair], axis=0)
            num, den = terms(q_noisy, self_ref[:, k_cols], self_ref[:, v_cols], same)
            for number, cols in enumerate(pair):
                num_ref[rows:, cols] += num[number * rows : (number + 1) * rows]
                den_ref[rows:, cols] += den[number * rows : (number + 1) * rows]


def attention_kernel(info, q_ref, num_in, den_in, *refs, pieces):
    count = len(pieces)
    num_ref, den_ref = refs[count : count + 2]
    width = q_ref.shape[1] // 2
    heads = width // HD
    for bit in sorted({offset.bit_length() for offset, _ in pieces}):
        group = [(which, ref) for (offset, which), ref in zip(pieces, refs) if offset.bit_length() == bit]

        @pl.when(jnp.bitwise_and(info[2], 1 << (bit - 1)) != 0)
        def _(group=group):
            for which in range(2):
                found = [ref[...] for one, ref in group if one == which]
                if found:
                    add_pieces(q_ref, num_ref, den_ref, head_base(info, which, width), heads, found)
            found = [ref for one, ref in group if one == 2]
            for kv_head in range(2 if found else 0):
                cols = slice(2 * kv_head * HD, 2 * (kv_head + 1) * HD)
                add_pieces(q_ref, num_ref, den_ref, kv_head * width, heads, [ref[:, cols] for ref in found])

    for out_ref in refs[count + 2 :]:
        for start in range(0, q_ref.shape[1], HD):
            cols = slice(start, start + HD)
            total = jnp.sum(den_ref[:, cols], axis=1, keepdims=True)
            out_ref[:, cols] = (num_ref[:, cols] / total).astype(BF16)


def out_first_kernel(info, heads, w_out, mixed_ref, *, tile):
    total = mixed_ref.shape[1]
    for start in range(0, total, tile):
        mine = pl.ds(pl.multiple_of(info[1] * total + start, 128), tile)
        mixed_ref[:, start : start + tile] = dot(heads[...], w_out[:, mine])


def out_last_kernel(info, live, heads, mixed_ref, w_far, clean_out, noisy_out, clean_ref, noisy_ref, sems, *, tile):
    rows, total = clean_ref.shape
    moves = []
    for start in range(0, total, tile):
        cols = slice(start, start + tile)
        mixed = mixed_ref[:, cols] + dot(heads[...], w_far[:, cols])
        clean_ref[:, cols] = mixed[:rows].astype(BF16)
        for block in range(rows // BLK):
            part_rows = mixed[rows + block * BLK : rows + (block + 1) * BLK]
            noisy_ref[block * BLK : (block + 1) * BLK, cols] = (part_rows * live[block].astype(F32)).astype(BF16)
        for source, target in ((clean_ref, clean_out), (noisy_ref, noisy_out)):
            moves.append(pltpu.make_async_copy(source.at[:, cols], target.at[:, cols], sems.at[len(moves)]))
            moves[-1].start()
    for move in moves:
        move.wait()


WHOLE = pl.BlockSpec(memory_space=pltpu.VMEM)
HBM = pl.BlockSpec(memory_space=pltpu.HBM)
HINT = 1


def call(kernel, scalars, ins, outs, arrays, flops, num_bytes, scratch=(), exps=0, grid=1, aliases=None, limit=20):
    return pl.pallas_call(
        kernel,
        grid_spec=pltpu.PrefetchScalarGridSpec(
            num_scalar_prefetch=len(scalars),
            grid=(grid,),
            in_specs=ins,
            out_specs=[spec for spec, _ in outs],
            scratch_shapes=list(scratch),
        ),
        out_shape=[shape for _, shape in outs],
        compiler_params=pltpu.CompilerParams(vmem_limit_bytes=limit << 20),
        cost_estimate=pl.CostEstimate(
            flops=flops // HINT, bytes_accessed=num_bytes // HINT, transcendentals=exps // HINT
        ),
        input_output_aliases=aliases or {},
    )(*scalars, *arrays)


def after(value, *others):
    return lax.optimization_barrier((value, *others))[0]


def on_device(
    mesh, clean_tokens, norm_gain, mask_embed, time_shift, w_query, w_key, w_value, w_out,
    q_gain, k_gain, masked, block_live, timesteps,
):
    rows, half = clean_tokens.shape
    heads_width = w_query.shape[1]
    kv_width = w_key.shape[1]
    ctx = mesh.shape["ctx"]
    c, p, t = lax.axis_index("copy"), lax.axis_index("ctx"), lax.axis_index("tp")
    info = jnp.stack([c, t, p, timesteps[0]]).astype(jnp.int32)
    pair = [(0, 1), (1, 0)]
    cross_x = lambda v: lax.ppermute(v, "copy", pair)
    cross_core = lambda v: lax.ppermute(v, "tp", pair)
    shape = jax.ShapeDtypeStruct

    cut = rows // 2
    out_cols = w_out.shape[1] // 2
    qg, kg = q_gain[None], k_gain[None]
    vmem = lambda dims, kind: (WHOLE, pltpu.VMEM(dims, kind))
    in_hbm = lambda v: pltpu.with_memory_space_constraint(v, pltpu.HBM)

    x, mask, shift, squares, strip = call(
        squares_kernel, [], [HBM] * 3,
        [vmem((rows, half), BF16), vmem((1, rows), jnp.int32), vmem((1, 2 * half), F32), vmem((1, rows), F32),
         vmem((cut, half), BF16)],
        [in_hbm(clean_tokens), in_hbm(masked), in_hbm(time_shift[None])], 2 * rows * half, rows * half * 2,
        [pltpu.SemaphoreType.DMA((3,))],
    )
    other_squares = cross_x(squares)
    near = cross_x(strip)
    stats = [squares, other_squares, mask]
    vectors = [norm_gain[None], mask_embed[None], shift]
    buffers = [(half, heads_width), (half, kv_width), (half, kv_width)]
    per_row = heads_width + 2 * kv_width

    pq, pk, pv, *weights, w_send = call(
        own_half_kernel, [info], [WHOLE] * 7 + [HBM] * 4,
        [vmem((2 * rows, width), F32) for width in (heads_width, kv_width, kv_width)]
        + [vmem(dims, BF16) for dims in buffers] + [vmem((heads_width, out_cols), BF16)],
        [x] + stats + vectors + [in_hbm(w) for w in (w_query, w_key, w_value, w_out)],
        32 * rows * half * per_row, 2 * half * per_row * 2,
        [pltpu.VMEM(dims, BF16) for dims in buffers] + [pltpu.SemaphoreType.DMA((10,))], limit=32,
    )
    near = after(near, pk)
    far = cross_core(near)

    kv, kva = call(
        clean_kv_kernel, [info], [WHOLE] * 12,
        [vmem((rows, 2 * kv_width), BF16), vmem((rows, kv_width), BF16)],
        [near, far] + stats + vectors[:2] + weights[1:] + [pk, pv, kg],
        4 * rows * half * kv_width, half * 2 * kv_width * 2,
    )

    trade = lambda v, offset: lax.ppermute(v, "ctx", [(i, i ^ offset) for i in range(ctx)])
    later = list(range(4, ctx, 2))
    early, late = later[: len(later) // 2], later[len(later) // 2 :]
    column = {offset: trade(kva, offset) for offset in early}
    left = trade(kv, 2)
    beside = trade(kv, 1)
    w_far = cross_core(after(w_send, kv))
    near = after(near, kv)
    q, own = call(
        other_half_kernel, [info], [WHOLE] * 16,
        [vmem((2 * rows, heads_width), BF16), vmem((rows, 2 * kv_width), BF16)],
        [near, far] + stats + vectors + weights + [pq, pk, pv, qg, kg],
        4 * rows * half * per_row, half * per_row * 2,
    )

    column.update({offset: trade(after(kva, q), offset) for offset in late})
    acc = [vmem((2 * rows, heads_width), F32)] * 2
    unit = rows * rows * heads_width // HD
    cost = lambda units: (16 * HD * unit * units, 8 * unit, (), unit * units)
    in_place = {2: 0, 3: 1}
    num, den = call(attention_own_kernel, [info], [WHOLE] * 3, acc, [q, kv, own], *cost(3))
    def attend(num, den, pieces, outs=()):
        return call(
            functools.partial(attention_kernel, pieces=tuple(key for key, _ in pieces)), [info],
            [WHOLE] * (3 + len(pieces)), acc + list(outs),
            [q, num, den] + [piece for _, piece in pieces], *cost(len(pieces)), aliases=in_place,
        )

    over_x, over_y, corner = {}, {}, {}

    def turn(offsets, done):
        for offset in offsets:
            column[offset] = after(column[offset], done)
            over_y[offset], over_x[offset] = trade(column[offset], 1), cross_x(column[offset])

    turn(early, num)
    num, den = attend(num, den, [((1, 2), beside)] + [((o, 0), column[o]) for o in early])
    right = trade(after(left, num), 1)
    corner.update({o: cross_x(after(over_y[o], num)) for o in early})
    turn(late, num)
    num, den = attend(
        num, den,
        [((2, 2), left)] + [((o, 0), column[o]) for o in late]
        + [((o, 0), over_y[o]) for o in early] + [((o, 1), over_x[o]) for o in early],
    )
    corner.update({o: cross_x(after(over_y[o], num)) for o in late})
    num, den = attend(
        num, den,
        [((3, 2), right)] + [((o, 0), over_y[o]) for o in late]
        + [((o, 1), over_x[o]) for o in late] + [((o, 1), corner[o]) for o in early],
    )
    num, den, near_heads = attend(
        num, den, [((o, 1), corner[o]) for o in late], [vmem((2 * rows, heads_width), BF16)]
    )
    far_heads = cross_core(near_heads)

    tile = 512
    half_cost = 4 * rows * heads_width * out_cols, heads_width * out_cols * 2
    mixed, = call(
        functools.partial(out_first_kernel, tile=tile), [info], [WHOLE] * 2, [vmem((2 * rows, out_cols), F32)],
        [near_heads, w_out], *half_cost,
    )
    out = shape((rows, out_cols), BF16)
    clean_out, noised_out = call(
        functools.partial(out_last_kernel, tile=tile), [info, block_live[0]], [WHOLE] * 3, [(HBM, out), (HBM, out)],
        [far_heads, mixed, w_far], *half_cost,
        [pltpu.VMEM((rows, out_cols), BF16)] * 2 + [pltpu.SemaphoreType.DMA((2 * (out_cols // tile),))],
    )
    return (clean_out, noised_out[None])


def solution(mesh):
    in_specs = (
        P("ctx", "copy"),
        P(),
        P(),
        P(),
        P(None, "tp"),
        P(None, "tp"),
        P(None, "tp"),
        P("tp", None),
        P(),
        P(),
        P("copy", "ctx"),
        P("copy", "ctx"),
        P("copy"),
    )
    out_specs = (P("ctx", "tp"), P("copy", "ctx", "tp"))
    return jax.shard_map(
        functools.partial(on_device, mesh), mesh=mesh, in_specs=in_specs, out_specs=out_specs, check_vma=False
    )
```

```python
import functools
import math

import jax
import jax.numpy as jnp
from jax import lax
from jax.experimental import pallas as pl
from jax.experimental.pallas import tpu as pltpu
from jax.sharding import PartitionSpec as P

HD = 128
BLK = 64
TSTEPS = 1000
EPS = 1e-06
F32 = jnp.float32
BF16 = jnp.bfloat16
SCORE_SCALE = math.log2(math.e) / math.sqrt(HD)


def to_column(row, n):
    eye = lax.broadcasted_iota(jnp.int32, (n, n), 0) == lax.broadcasted_iota(jnp.int32, (n, n), 1)
    return jnp.sum(jnp.where(eye, jnp.broadcast_to(row, (n, n)), 0.0), axis=1, keepdims=True)


def row_scales(own_ref, other_ref, mask_ref, embed_ref, width):
    n = own_ref.shape[1]
    clean = lax.rsqrt(to_column(own_ref[...] + other_ref[...], n) * (1.0 / width) + EPS)
    embed = embed_ref[...].astype(F32)
    embed_scale = lax.rsqrt(jnp.sum(embed * embed, axis=1, keepdims=True) * (1.0 / width) + EPS)
    masked = to_column(mask_ref[...].astype(F32), n)
    return clean, embed_scale, masked


def normed_clean(x, clean_scale, gain):
    return (x * clean_scale * gain).astype(BF16)


def normed_noisy(x, clean_scale, embed_scale, masked, gain, embed, condition):
    is_masked = masked == 1.0
    noisy = jnp.where(is_masked, embed, x)
    scale = jnp.where(is_masked, embed_scale, clean_scale)
    return (noisy * scale * gain * condition).astype(BF16)


def dot(a, b):
    return jnp.dot(a, b, preferred_element_type=F32)


def head_norm(wide, gain):
    scale = lax.rsqrt(jnp.mean(wide * wide, axis=1, keepdims=True) + EPS)
    return (wide * scale * gain).astype(BF16)


def both_streams(x, scales, gain, embed, condition):
    clean = normed_clean(x, scales[0], gain)
    noisy = normed_noisy(x, scales[0], scales[1], scales[2], gain, embed, condition)
    return clean, noisy


def half_vectors(at, info, gain_ref, embed_ref, shift_ref):
    gain = gain_ref[:, at].astype(F32)
    embed = embed_ref[:, at].astype(F32)
    condition = 1.0 + info[3].astype(F32) / TSTEPS * shift_ref[:, at]
    return gain, embed, condition


def both_streams(x, scales, gain, embed, condition):
    clean = normed_clean(x, scales[0], gain)
    noisy = normed_noisy(x, scales[0], scales[1], scales[2], gain, embed, condition)
    return clean, noisy


def vectors_at(at, info, gain_ref, embed_ref, shift_ref):
    gain = gain_ref[:, at].astype(F32)
    embed = embed_ref[:, at].astype(F32)
    condition = 1.0 + info[3].astype(F32) / TSTEPS * shift_ref[:, at]
    return gain, embed, condition


def squares_kernel(x_hbm, mask_hbm, shift_hbm, x_ref, mask_ref, shift_ref, squares_ref, strip_ref, sems):
    moves = [
        pltpu.make_async_copy(source, target, sems.at[number])
        for number, (source, target) in enumerate(((x_hbm, x_ref), (mask_hbm, mask_ref), (shift_hbm, shift_ref)))
    ]
    for move in moves:
        move.start()
    for move in moves:
        move.wait()
    rows = x_ref.shape[0]
    x = x_ref[...].astype(F32)
    sums = jnp.sum(x * x, axis=1, keepdims=True)
    eye = lax.broadcasted_iota(jnp.int32, (rows, rows), 0) == lax.broadcasted_iota(jnp.int32, (rows, rows), 1)
    squares_ref[...] = jnp.sum(jnp.where(eye, jnp.broadcast_to(sums, (rows, rows)), 0.0), axis=0, keepdims=True)
    cut = strip_ref.shape[0]
    strip = pl.ds(pl.multiple_of(lax.axis_index("tp") * cut, 128), cut)
    strip_ref[...] = x_ref[strip]


def own_half_kernel(
    info, x_ref, own_ref, other_ref, mask_ref, gain_ref, embed_ref, shift_ref, wq, wk, wv, w_out,
    q_ref, k_ref, v_ref, rest_q, rest_k, rest_v, w_send, own_q, own_k, own_v, sems,
):
    half = x_ref.shape[1]
    depth = half // 2
    first = info[0] * half
    moves = []

    def move(source, target):
        moves.append(pltpu.make_async_copy(source, target, sems.at[len(moves)]))
        moves[-1].start()

    for chunk in range(2):
        there = pl.ds(pl.multiple_of(first + chunk * depth, 128), depth)
        here = pl.ds(chunk * depth, depth)
        for source, target in ((wk, own_k), (wv, own_v), (wq, own_q)):
            move(source.at[there], target.at[here])
    rest = pl.ds(pl.multiple_of(half - first, 128), half)
    for source, target in ((wk, rest_k), (wv, rest_v), (wq, rest_q)):
        move(source.at[rest], target)
    cols = w_send.shape[1]
    move(w_out.at[:, pl.ds(pl.multiple_of((1 - info[1]) * cols, 128), cols)], w_send)

    scales = row_scales(own_ref, other_ref, mask_ref, embed_ref, embed_ref.shape[1])
    at = pl.ds(pl.multiple_of(first, 128), half)
    gain, embed, condition = vectors_at(at, info, gain_ref, embed_ref, shift_ref)
    clean, noisy = both_streams(x_ref[...].astype(F32), scales, gain, embed, condition)
    both = jnp.concatenate([clean, noisy], axis=0)
    for chunk in range(2):
        here = slice(chunk * depth, (chunk + 1) * depth)
        for number, (target, weight) in enumerate(((k_ref, own_k), (v_ref, own_v), (q_ref, own_q))):
            moves[3 * chunk + number].wait()
            product = dot(both[:, here], weight[here])
            target[...] = product if chunk == 0 else target[...] + product
    for copy in moves[6:]:
        copy.wait()


def other_rows(info, near_ref, far_ref):
    near, far = near_ref[...].astype(F32), far_ref[...].astype(F32)
    first = info[1] == 0
    return jnp.concatenate([jnp.where(first, near, far), jnp.where(first, far, near)], axis=0)


def other_half(info, half):
    return pl.ds(pl.multiple_of((1 - info[0]) * half, 128), half)


def kv_out(ref, k, v, gain):
    for head in range(k.shape[1] // HD):
        cols = slice(head * HD, (head + 1) * HD)
        ref[:, 2 * head * HD : (2 * head + 1) * HD] = head_norm(k[:, cols], gain)
        ref[:, (2 * head + 1) * HD : 2 * (head + 1) * HD] = v[:, cols].astype(BF16)


def clean_kv_kernel(
    info, near_ref, far_ref, own_ref, other_ref, mask_ref, gain_ref, embed_ref,
    wk_ref, wv_ref, pk_ref, pv_ref, kgain_ref, all_ref, one_ref,
):
    rows = all_ref.shape[0]
    width = embed_ref.shape[1]
    clean_scale = row_scales(own_ref, other_ref, mask_ref, embed_ref, width)[0]
    at = other_half(info, near_ref.shape[1])
    clean = normed_clean(other_rows(info, near_ref, far_ref), clean_scale, gain_ref[:, at].astype(F32))
    k = pk_ref[:rows] + dot(clean, wk_ref[...])
    v = pv_ref[:rows] + dot(clean, wv_ref[...])
    kv_out(all_ref, k, v, kgain_ref[...])
    cols = one_ref.shape[1]
    one_ref[...] = all_ref[:, pl.ds(pl.multiple_of(info[0] * cols, 128), cols)]


def other_half_kernel(
    info, near_ref, far_ref, own_ref, other_ref, mask_ref, gain_ref, embed_ref, shift_ref,
    wq_ref, wk_ref, wv_ref, pq_ref, pk_ref, pv_ref, qgain_ref, kgain_ref, q_ref, self_ref,
):
    rows = self_ref.shape[0]
    width = embed_ref.shape[1]
    scales = row_scales(own_ref, other_ref, mask_ref, embed_ref, width)
    at = other_half(info, near_ref.shape[1])
    gain, embed, condition = vectors_at(at, info, gain_ref, embed_ref, shift_ref)
    clean, noisy = both_streams(other_rows(info, near_ref, far_ref), scales, gain, embed, condition)
    k = pk_ref[rows:] + dot(noisy, wk_ref[...])
    v = pv_ref[rows:] + dot(noisy, wv_ref[...])
    kv_out(self_ref, k, v, kgain_ref[...])
    q = pq_ref[...] + dot(jnp.concatenate([clean, noisy], axis=0), wq_ref[...])
    for head in range(q_ref.shape[1] // HD):
        cols = slice(head * HD, (head + 1) * HD)
        q_ref[:, cols] = head_norm(q[:, cols], qgain_ref[...])


def terms(q, k, v, mask):
    scores = lax.dot_general(q, k, (((1,), (1,)), ((), ())), preferred_element_type=F32)
    e = jnp.exp2(scores * SCORE_SCALE)
    if mask is not None:
        e = jnp.where(mask, e, 0.0)
    den = e[:, :HD]
    for start in range(HD, e.shape[1], HD):
        den = den + e[:, start : start + HD]
    return dot(e.astype(BF16), v), den


def add_pieces(q_ref, num_ref, den_ref, base, heads, pieces):
    k = jnp.concatenate([piece[:, :HD] for piece in pieces], axis=0)
    v = jnp.concatenate([piece[:, HD:] for piece in pieces], axis=0)
    for head in range(heads):
        cols = pl.ds(base + head * HD, HD)
        num, den = terms(q_ref[:, cols], k, v, None)
        num_ref[:, cols] += num
        den_ref[:, cols] += den


def head_base(info, which, width):
    return pl.multiple_of((info[0] if which == 0 else 1 - info[0]) * width, 128)


def attention_own_kernel(info, q_ref, kv_ref, self_ref, num_ref, den_ref):
    rows = kv_ref.shape[0]
    kv_heads = kv_ref.shape[1] // (2 * HD)
    group = q_ref.shape[1] // HD // kv_heads
    row = lax.broadcasted_iota(jnp.int32, (2 * rows, rows), 0)
    key_block = lax.broadcasted_iota(jnp.int32, (2 * rows, rows), 1) // BLK
    noisy = row >= rows
    row_block = jnp.where(noisy, row - rows, row) // BLK
    same = key_block == row_block
    allowed = jnp.logical_or(key_block < row_block, jnp.logical_and(same, jnp.logical_not(noisy)))
    for kv_head in range(kv_heads):
        k_cols = slice(2 * kv_head * HD, (2 * kv_head + 1) * HD)
        v_cols = slice((2 * kv_head + 1) * HD, 2 * (kv_head + 1) * HD)
        for head in range(kv_head * group, (kv_head + 1) * group, 2):
            pair = [slice(one * HD, (one + 1) * HD) for one in (head, head + 1)]
            for cols in pair:
                num_ref[:, cols], den_ref[:, cols] = terms(q_ref[:, cols], kv_ref[:, k_cols], kv_ref[:, v_cols], allowed)
            q_noisy = jnp.concatenate([q_ref[rows:, cols] for cols in pair], axis=0)
            num, den = terms(q_noisy, self_ref[:, k_cols], self_ref[:, v_cols], same)
            for number, cols in enumerate(pair):
                num_ref[rows:, cols] += num[number * rows : (number + 1) * rows]
                den_ref[rows:, cols] += den[number * rows : (number + 1) * rows]


def attention_kernel(info, q_ref, num_in, den_in, *refs, pieces):
    count = len(pieces)
    num_ref, den_ref = refs[count : count + 2]
    width = q_ref.shape[1] // 2
    heads = width // HD
    for bit in sorted({offset.bit_length() for offset, _ in pieces}):
        group = [(which, ref) for (offset, which), ref in zip(pieces, refs) if offset.bit_length() == bit]

        @pl.when(jnp.bitwise_and(info[2], 1 << (bit - 1)) != 0)
        def _(group=group):
            for which in range(2):
                found = [ref[...] for one, ref in group if one == which]
                if found:
                    add_pieces(q_ref, num_ref, den_ref, head_base(info, which, width), heads, found)
            found = [ref for one, ref in group if one == 2]
            for kv_head in range(2 if found else 0):
                cols = slice(2 * kv_head * HD, 2 * (kv_head + 1) * HD)
                add_pieces(q_ref, num_ref, den_ref, kv_head * width, heads, [ref[:, cols] for ref in found])

    for out_ref in refs[count + 2 :]:
        for start in range(0, q_ref.shape[1], HD):
            cols = slice(start, start + HD)
            total = jnp.sum(den_ref[:, cols], axis=1, keepdims=True)
            out_ref[:, cols] = (num_ref[:, cols] / total).astype(BF16)


def out_first_kernel(info, heads, w_out, mixed_ref, *, tile):
    total = mixed_ref.shape[1]
    for start in range(0, total, tile):
        mine = pl.ds(pl.multiple_of(info[1] * total + start, 128), tile)
        mixed_ref[:, start : start + tile] = dot(heads[...], w_out[:, mine])


def out_last_kernel(info, live, heads, mixed_ref, w_far, clean_out, noisy_out, clean_ref, noisy_ref, sems, *, tile):
    rows, total = clean_ref.shape
    moves = []
    for start in range(0, total, tile):
        cols = slice(start, start + tile)
        mixed = mixed_ref[:, cols] + dot(heads[...], w_far[:, cols])
        clean_ref[:, cols] = mixed[:rows].astype(BF16)
        for block in range(rows // BLK):
            part_rows = mixed[rows + block * BLK : rows + (block + 1) * BLK]
            noisy_ref[block * BLK : (block + 1) * BLK, cols] = (part_rows * live[block].astype(F32)).astype(BF16)
        for source, target in ((clean_ref, clean_out), (noisy_ref, noisy_out)):
            moves.append(pltpu.make_async_copy(source.at[:, cols], target.at[:, cols], sems.at[len(moves)]))
            moves[-1].start()
    for move in moves:
        move.wait()


WHOLE = pl.BlockSpec(memory_space=pltpu.VMEM)
HBM = pl.BlockSpec(memory_space=pltpu.HBM)
HINT = 1


def call(kernel, scalars, ins, outs, arrays, flops, num_bytes, scratch=(), exps=0, grid=1, aliases=None, limit=20):
    return pl.pallas_call(
        kernel,
        grid_spec=pltpu.PrefetchScalarGridSpec(
            num_scalar_prefetch=len(scalars),
            grid=(grid,),
            in_specs=ins,
            out_specs=[spec for spec, _ in outs],
            scratch_shapes=list(scratch),
        ),
        out_shape=[shape for _, shape in outs],
        compiler_params=pltpu.CompilerParams(vmem_limit_bytes=limit << 20),
        cost_estimate=pl.CostEstimate(
            flops=flops // HINT, bytes_accessed=num_bytes // HINT, transcendentals=exps // HINT
        ),
        input_output_aliases=aliases or {},
    )(*scalars, *arrays)


def after(value, *others):
    return lax.optimization_barrier((value, *others))[0]


def on_device(
    mesh, clean_tokens, norm_gain, mask_embed, time_shift, w_query, w_key, w_value, w_out,
    q_gain, k_gain, masked, block_live, timesteps,
):
    rows, half = clean_tokens.shape
    heads_width = w_query.shape[1]
    kv_width = w_key.shape[1]
    ctx = mesh.shape["ctx"]
    c, p, t = lax.axis_index("copy"), lax.axis_index("ctx"), lax.axis_index("tp")
    info = jnp.stack([c, t, p, timesteps[0]]).astype(jnp.int32)
    pair = [(0, 1), (1, 0)]
    cross_x = lambda v: lax.ppermute(v, "copy", pair)
    cross_core = lambda v: lax.ppermute(v, "tp", pair)
    shape = jax.ShapeDtypeStruct

    cut = rows // 2
    out_cols = w_out.shape[1] // 2
    qg, kg = q_gain[None], k_gain[None]
    vmem = lambda dims, kind: (WHOLE, pltpu.VMEM(dims, kind))
    in_hbm = lambda v: pltpu.with_memory_space_constraint(v, pltpu.HBM)

    x, mask, shift, squares, strip = call(
        squares_kernel, [], [HBM] * 3,
        [vmem((rows, half), BF16), vmem((1, rows), jnp.int32), vmem((1, 2 * half), F32), vmem((1, rows), F32),
         vmem((cut, half), BF16)],
        [in_hbm(clean_tokens), in_hbm(masked), in_hbm(time_shift[None])], 2 * rows * half, rows * half * 2,
        [pltpu.SemaphoreType.DMA((3,))],
    )
    other_squares = cross_x(squares)
    near = cross_x(strip)
    stats = [squares, other_squares, mask]
    vectors = [norm_gain[None], mask_embed[None], shift]
    buffers = [(half, heads_width), (half, kv_width), (half, kv_width)]
    per_row = heads_width + 2 * kv_width

    pq, pk, pv, *weights, w_send = call(
        own_half_kernel, [info], [WHOLE] * 7 + [HBM] * 4,
        [vmem((2 * rows, width), F32) for width in (heads_width, kv_width, kv_width)]
        + [vmem(dims, BF16) for dims in buffers] + [vmem((heads_width, out_cols), BF16)],
        [x] + stats + vectors + [in_hbm(w) for w in (w_query, w_key, w_value, w_out)],
        32 * rows * half * per_row, 2 * half * per_row * 2,
        [pltpu.VMEM(dims, BF16) for dims in buffers] + [pltpu.SemaphoreType.DMA((10,))], limit=32,
    )
    near = after(near, pk)
    far = cross_core(near)

    kv, kva = call(
        clean_kv_kernel, [info], [WHOLE] * 12,
        [vmem((rows, 2 * kv_width), BF16), vmem((rows, kv_width), BF16)],
        [near, far] + stats + vectors[:2] + weights[1:] + [pk, pv, kg],
        4 * rows * half * kv_width, half * 2 * kv_width * 2,
    )

    trade = lambda v, offset: lax.ppermute(v, "ctx", [(i, i ^ offset) for i in range(ctx)])
    later = list(range(4, ctx, 2))
    early, late = later[: len(later) // 2], later[len(later) // 2 :]
    column = {offset: trade(kva, offset) for offset in early}
    left = trade(kv, 2)
    beside = trade(kv, 1)
    w_far = cross_core(after(w_send, kv))
    near = after(near, kv)
    q, own = call(
        other_half_kernel, [info], [WHOLE] * 16,
        [vmem((2 * rows, heads_width), BF16), vmem((rows, 2 * kv_width), BF16)],
        [near, far] + stats + vectors + weights + [pq, pk, pv, qg, kg],
        4 * rows * half * per_row, half * per_row * 2,
    )

    column.update({offset: trade(after(kva, q), offset) for offset in late})
    acc = [vmem((2 * rows, heads_width), F32)] * 2
    unit = rows * rows * heads_width // HD
    cost = lambda units: (16 * HD * unit * units, 8 * unit, (), unit * units)
    in_place = {2: 0, 3: 1}
    num, den = call(attention_own_kernel, [info], [WHOLE] * 3, acc, [q, kv, own], *cost(3))
    def attend(num, den, pieces, outs=()):
        return call(
            functools.partial(attention_kernel, pieces=tuple(key for key, _ in pieces)), [info],
            [WHOLE] * (3 + len(pieces)), acc + list(outs),
            [q, num, den] + [piece for _, piece in pieces], *cost(len(pieces)), aliases=in_place,
        )

    over_x, over_y, corner = {}, {}, {}

    def turn(offsets, done):
        for offset in offsets:
            column[offset] = after(column[offset], done)
            over_y[offset], over_x[offset] = trade(column[offset], 1), cross_x(column[offset])

    turn(early, num)
    num, den = attend(num, den, [((1, 2), beside)])
    right = trade(after(left, num), 1)
    corner.update({o: cross_x(after(over_y[o], num)) for o in early})
    turn(late, num)
    num, den = attend(
        num, den,
        [((2, 2), left)] + [((o, 0), column[o]) for o in later]
        + [((o, 0), over_y[o]) for o in early] + [((o, 1), over_x[o]) for o in early],
    )
    corner.update({o: cross_x(after(over_y[o], num)) for o in late})
    num, den = attend(
        num, den,
        [((3, 2), right)] + [((o, 0), over_y[o]) for o in late]
        + [((o, 1), over_x[o]) for o in late] + [((o, 1), corner[o]) for o in early],
    )
    num, den, near_heads = attend(
        num, den, [((o, 1), corner[o]) for o in late], [vmem((2 * rows, heads_width), BF16)]
    )
    far_heads = cross_core(near_heads)

    tile = 512
    half_cost = 4 * rows * heads_width * out_cols, heads_width * out_cols * 2
    mixed, = call(
        functools.partial(out_first_kernel, tile=tile), [info], [WHOLE] * 2, [vmem((2 * rows, out_cols), F32)],
        [near_heads, w_out], *half_cost,
    )
    out = shape((rows, out_cols), BF16)
    clean_out, noised_out = call(
        functools.partial(out_last_kernel, tile=tile), [info, block_live[0]], [WHOLE] * 3, [(HBM, out), (HBM, out)],
        [far_heads, mixed, w_far], *half_cost,
        [pltpu.VMEM((rows, out_cols), BF16)] * 2 + [pltpu.SemaphoreType.DMA((2 * (out_cols // tile),))],
    )
    return (clean_out, noised_out[None])


def solution(mesh):
    in_specs = (
        P("ctx", "copy"),
        P(),
        P(),
        P(),
        P(None, "tp"),
        P(None, "tp"),
        P(None, "tp"),
        P("tp", None),
        P(),
        P(),
        P("copy", "ctx"),
        P("copy", "ctx"),
        P("copy"),
    )
    out_specs = (P("ctx", "tp"), P("copy", "ctx", "tp"))
    return jax.shard_map(
        functools.partial(on_device, mesh), mesh=mesh, in_specs=in_specs, out_specs=out_specs, check_vma=False
    )
```

```python
import functools
import math

import jax
import jax.numpy as jnp
from jax import lax
from jax.experimental import pallas as pl
from jax.experimental.pallas import tpu as pltpu
from jax.sharding import PartitionSpec as P

HD = 128
BLK = 64
TSTEPS = 1000
EPS = 1e-06
F32 = jnp.float32
BF16 = jnp.bfloat16
SCORE_SCALE = math.log2(math.e) / math.sqrt(HD)


def to_column(row, n):
    eye = lax.broadcasted_iota(jnp.int32, (n, n), 0) == lax.broadcasted_iota(jnp.int32, (n, n), 1)
    return jnp.sum(jnp.where(eye, jnp.broadcast_to(row, (n, n)), 0.0), axis=1, keepdims=True)


def row_scales(own_ref, other_ref, mask_ref, embed_ref, width):
    n = own_ref.shape[1]
    clean = lax.rsqrt(to_column(own_ref[...] + other_ref[...], n) * (1.0 / width) + EPS)
    embed = embed_ref[...].astype(F32)
    embed_scale = lax.rsqrt(jnp.sum(embed * embed, axis=1, keepdims=True) * (1.0 / width) + EPS)
    masked = to_column(mask_ref[...].astype(F32), n)
    return clean, embed_scale, masked


def normed_clean(x, clean_scale, gain):
    return (x * clean_scale * gain).astype(BF16)


def normed_noisy(x, clean_scale, embed_scale, masked, gain, embed, condition):
    is_masked = masked == 1.0
    noisy = jnp.where(is_masked, embed, x)
    scale = jnp.where(is_masked, embed_scale, clean_scale)
    return (noisy * scale * gain * condition).astype(BF16)


def dot(a, b):
    return jnp.dot(a, b, preferred_element_type=F32)


def head_norm(wide, gain):
    scale = lax.rsqrt(jnp.mean(wide * wide, axis=1, keepdims=True) + EPS)
    return (wide * scale * gain).astype(BF16)


def both_streams(x, scales, gain, embed, condition):
    clean = normed_clean(x, scales[0], gain)
    noisy = normed_noisy(x, scales[0], scales[1], scales[2], gain, embed, condition)
    return clean, noisy


def half_vectors(at, info, gain_ref, embed_ref, shift_ref):
    gain = gain_ref[:, at].astype(F32)
    embed = embed_ref[:, at].astype(F32)
    condition = 1.0 + info[3].astype(F32) / TSTEPS * shift_ref[:, at]
    return gain, embed, condition


def both_streams(x, scales, gain, embed, condition):
    clean = normed_clean(x, scales[0], gain)
    noisy = normed_noisy(x, scales[0], scales[1], scales[2], gain, embed, condition)
    return clean, noisy


def vectors_at(at, info, gain_ref, embed_ref, shift_ref):
    gain = gain_ref[:, at].astype(F32)
    embed = embed_ref[:, at].astype(F32)
    condition = 1.0 + info[3].astype(F32) / TSTEPS * shift_ref[:, at]
    return gain, embed, condition


def squares_kernel(x_hbm, mask_hbm, shift_hbm, x_ref, mask_ref, shift_ref, squares_ref, strip_ref, sems):
    moves = [
        pltpu.make_async_copy(source, target, sems.at[number])
        for number, (source, target) in enumerate(((x_hbm, x_ref), (mask_hbm, mask_ref), (shift_hbm, shift_ref)))
    ]
    for move in moves:
        move.start()
    for move in moves:
        move.wait()
    rows = x_ref.shape[0]
    x = x_ref[...].astype(F32)
    sums = jnp.sum(x * x, axis=1, keepdims=True)
    eye = lax.broadcasted_iota(jnp.int32, (rows, rows), 0) == lax.broadcasted_iota(jnp.int32, (rows, rows), 1)
    squares_ref[...] = jnp.sum(jnp.where(eye, jnp.broadcast_to(sums, (rows, rows)), 0.0), axis=0, keepdims=True)
    cut = strip_ref.shape[0]
    strip = pl.ds(pl.multiple_of(lax.axis_index("tp") * cut, 128), cut)
    strip_ref[...] = x_ref[strip]


def own_half_kernel(
    info, x_ref, own_ref, other_ref, mask_ref, gain_ref, embed_ref, shift_ref, wq, wk, wv, w_out,
    q_ref, k_ref, v_ref, rest_q, rest_k, rest_v, w_send, own_q, own_k, own_v, sems,
):
    half = x_ref.shape[1]
    depth = half // 2
    first = info[0] * half
    moves = []

    def move(source, target):
        moves.append(pltpu.make_async_copy(source, target, sems.at[len(moves)]))
        moves[-1].start()

    for chunk in range(2):
        there = pl.ds(pl.multiple_of(first + chunk * depth, 128), depth)
        here = pl.ds(chunk * depth, depth)
        for source, target in ((wk, own_k), (wv, own_v), (wq, own_q)):
            move(source.at[there], target.at[here])
    rest = pl.ds(pl.multiple_of(half - first, 128), half)
    for source, target in ((wk, rest_k), (wv, rest_v), (wq, rest_q)):
        move(source.at[rest], target)
    cols = w_send.shape[1]
    move(w_out.at[:, pl.ds(pl.multiple_of((1 - info[1]) * cols, 128), cols)], w_send)

    scales = row_scales(own_ref, other_ref, mask_ref, embed_ref, embed_ref.shape[1])
    at = pl.ds(pl.multiple_of(first, 128), half)
    gain, embed, condition = vectors_at(at, info, gain_ref, embed_ref, shift_ref)
    clean, noisy = both_streams(x_ref[...].astype(F32), scales, gain, embed, condition)
    both = jnp.concatenate([clean, noisy], axis=0)
    for chunk in range(2):
        here = slice(chunk * depth, (chunk + 1) * depth)
        for number, (target, weight) in enumerate(((k_ref, own_k), (v_ref, own_v), (q_ref, own_q))):
            moves[3 * chunk + number].wait()
            product = dot(both[:, here], weight[here])
            target[...] = product if chunk == 0 else target[...] + product
    for copy in moves[6:]:
        copy.wait()


def other_rows(info, near_ref, far_ref):
    near, far = near_ref[...].astype(F32), far_ref[...].astype(F32)
    first = info[1] == 0
    return jnp.concatenate([jnp.where(first, near, far), jnp.where(first, far, near)], axis=0)


def other_half(info, half):
    return pl.ds(pl.multiple_of((1 - info[0]) * half, 128), half)


def kv_out(ref, k, v, gain):
    for head in range(k.shape[1] // HD):
        cols = slice(head * HD, (head + 1) * HD)
        ref[:, 2 * head * HD : (2 * head + 1) * HD] = head_norm(k[:, cols], gain)
        ref[:, (2 * head + 1) * HD : 2 * (head + 1) * HD] = v[:, cols].astype(BF16)


def clean_kv_kernel(
    info, near_ref, far_ref, own_ref, other_ref, mask_ref, gain_ref, embed_ref,
    wk_ref, wv_ref, pk_ref, pv_ref, kgain_ref, all_ref, one_ref,
):
    rows = all_ref.shape[0]
    width = embed_ref.shape[1]
    clean_scale = row_scales(own_ref, other_ref, mask_ref, embed_ref, width)[0]
    at = other_half(info, near_ref.shape[1])
    clean = normed_clean(other_rows(info, near_ref, far_ref), clean_scale, gain_ref[:, at].astype(F32))
    k = pk_ref[:rows] + dot(clean, wk_ref[...])
    v = pv_ref[:rows] + dot(clean, wv_ref[...])
    kv_out(all_ref, k, v, kgain_ref[...])
    cols = one_ref.shape[1]
    one_ref[...] = all_ref[:, pl.ds(pl.multiple_of(info[0] * cols, 128), cols)]


def other_half_kernel(
    info, near_ref, far_ref, own_ref, other_ref, mask_ref, gain_ref, embed_ref, shift_ref,
    wq_ref, wk_ref, wv_ref, pq_ref, pk_ref, pv_ref, qgain_ref, kgain_ref, q_ref, self_ref,
):
    rows = self_ref.shape[0]
    width = embed_ref.shape[1]
    scales = row_scales(own_ref, other_ref, mask_ref, embed_ref, width)
    at = other_half(info, near_ref.shape[1])
    gain, embed, condition = vectors_at(at, info, gain_ref, embed_ref, shift_ref)
    clean, noisy = both_streams(other_rows(info, near_ref, far_ref), scales, gain, embed, condition)
    k = pk_ref[rows:] + dot(noisy, wk_ref[...])
    v = pv_ref[rows:] + dot(noisy, wv_ref[...])
    kv_out(self_ref, k, v, kgain_ref[...])
    q = pq_ref[...] + dot(jnp.concatenate([clean, noisy], axis=0), wq_ref[...])
    for head in range(q_ref.shape[1] // HD):
        cols = slice(head * HD, (head + 1) * HD)
        q_ref[:, cols] = head_norm(q[:, cols], qgain_ref[...])


def terms(q, k, v, mask):
    scores = lax.dot_general(q, k, (((1,), (1,)), ((), ())), preferred_element_type=F32)
    e = jnp.exp2(scores * SCORE_SCALE)
    if mask is not None:
        e = jnp.where(mask, e, 0.0)
    den = e[:, :HD]
    for start in range(HD, e.shape[1], HD):
        den = den + e[:, start : start + HD]
    return dot(e.astype(BF16), v), den


def add_pieces(q_ref, num_ref, den_ref, base, heads, pieces):
    k = jnp.concatenate([piece[:, :HD] for piece in pieces], axis=0)
    v = jnp.concatenate([piece[:, HD:] for piece in pieces], axis=0)
    for head in range(heads):
        cols = pl.ds(base + head * HD, HD)
        num, den = terms(q_ref[:, cols], k, v, None)
        num_ref[:, cols] += num
        den_ref[:, cols] += den


def head_base(info, which, width):
    return pl.multiple_of((info[0] if which == 0 else 1 - info[0]) * width, 128)


def attention_own_kernel(info, q_ref, kv_ref, self_ref, num_ref, den_ref):
    rows = kv_ref.shape[0]
    kv_heads = kv_ref.shape[1] // (2 * HD)
    group = q_ref.shape[1] // HD // kv_heads
    row = lax.broadcasted_iota(jnp.int32, (2 * rows, rows), 0)
    key_block = lax.broadcasted_iota(jnp.int32, (2 * rows, rows), 1) // BLK
    noisy = row >= rows
    row_block = jnp.where(noisy, row - rows, row) // BLK
    same = key_block == row_block
    allowed = jnp.logical_or(key_block < row_block, jnp.logical_and(same, jnp.logical_not(noisy)))
    for kv_head in range(kv_heads):
        k_cols = slice(2 * kv_head * HD, (2 * kv_head + 1) * HD)
        v_cols = slice((2 * kv_head + 1) * HD, 2 * (kv_head + 1) * HD)
        for head in range(kv_head * group, (kv_head + 1) * group, 2):
            pair = [slice(one * HD, (one + 1) * HD) for one in (head, head + 1)]
            for cols in pair:
                num_ref[:, cols], den_ref[:, cols] = terms(q_ref[:, cols], kv_ref[:, k_cols], kv_ref[:, v_cols], allowed)
            q_noisy = jnp.concatenate([q_ref[rows:, cols] for cols in pair], axis=0)
            num, den = terms(q_noisy, self_ref[:, k_cols], self_ref[:, v_cols], same)
            for number, cols in enumerate(pair):
                num_ref[rows:, cols] += num[number * rows : (number + 1) * rows]
                den_ref[rows:, cols] += den[number * rows : (number + 1) * rows]


def attention_kernel(info, q_ref, num_in, den_in, *refs, pieces, end):
    count = len(pieces)
    num_ref, den_ref, out_ref = (*refs[-3:],) if end is not None else (*refs[-2:], None)
    width = q_ref.shape[1] // 2
    heads = width // HD
    for bit in sorted({offset.bit_length() for offset, _ in pieces}):
        group = [(which, ref) for (offset, which), ref in zip(pieces, refs) if offset.bit_length() == bit]

        @pl.when(jnp.bitwise_and(info[2], 1 << (bit - 1)) != 0)
        def _(group=group):
            for which in range(2):
                found = [ref[...] for one, ref in group if one == which]
                if found:
                    add_pieces(q_ref, num_ref, den_ref, head_base(info, which, width), heads, found)
            found = [ref for one, ref in group if one == 2]
            for kv_head in range(2 if found else 0):
                cols = slice(2 * kv_head * HD, 2 * (kv_head + 1) * HD)
                add_pieces(q_ref, num_ref, den_ref, kv_head * width, heads, [ref[:, cols] for ref in found])

    for head in range(heads if end is not None else 0):
        cols = pl.ds(head_base(info, end, width) + head * HD, HD)
        total = jnp.sum(den_ref[:, cols], axis=1, keepdims=True)
        out_ref[:, cols] = (num_ref[:, cols] / total).astype(BF16)


def out_first_kernel(info, heads, w_out, mixed_ref, *, tile):
    total = mixed_ref.shape[1]
    for start in range(0, total, tile):
        mine = pl.ds(pl.multiple_of(info[1] * total + start, 128), tile)
        mixed_ref[:, start : start + tile] = dot(heads[...], w_out[:, mine])


def out_last_kernel(info, live, heads, mixed_ref, w_far, clean_out, noisy_out, clean_ref, noisy_ref, sems, *, tile):
    rows, total = clean_ref.shape
    moves = []
    for start in range(0, total, tile):
        cols = slice(start, start + tile)
        mixed = mixed_ref[:, cols] + dot(heads[...], w_far[:, cols])
        clean_ref[:, cols] = mixed[:rows].astype(BF16)
        for block in range(rows // BLK):
            part_rows = mixed[rows + block * BLK : rows + (block + 1) * BLK]
            noisy_ref[block * BLK : (block + 1) * BLK, cols] = (part_rows * live[block].astype(F32)).astype(BF16)
        for source, target in ((clean_ref, clean_out), (noisy_ref, noisy_out)):
            moves.append(pltpu.make_async_copy(source.at[:, cols], target.at[:, cols], sems.at[len(moves)]))
            moves[-1].start()
    for move in moves:
        move.wait()


WHOLE = pl.BlockSpec(memory_space=pltpu.VMEM)
HBM = pl.BlockSpec(memory_space=pltpu.HBM)
HINT = 1


def call(kernel, scalars, ins, outs, arrays, flops, num_bytes, scratch=(), exps=0, grid=1, aliases=None, limit=20):
    return pl.pallas_call(
        kernel,
        grid_spec=pltpu.PrefetchScalarGridSpec(
            num_scalar_prefetch=len(scalars),
            grid=(grid,),
            in_specs=ins,
            out_specs=[spec for spec, _ in outs],
            scratch_shapes=list(scratch),
        ),
        out_shape=[shape for _, shape in outs],
        compiler_params=pltpu.CompilerParams(vmem_limit_bytes=limit << 20),
        cost_estimate=pl.CostEstimate(
            flops=flops // HINT, bytes_accessed=num_bytes // HINT, transcendentals=exps // HINT
        ),
        input_output_aliases=aliases or {},
    )(*scalars, *arrays)


def after(value, *others):
    return lax.optimization_barrier((value, *others))[0]


def on_device(
    mesh, clean_tokens, norm_gain, mask_embed, time_shift, w_query, w_key, w_value, w_out,
    q_gain, k_gain, masked, block_live, timesteps,
):
    rows, half = clean_tokens.shape
    heads_width = w_query.shape[1]
    kv_width = w_key.shape[1]
    ctx = mesh.shape["ctx"]
    c, p, t = lax.axis_index("copy"), lax.axis_index("ctx"), lax.axis_index("tp")
    info = jnp.stack([c, t, p, timesteps[0]]).astype(jnp.int32)
    pair = [(0, 1), (1, 0)]
    cross_x = lambda v: lax.ppermute(v, "copy", pair)
    cross_core = lambda v: lax.ppermute(v, "tp", pair)
    shape = jax.ShapeDtypeStruct

    cut = rows // 2
    out_cols = w_out.shape[1] // 2
    qg, kg = q_gain[None], k_gain[None]
    vmem = lambda dims, kind: (WHOLE, pltpu.VMEM(dims, kind))
    in_hbm = lambda v: pltpu.with_memory_space_constraint(v, pltpu.HBM)

    x, mask, shift, squares, strip = call(
        squares_kernel, [], [HBM] * 3,
        [vmem((rows, half), BF16), vmem((1, rows), jnp.int32), vmem((1, 2 * half), F32), vmem((1, rows), F32),
         vmem((cut, half), BF16)],
        [in_hbm(clean_tokens), in_hbm(masked), in_hbm(time_shift[None])], 2 * rows * half, rows * half * 2,
        [pltpu.SemaphoreType.DMA((3,))],
    )
    other_squares = cross_x(squares)
    near = cross_x(strip)
    stats = [squares, other_squares, mask]
    vectors = [norm_gain[None], mask_embed[None], shift]
    buffers = [(half, heads_width), (half, kv_width), (half, kv_width)]
    per_row = heads_width + 2 * kv_width

    pq, pk, pv, *weights, w_send = call(
        own_half_kernel, [info], [WHOLE] * 7 + [HBM] * 4,
        [vmem((2 * rows, width), F32) for width in (heads_width, kv_width, kv_width)]
        + [vmem(dims, BF16) for dims in buffers] + [vmem((heads_width, out_cols), BF16)],
        [x] + stats + vectors + [in_hbm(w) for w in (w_query, w_key, w_value, w_out)],
        32 * rows * half * per_row, 2 * half * per_row * 2,
        [pltpu.VMEM(dims, BF16) for dims in buffers] + [pltpu.SemaphoreType.DMA((10,))], limit=32,
    )
    near = after(near, pk)
    far = cross_core(near)

    kv, kva = call(
        clean_kv_kernel, [info], [WHOLE] * 12,
        [vmem((rows, 2 * kv_width), BF16), vmem((rows, kv_width), BF16)],
        [near, far] + stats + vectors[:2] + weights[1:] + [pk, pv, kg],
        4 * rows * half * kv_width, half * 2 * kv_width * 2,
    )

    trade = lambda v, offset: lax.ppermute(v, "ctx", [(i, i ^ offset) for i in range(ctx)])
    later = list(range(4, ctx, 2))
    early, late = later[: len(later) // 2], later[len(later) // 2 :]
    column = {offset: trade(kva, offset) for offset in early}
    left = trade(kv, 2)
    beside = trade(kv, 1)
    w_far = cross_core(after(w_send, kv))
    near = after(near, kv)
    q, own = call(
        other_half_kernel, [info], [WHOLE] * 16,
        [vmem((2 * rows, heads_width), BF16), vmem((rows, 2 * kv_width), BF16)],
        [near, far] + stats + vectors + weights + [pq, pk, pv, qg, kg],
        4 * rows * half * per_row, half * per_row * 2,
    )

    column.update({offset: trade(after(kva, q), offset) for offset in late})
    acc = [vmem((2 * rows, heads_width), F32)] * 2
    unit = rows * rows * heads_width // HD
    cost = lambda units: (16 * HD * unit * units, 8 * unit, (), unit * units)
    in_place = {2: 0, 3: 1}
    num, den = call(attention_own_kernel, [info], [WHOLE] * 3, acc, [q, kv, own], *cost(3))
    def attend(num, den, pieces, end=None, before=()):
        outs = [] if end is None else [vmem((2 * rows, heads_width), BF16)]
        aliases = {**in_place, 4 + len(pieces): 2} if before else in_place
        return call(
            functools.partial(attention_kernel, pieces=tuple(key for key, _ in pieces), end=end), [info],
            [WHOLE] * (3 + len(pieces) + len(before)), acc + outs,
            [q, num, den] + [piece for _, piece in pieces] + list(before), *cost(len(pieces)), aliases=aliases,
        )

    over_x, over_y, corner = {}, {}, {}

    def turn(offsets, done):
        for offset in offsets:
            column[offset] = after(column[offset], done)
            over_y[offset], over_x[offset] = trade(column[offset], 1), cross_x(column[offset])

    turn(early, num)
    num, den = attend(num, den, [((1, 2), beside)])
    right = trade(after(left, num), 1)
    corner.update({o: cross_x(after(over_y[o], num)) for o in early})
    turn(late, num)
    num, den = attend(
        num, den,
        [((2, 2), left)] + [((o, 0), column[o]) for o in later]
        + [((o, 0), over_y[o]) for o in early] + [((o, 1), over_x[o]) for o in early],
    )
    corner.update({o: cross_x(after(over_y[o], num)) for o in late})
    num, den, near_heads = attend(
        num, den,
        [((3, 2), right)] + [((o, 0), over_y[o]) for o in late]
        + [((o, 1), over_x[o]) for o in late] + [((o, 1), corner[o]) for o in early], 0,
    )
    num, den, near_heads = attend(
        num, den, [((o, 1), corner[o]) for o in late], 1, [near_heads]
    )
    far_heads = cross_core(near_heads)

    tile = 512
    half_cost = 4 * rows * heads_width * out_cols, heads_width * out_cols * 2
    mixed, = call(
        functools.partial(out_first_kernel, tile=tile), [info], [WHOLE] * 2, [vmem((2 * rows, out_cols), F32)],
        [near_heads, w_out], *half_cost,
    )
    out = shape((rows, out_cols), BF16)
    clean_out, noised_out = call(
        functools.partial(out_last_kernel, tile=tile), [info, block_live[0]], [WHOLE] * 3, [(HBM, out), (HBM, out)],
        [far_heads, mixed, w_far], *half_cost,
        [pltpu.VMEM((rows, out_cols), BF16)] * 2 + [pltpu.SemaphoreType.DMA((2 * (out_cols // tile),))],
    )
    return (clean_out, noised_out[None])


def solution(mesh):
    in_specs = (
        P("ctx", "copy"),
        P(),
        P(),
        P(),
        P(None, "tp"),
        P(None, "tp"),
        P(None, "tp"),
        P("tp", None),
        P(),
        P(),
        P("copy", "ctx"),
        P("copy", "ctx"),
        P("copy"),
    )
    out_specs = (P("ctx", "tp"), P("copy", "ctx", "tp"))
    return jax.shard_map(
        functools.partial(on_device, mesh), mesh=mesh, in_specs=in_specs, out_specs=out_specs, check_vma=False
    )
```
